32 devices in a mesh: seq: 16 (over z, y, core), stream: 2 (over x).
Axes of the slice: x: 2, y: 2, z: 4, core: 2. Of those that a mesh axis runs over, the one named last changes fastest.
Arguments:
- tokens: bfloat16 [2, 8192, 768], P('stream', 'seq'), may hold values from -6 to 6
- lengths: int32 [16, 4], P('seq'), may hold values from 0 to 512, as said below
- cotangent: bfloat16 [2, 8192, 768], P('stream', 'seq'), may hold values from -6 to 6
- attn_gain: bfloat16 [768], P(('seq', 'stream')), may hold values from 0.099609375 to 1.8984375
- qkv_weight: bfloat16 [768, 2304], P(('seq', 'stream')), may hold values from -0.21875 to 0.21875
- out_weight: bfloat16 [768, 768], P(('seq', 'stream')), may hold values from -0.875 to 0.875
- mlp_gain: bfloat16 [768], P(('seq', 'stream')), may hold values from 0.099609375 to 1.8984375
- up_weight: bfloat16 [768, 3072], P(('seq', 'stream')), may hold values from -0.21875 to 0.21875
- up_bias: bfloat16 [3072], P(('seq', 'stream')), may hold values from -3 to 3
- down_weight: bfloat16 [3072, 768], P(('seq', 'stream')), may hold values from -0.109375 to 0.109375
- down_bias: bfloat16 [768], P(('seq', 'stream')), may hold values from -2 to 2
Outputs:
- layer_out: bfloat16 [2, 8192, 768], P('stream', 'seq')
- grad_tokens: float32 [2, 8192, 768], P('stream', 'seq')
- grad_attn_gain: float32 [768], P(('seq', 'stream'))
- grad_qkv_weight: float32 [768, 2304], P(('seq', 'stream'))
- grad_out_weight: float32 [768, 768], P(('seq', 'stream'))
- grad_mlp_gain: float32 [768], P(('seq', 'stream'))
- grad_up_weight: float32 [768, 3072], P(('seq', 'stream'))
- grad_up_bias: float32 [3072], P(('seq', 'stream'))
- grad_down_weight: float32 [3072, 768], P(('seq', 'stream'))
- grad_down_bias: float32 [768], P(('seq', 'stream'))
The draws below stay inside these ranges and needn't reach their ends.
Inputs may be any that keep to these rules, and one draw needn't show every extreme that they name: `lengths`: each row sums to 512; a 0 is an empty slot; some row holds a single sequence of 512 tokens.
All inputs are finite; a program needn't handle non-finite values.
Results may differ from the reference program's by a relative error of at most 0.014.
Values may be sent and summed in bfloat16 or wider, within the bound.
No kernel may reach another device: no remote copies, remote signals or barrier semaphores. Data moves between devices by JAX's collectives and lax.ppermute only.
A program may use at most 192 MiB of HBM per device.

```python
import math
import jax
import jax.numpy as jnp
from jax import lax

D = 768
HEADS = 12
HEAD_DIM = 64
FF = 3072
BLOCK = 16
DOCS = 4
TOK_DEV = 512
GROUPS = 16
TOKENS = 8192


def draw_lengths(key, part):
    first_key, second_key, third_key = jax.random.split(key, 3)
    entire = jax.random.randint(first_key, (GROUPS,), 0, 3) == 0
    chosen = jax.random.randint(second_key, (), 0, GROUPS)
    entire = entire | (jnp.arange(GROUPS, dtype=jnp.int32) == chosen)
    jitter = jax.random.randint(third_key, (GROUPS, DOCS - 1), -1, 2) * (TOK_DEV // 16)
    leading = TOK_DEV // DOCS + jitter
    closing = TOK_DEV - jnp.sum(leading, axis=1, keepdims=True)
    packed = jnp.concatenate([leading, closing], axis=1).astype(jnp.int32)
    single = jnp.concatenate([jnp.full((GROUPS, 1), TOK_DEV, dtype=jnp.int32), jnp.zeros((GROUPS, DOCS - 1), dtype=jnp.int32)], axis=1)
    return jnp.where(entire[:, None], single, packed).astype(jnp.int32)


def block_scale(key, extent, cuts, least, largest):
    def one(dim, blocks):
        heights = jax.random.uniform(jax.random.fold_in(jax.random.fold_in(key, 6), dim), (blocks,), jnp.float32, least / len(cuts), largest / len(cuts))
        return jnp.repeat(jnp.exp(heights), extent[dim] // blocks).reshape((-1,) + (1,) * (len(extent) - dim - 1))

    factor_of = one(*cuts[0])
    for cut in cuts[1:]:
        factor_of = factor_of * one(*cut)
    return factor_of


def bell_draw(rng, shape, scale, most, shards=(), kind=jnp.bfloat16):
    result = scale * jax.random.normal(rng, shape, jnp.float32)
    if shards:
        result = result * block_scale(rng, shape, shards, -0.22, 0.18)
    return jnp.clip(result, -most, most).astype(kind)


def setup_inputs(seed: int = 0) -> dict:
    key_list = jax.random.split(jax.random.key(seed), 12)
    tokens = bell_draw(key_list[0], (2, TOKENS, D), 1.0, 6.0, ((0, 2), (1, 16)))
    lengths = draw_lengths(jax.random.fold_in(key_list[11], 71), 0)
    cotangent = bell_draw(key_list[2], (2, TOKENS, D), 1.0, 6.0, ((0, 2), (1, 16)))
    attn_gain = jnp.clip(1.0 + 0.18 * jax.random.normal(key_list[3], (D,), jnp.float32), 0.099609375, 1.8984375).astype(jnp.bfloat16)
    qkv_weight = bell_draw(key_list[4], (D, 3 * D), D ** -0.5, 0.21875, ((0, 32),))
    out_weight = bell_draw(key_list[5], (D, D), (D // 16) ** -0.5, 0.875, ((0, 32),))
    mlp_gain = jnp.clip(1.0 + 0.18 * jax.random.normal(key_list[6], (D,), jnp.float32), 0.099609375, 1.8984375).astype(jnp.bfloat16)
    up_weight = bell_draw(key_list[7], (D, FF), D ** -0.5, 0.21875, ((0, 32),))
    up_bias = bell_draw(key_list[8], (FF,), 0.5, 3.0, ((0, 32),))
    down_weight = bell_draw(key_list[9], (FF, D), FF ** -0.5, 0.109375, ((0, 32),))
    down_bias = bell_draw(key_list[10], (D,), 0.3, 2.0, ((0, 32),))
    return dict(tokens=tokens, lengths=lengths, cotangent=cotangent, attn_gain=attn_gain, qkv_weight=qkv_weight, out_weight=out_weight, mlp_gain=mlp_gain, up_weight=up_weight, up_bias=up_bias, down_weight=down_weight, down_bias=down_bias)


@jax.custom_vjp
def low(v):
    return lax.optimization_barrier(v.astype(jnp.bfloat16)).astype(jnp.float32)

@jax.custom_vjp
def low_back(v):
    return v

def low_keep(v):
    return (low(v), None)

def low_pass(kept, grad):
    return (grad,)

def back_keep(v):
    return (v, None)

def back_low(kept, grad):
    return (low(grad),)
low.defvjp(low_keep, low_pass)
low_back.defvjp(back_keep, back_low)
EPSILON = 1e-05
NEG_FILL = -1e+30
HIGHEST_MODE = lax.Precision.HIGHEST

def doc_layout(pack_lengths, row_count):
    seq_ends = jnp.cumsum(pack_lengths).astype(jnp.int32)
    row_index = jnp.arange(row_count, dtype=jnp.int32)
    passed = seq_ends[None, :] <= row_index[:, None]
    doc_ids = lax.optimization_barrier(jnp.sum(passed.astype(jnp.int32), axis=1)).astype(jnp.int32)
    starts = lax.optimization_barrier(jnp.max(jnp.where(passed, seq_ends[None, :], 0), axis=1)).astype(jnp.int32)
    return (doc_ids, row_index - starts)

def rotary_tables(positions, head_size):
    half_size = head_size // 2
    frequency = jnp.exp(jnp.arange(half_size, dtype=jnp.float32) * (-2.0 * math.log(10000.0) / head_size))
    angles = positions.astype(jnp.float32)[:, None] * frequency[None, :]
    return (jnp.cos(angles), jnp.sin(angles))

def rotate(tensor, cosine, sine_part):
    half_size = tensor.shape[-1] // 2
    first_half = tensor[..., :half_size]
    second_half = tensor[..., half_size:]
    cos_heads = cosine[:, None, :]
    sin_heads = sine_part[:, None, :]
    return jnp.concatenate([first_half * cos_heads - second_half * sin_heads, second_half * cos_heads + first_half * sin_heads], axis=-1)

def norm_rows(values, gain_row):
    center = values - lax.optimization_barrier(jnp.mean(values, axis=-1, keepdims=True))
    return center * lax.rsqrt(lax.optimization_barrier(jnp.mean(center * center, axis=-1, keepdims=True)) + EPSILON) * gain_row

def attention(queries, key_rows, value_rows, allowed):
    raw_scores = low_back(jnp.einsum('qhd,khd->hqk', queries, key_rows, precision=HIGHEST_MODE))
    scores = jnp.where(allowed[None], raw_scores * HEAD_DIM ** (-0.5), NEG_FILL)
    row_max = lax.optimization_barrier(jnp.max(scores, axis=-1, keepdims=True))
    exponent = jnp.exp(scores - row_max)
    weights_low = low(exponent / lax.optimization_barrier(jnp.sum(exponent, axis=-1, keepdims=True)))
    return jnp.einsum('hqk,khd->qhd', weights_low, value_rows, precision=HIGHEST_MODE)

def layer_pass(pack_rows, pack_lengths, param_set):
    attn_gain, qkv_weight, out_weight, mlp_gain, up_weight, up_bias, down_weight, down_bias = param_set
    row_count = pack_rows.shape[1]
    doc_ids, positions = doc_layout(pack_lengths, row_count)
    cosine, sine_part = rotary_tables(positions, HEAD_DIM)
    block_ids = positions // BLOCK
    same_doc = doc_ids[:, None] == doc_ids[None, :]
    causal_ok = same_doc & (block_ids[:, None] >= block_ids[None, :])
    diagonal_ok = same_doc & (block_ids[:, None] == block_ids[None, :])
    earlier_ok = same_doc & (block_ids[:, None] > block_ids[None, :])
    first_in = low(norm_rows(pack_rows, attn_gain))
    projected = low_back(jnp.einsum('std,de->ste', first_in, qkv_weight, precision=HIGHEST_MODE))
    shape_heads = (2, row_count, HEADS, HEAD_DIM)
    queries = low(rotate(projected[..., :D].reshape(shape_heads), cosine, sine_part))
    keys_all = low(rotate(projected[..., D:2 * D].reshape(shape_heads), cosine, sine_part))
    values_all = low(projected[..., 2 * D:].reshape(shape_heads))
    clean_mixed = attention(queries[0], keys_all[0], values_all[0], causal_ok)
    noisy_mixed = attention(queries[1], jnp.concatenate([keys_all[1], keys_all[0]], axis=0), jnp.concatenate([values_all[1], values_all[0]], axis=0), jnp.concatenate([diagonal_ok, earlier_ok], axis=1))
    attn_low = low(low_back(jnp.stack([clean_mixed, noisy_mixed]).reshape(2, row_count, D)))
    after_attn = pack_rows + low_back(jnp.einsum('std,de->ste', attn_low, out_weight, precision=HIGHEST_MODE))
    second_in = low(norm_rows(after_attn, mlp_gain))
    pre_act = low_back(jnp.einsum('std,df->stf', second_in, up_weight, precision=HIGHEST_MODE) + up_bias)
    activated = low(jax.nn.gelu(pre_act, approximate=True))
    return after_attn + low_back(jnp.einsum('stf,fd->std', activated, down_weight, precision=HIGHEST_MODE) + down_bias)

def reference(tokens, lengths, cotangent, attn_gain, qkv_weight, out_weight, mlp_gain, up_weight, up_bias, down_weight, down_bias):
    params = (attn_gain.astype(jnp.float32), qkv_weight.astype(jnp.float32), out_weight.astype(jnp.float32), mlp_gain.astype(jnp.float32), up_weight.astype(jnp.float32), up_bias.astype(jnp.float32), down_weight.astype(jnp.float32), down_bias.astype(jnp.float32))
    pack_stack = tokens.astype(jnp.float32).reshape(2, GROUPS, TOK_DEV, D).transpose(1, 0, 2, 3)
    cot_stack = cotangent.astype(jnp.float32).reshape(2, GROUPS, TOK_DEV, D).transpose(1, 0, 2, 3)

    def forward(stacked, param_set):

        def one_pack(block_in):
            return layer_pass(block_in[0], block_in[1], param_set)
        return lax.map(jax.checkpoint(one_pack), (stacked, lengths))
    outputs, pull_back = jax.vjp(forward, pack_stack, params)
    grad_stack, grad_params = pull_back(cot_stack)
    layer_out = outputs.transpose(1, 0, 2, 3).reshape(2, TOKENS, D).astype(jnp.bfloat16)
    grad_tokens = grad_stack.transpose(1, 0, 2, 3).reshape(2, TOKENS, D)
    return (layer_out, grad_tokens, grad_params[0], grad_params[1], grad_params[2], grad_params[3], grad_params[4], grad_params[5], grad_params[6], grad_params[7])
```

```python
from functools import partial
import math

import jax
import jax.numpy as jnp
from jax import lax
from jax.experimental import pallas as pl
from jax.experimental.pallas import tpu as pltpu
from jax.sharding import PartitionSpec as P

HEADS = 12
HEAD_DIM = 64
BLOCK = 16


EPSILON = 1e-05
NEG_FILL = -1e30


def shifted(block, axis, distance):
    devices = range(lax.axis_size(axis))
    route = [(i - distance, i) for i in devices if i - distance in devices]
    return lax.ppermute(block, axis, route)


ALL = ("seq", "stream")
STREAM_BIT, CORE_BIT, NEAR_BIT = 1, 2, 4


def device_count():
    return lax.axis_size("seq") * lax.axis_size("stream")


def far_groups():
    bits = []
    bit = 2 * NEAR_BIT
    while bit < device_count():
        bits.append(bit)
        bit *= 2
    groups = []
    while bits:
        taken, bits = bits[:2], bits[2:]
        groups.append(taken if len(taken) == 1 else [taken[0], taken[1], taken[0] + taken[1]])
    return groups


def flip(block, mask):
    return lax.ppermute(block, ALL, [(i, i ^ mask) for i in range(device_count())])


def place(pieces, keys, me):
    total = sum(len(k) for k in keys)
    shape = (total,) + pieces[0].shape[1:]

    def body(me_ref, *refs):
        out, sem = refs[-2], refs[-1]
        for piece, key in zip(refs[:-2], keys):
            for j, rel in enumerate(key):
                pltpu.make_async_copy(piece.at[j], out.at[me_ref[0] ^ rel], sem).start()
        pltpu.make_async_copy(out, out, sem).wait()

    return pl.pallas_call(
        body,
        out_shape=jax.ShapeDtypeStruct(shape, pieces[0].dtype),
        in_specs=[pl.BlockSpec(memory_space=pltpu.SMEM)]
        + [pl.BlockSpec(memory_space=pl.ANY)] * len(pieces),
        out_specs=pl.BlockSpec(memory_space=pltpu.VMEM),
        scratch_shapes=[pltpu.SemaphoreType.DMA],
    )(me, *pieces)


def gather(shard, near_order, me):
    piece, key = shard[None], [0]
    for group in far_groups():
        got = [piece] + [flip(piece, mask) for mask in group]
        key = [k ^ mask for mask in [0] + group for k in key]
        piece = jnp.concatenate(got, axis=0)
    pieces, keys = [piece], [key]
    for bit in near_order + (CORE_BIT,):
        pieces = pieces + [flip(p, bit) for p in pieces]
        keys = keys + [[k ^ bit for k in key] for key in keys]
    return place(pieces, keys, me)


def spread(whole, orders, me):
    def body(me_ref, src, *refs):
        sem = refs[-1]
        for out, order in zip(refs[:-1], orders):
            for j, rel in enumerate(order):
                pltpu.make_async_copy(src.at[me_ref[0] ^ rel], out.at[j], sem).start()
        pltpu.make_async_copy(src, src, sem).wait()

    return pl.pallas_call(
        body,
        out_shape=[
            jax.ShapeDtypeStruct((len(order),) + whole.shape[1:], whole.dtype) for order in orders
        ],
        in_specs=[pl.BlockSpec(memory_space=pltpu.SMEM), pl.BlockSpec(memory_space=pltpu.VMEM)],
        out_specs=[pl.BlockSpec(memory_space=pl.ANY)] * len(orders),
        scratch_shapes=[pltpu.SemaphoreType.DMA],
    )(me, whole)


def scatter_sum(whole, near_order, me):
    kind = whole.dtype
    order = [0]
    for group in far_groups():
        order = [k ^ mask for mask in [0] + group for k in order]
    for bit in reversed(near_order):
        order = [k ^ b for b in (0, bit) for k in order]
    keep, send = spread(whole, [order, [k ^ CORE_BIT for k in order]], me)
    total = keep.astype(jnp.float32) + flip(send, CORE_BIT).astype(jnp.float32)
    for bit in near_order:
        half = total.shape[0] // 2
        recv = flip(total[half:].astype(kind), bit)
        total = total[:half] + recv.astype(jnp.float32)
    for group in reversed(far_groups()):
        part = total.shape[0] // (len(group) + 1)
        recv = [
            flip(total[(i + 1) * part : (i + 2) * part].astype(kind), mask)
            for i, mask in enumerate(group)
        ]
        total = total[:part]
        for r in recv:
            total = total + r.astype(jnp.float32)
    return total[0]


ORDER_A = (STREAM_BIT, NEAR_BIT)
ORDER_B = (NEAR_BIT, STREAM_BIT)


def doc_layout(pack_lengths, row_count):
    ends = [pack_lengths[0]]
    for i in range(1, pack_lengths.shape[0]):
        ends.append(ends[-1] + pack_lengths[i])
    seq_ends = jnp.stack(ends)
    row_index = jnp.arange(row_count, dtype=jnp.int32)
    passed = seq_ends[None, :] <= row_index[:, None]
    doc_ids = jnp.sum(passed.astype(jnp.int32), axis=1)
    starts = jnp.max(jnp.where(passed, seq_ends[None, :], 0), axis=1)
    return (doc_ids, row_index - starts)


def rotary_tables(positions, head_size):
    half_size = head_size // 2
    frequency = jnp.exp(
        jnp.arange(half_size, dtype=jnp.float32) * (-2.0 * math.log(10000.0) / head_size)
    )
    angles = positions.astype(jnp.float32)[:, None] * frequency[None, :]
    return (jnp.cos(angles), jnp.sin(angles))


def rotate(tensor, cosine, sine_part):
    half_size = tensor.shape[-1] // 2
    first_half = tensor[..., :half_size]
    second_half = tensor[..., half_size:]
    cos_heads = cosine[:, None, :]
    sin_heads = sine_part[:, None, :]
    return jnp.concatenate(
        [
            first_half * cos_heads - second_half * sin_heads,
            second_half * cos_heads + first_half * sin_heads,
        ],
        axis=-1,
    )


def rotate_back(tensor, cosine, sine_part):
    half_size = tensor.shape[-1] // 2
    first_half = tensor[..., :half_size]
    second_half = tensor[..., half_size:]
    cos_heads = cosine[:, None, :]
    sin_heads = sine_part[:, None, :]
    return jnp.concatenate(
        [
            first_half * cos_heads + second_half * sin_heads,
            second_half * cos_heads - first_half * sin_heads,
        ],
        axis=-1,
    )


def norm_rows(values, gain_row):
    center = values - jnp.mean(values, axis=-1, keepdims=True)
    inverse_dev = lax.rsqrt(jnp.mean(center * center, axis=-1, keepdims=True) + EPSILON)
    normed = center * inverse_dev
    return (normed * gain_row, normed, inverse_dev)


def norm_back(grad_out, normed, inverse_dev, gain_row):
    grad_norm = grad_out * gain_row
    grad_gain = jnp.sum(grad_out * normed, axis=0)
    grad_in = inverse_dev * (
        grad_norm
        - jnp.mean(grad_norm, axis=-1, keepdims=True)
        - normed * jnp.mean(grad_norm * normed, axis=-1, keepdims=True)
    )
    return (grad_in, grad_gain)


def local(
    tokens,
    lengths,
    cotangent,
    attn_gain,
    qkv_weight,
    out_weight,
    mlp_gain,
    up_weight,
    up_bias,
    down_weight,
    down_bias,
):
    row_count = tokens.shape[1]
    model_width = tokens.shape[2]
    head_scale = HEAD_DIM ** (-0.5)
    block_rows = min(512, row_count)
    block_count = row_count // block_rows
    me_flat = (lax.axis_index("seq") * 2 + lax.axis_index("stream")).astype(jnp.int32)
    me = me_flat[None]
    n_dev = device_count()
    small_sizes = (attn_gain.shape[0], mlp_gain.shape[0], down_bias.shape[0], up_bias.shape[0])
    small = jnp.concatenate([attn_gain, mlp_gain, down_bias, up_bias])
    small_width = -(-small.shape[0] // 128) * 128
    small = jnp.pad(small, (0, small_width - small.shape[0])).reshape(1, small_width)
    small_all = gather(small, ORDER_A, me).reshape(n_dev, small_width)

    def small_part(i):
        start = sum(small_sizes[:i])
        return small_all[:, start : start + small_sizes[i]].reshape(-1)

    gain_one = small_part(0)
    qkv_full = gather(qkv_weight, ORDER_A, me).reshape(-1, qkv_weight.shape[1])
    out_full = gather(out_weight, ORDER_B, me).reshape(-1, out_weight.shape[1])
    resid_in = tokens[0].astype(jnp.float32)
    first_full, normed_one, inverse_one = norm_rows(resid_in, gain_one.astype(jnp.float32))
    first_in = first_full.astype(jnp.bfloat16)
    projected = jnp.dot(first_in, qkv_full, preferred_element_type=jnp.float32)
    doc_ids, positions = doc_layout(lengths[0], row_count)
    cosine, sine_part = rotary_tables(positions, HEAD_DIM)
    queries = rotate(
        projected[:, :model_width].reshape(row_count, HEADS, HEAD_DIM), cosine, sine_part
    ).astype(jnp.bfloat16)
    own_keys = rotate(
        projected[:, model_width : 2 * model_width].reshape(row_count, HEADS, HEAD_DIM),
        cosine,
        sine_part,
    ).astype(jnp.bfloat16)
    own_values = projected[:, 2 * model_width :].astype(jnp.bfloat16)
    partner = shifted(
        jnp.stack([own_keys.reshape(row_count, model_width), own_values]), "stream", 1
    )
    key_rows = jnp.concatenate([own_keys, partner[0].reshape(row_count, HEADS, HEAD_DIM)], axis=0)
    value_rows = jnp.concatenate([own_values, partner[1]], axis=0).reshape(
        2 * row_count, HEADS, HEAD_DIM
    )
    is_noisy = lax.axis_index("stream") == 1
    block_ids = positions // BLOCK
    same_doc = doc_ids[:, None] == doc_ids[None, :]
    own_ok = same_doc & jnp.where(
        is_noisy, block_ids[:, None] == block_ids[None, :], block_ids[:, None] >= block_ids[None, :]
    )
    partner_ok = same_doc & (block_ids[:, None] > block_ids[None, :]) & is_noisy
    allowed = jnp.concatenate([own_ok, partner_ok], axis=1).reshape(
        block_count, block_rows, 2 * row_count
    )
    query_blocks = queries.reshape(block_count, block_rows, HEADS, HEAD_DIM)

    def scores_of(query_block, mask_block, key_set):
        raw_scores = jnp.einsum(
            "qhd,khd->hqk", query_block, key_set, preferred_element_type=jnp.float32
        )
        return jnp.where(mask_block[None], raw_scores * head_scale, NEG_FILL)

    def run_forward(key_set, value_set, mask_set):

        def attend(running, block_in):
            query_block, mask_block = block_in
            scores = scores_of(query_block, mask_block, key_set)
            row_max = jnp.max(scores, axis=-1, keepdims=True)
            exponent = jnp.exp(scores - row_max)
            row_sum = jnp.sum(exponent, axis=-1, keepdims=True)
            weights_low = (exponent / row_sum).astype(jnp.bfloat16)
            mixed_rows = jnp.einsum(
                "hqk,khd->qhd", weights_low, value_set, preferred_element_type=jnp.float32
            )
            return (running, (mixed_rows, (row_max + jnp.log(row_sum))[..., 0]))

        return lax.scan(attend, 0, (query_blocks, mask_set))[1]

    attn_rows, log_sums = lax.cond(
        is_noisy,
        lambda: run_forward(key_rows, value_rows, allowed),
        lambda: run_forward(key_rows[:row_count], value_rows[:row_count], allowed[..., :row_count]),
    )
    attn_low = attn_rows.reshape(row_count, model_width).astype(jnp.bfloat16)
    after_attn = resid_in + jnp.dot(attn_low, out_full, preferred_element_type=jnp.float32)
    up_full = gather(up_weight, ORDER_B, me).reshape(-1, up_weight.shape[1])
    down_full = gather(down_weight, ORDER_A, me).reshape(-1, down_weight.shape[1])
    gain_two, down_bias_full, up_bias_full = small_part(1), small_part(2), small_part(3)
    second_full, normed_two, inverse_two = norm_rows(after_attn, gain_two.astype(jnp.float32))
    second_in = second_full.astype(jnp.bfloat16)
    pre_act = jnp.dot(second_in, up_full, preferred_element_type=jnp.float32) + up_bias_full.astype(
        jnp.float32
    )
    activated = jax.nn.gelu(pre_act, approximate=True).astype(jnp.bfloat16)
    layer_full = (
        after_attn
        + jnp.dot(activated, down_full, preferred_element_type=jnp.float32)
        + down_bias_full.astype(jnp.float32)
    )
    layer_out = layer_full.astype(jnp.bfloat16)[None]
    gain_back_two, up_back, down_back = gain_two, up_full, down_full
    grad_top = cotangent[0]
    grad_down_bias = jnp.sum(grad_top, axis=0, dtype=jnp.float32)
    grad_down_w = jnp.einsum("tf,td->fd", activated, grad_top, preferred_element_type=jnp.float32)
    grad_act = jnp.einsum("td,fd->tf", grad_top, down_back, preferred_element_type=jnp.float32)
    _, gelu_pull = jax.vjp(partial(jax.nn.gelu, approximate=True), pre_act)
    grad_pre = gelu_pull(grad_act)[0].astype(jnp.bfloat16)
    grad_up_b = jnp.sum(grad_pre, axis=0, dtype=jnp.float32)
    grad_up_w = jnp.einsum("td,tf->df", second_in, grad_pre, preferred_element_type=jnp.float32)
    grad_second = jnp.einsum("tf,df->td", grad_pre, up_back, preferred_element_type=jnp.float32)
    grad_mid, grad_gain_two = norm_back(
        grad_second, normed_two, inverse_two, gain_back_two.astype(jnp.float32)
    )
    grad_after = grad_top.astype(jnp.float32) + grad_mid
    owned_up = scatter_sum(
        grad_up_w.astype(jnp.bfloat16).reshape(n_dev, -1, grad_up_w.shape[1]), ORDER_B, me
    )
    owned_down = scatter_sum(
        grad_down_w.astype(jnp.bfloat16).reshape(n_dev, -1, grad_down_w.shape[1]), ORDER_A, me
    )
    gain_back_one, qkv_back, out_back = gain_one, qkv_full, out_full
    grad_attn_low = grad_after.astype(jnp.bfloat16)
    grad_out_w = jnp.einsum(
        "td,te->de", attn_low, grad_attn_low, preferred_element_type=jnp.float32
    )
    grad_mixed = jnp.einsum(
        "te,de->td", grad_attn_low, out_back, preferred_element_type=jnp.float32
    ).astype(jnp.bfloat16)
    grad_mixed = grad_mixed.reshape(block_count, block_rows, HEADS, HEAD_DIM)

    def run_backward(key_set, value_set, mask_set):

        def attend_back(running, block_in):
            key_acc, value_acc = running
            query_block, mask_block, lse_block, grad_block = block_in
            scores = scores_of(query_block, mask_block, key_set)
            probs_full = jnp.exp(scores - lse_block[..., None])
            grad_probs = jnp.einsum(
                "qhd,khd->hqk", grad_block, value_set, preferred_element_type=jnp.float32
            )
            delta_rows = jnp.sum(grad_probs * probs_full, axis=-1, keepdims=True)
            grad_scores = (probs_full * (grad_probs - delta_rows) * head_scale).astype(jnp.bfloat16)
            grad_query = jnp.einsum(
                "hqk,khd->qhd", grad_scores, key_set, preferred_element_type=jnp.float32
            )
            key_acc = key_acc + jnp.einsum(
                "hqk,qhd->khd", grad_scores, query_block, preferred_element_type=jnp.float32
            )
            value_acc = value_acc + jnp.einsum(
                "hqk,qhd->khd",
                probs_full.astype(jnp.bfloat16),
                grad_block,
                preferred_element_type=jnp.float32,
            )
            return ((key_acc, value_acc), grad_query)

        zero_state = jnp.zeros(key_set.shape, jnp.float32)
        return lax.scan(
            attend_back, (zero_state, zero_state), (query_blocks, mask_set, log_sums, grad_mixed)
        )

    def backward_own():
        (key_part, value_part), grad_part = run_backward(
            key_rows[:row_count], value_rows[:row_count], allowed[..., :row_count]
        )
        padding = jnp.zeros(key_part.shape, jnp.float32)
        return (
            (
                jnp.concatenate([key_part, padding], axis=0),
                jnp.concatenate([value_part, padding], axis=0),
            ),
            grad_part,
        )

    (key_acc, value_acc), grad_queries = lax.cond(
        is_noisy, lambda: run_backward(key_rows, value_rows, allowed), backward_own
    )
    returned = shifted(
        jnp.stack(
            [
                key_acc[row_count:].reshape(row_count, model_width),
                value_acc[row_count:].reshape(row_count, model_width),
            ]
        ).astype(jnp.bfloat16),
        "stream",
        -1,
    ).astype(jnp.float32)
    grad_keys = key_acc[:row_count] + returned[0].reshape(row_count, HEADS, HEAD_DIM)
    grad_values = value_acc[:row_count].reshape(row_count, model_width) + returned[1]
    grad_q_turn = rotate_back(grad_queries.reshape(row_count, HEADS, HEAD_DIM), cosine, sine_part)
    grad_k_turn = rotate_back(grad_keys, cosine, sine_part)
    grad_proj = jnp.concatenate(
        [
            grad_q_turn.reshape(row_count, model_width),
            grad_k_turn.reshape(row_count, model_width),
            grad_values,
        ],
        axis=1,
    ).astype(jnp.bfloat16)
    grad_qkv_w = jnp.einsum("td,te->de", first_in, grad_proj, preferred_element_type=jnp.float32)
    grad_first = jnp.einsum("te,de->td", grad_proj, qkv_back, preferred_element_type=jnp.float32)
    grad_in_norm, grad_gain_one = norm_back(
        grad_first, normed_one, inverse_one, gain_back_one.astype(jnp.float32)
    )
    grad_input = (grad_after + grad_in_norm)[None]
    owned_qkv = scatter_sum(
        grad_qkv_w.astype(jnp.bfloat16).reshape(n_dev, -1, grad_qkv_w.shape[1]), ORDER_A, me
    )
    owned_out = scatter_sum(
        grad_out_w.astype(jnp.bfloat16).reshape(n_dev, -1, grad_out_w.shape[1]), ORDER_B, me
    )
    small_grad = jnp.concatenate(
        [
            g.reshape(n_dev, -1)
            for g in (grad_gain_one, grad_gain_two, grad_down_bias, grad_up_b)
        ],
        axis=1,
    )
    small_grad = jnp.pad(small_grad, ((0, 0), (0, small_width - small_grad.shape[1])))
    owned_small = scatter_sum(small_grad.reshape(n_dev, 1, small_width), ORDER_A, me)[0]

    def small_owned(i):
        start = sum(small_sizes[:i])
        return owned_small[start : start + small_sizes[i]]

    return (
        layer_out,
        grad_input,
        small_owned(0),
        owned_qkv,
        owned_out,
        small_owned(1),
        owned_up,
        small_owned(3),
        owned_down,
        small_owned(2),
    )


def solution(mesh):
    placed = (
        P("stream", "seq", None),
        P("seq", None),
        P("stream", "seq", None),
        P(("seq", "stream")),
        P(("seq", "stream"), None),
        P(("seq", "stream"), None),
        P(("seq", "stream")),
        P(("seq", "stream"), None),
        P(("seq", "stream")),
        P(("seq", "stream"), None),
        P(("seq", "stream")),
    )
    return jax.shard_map(
        local,
        mesh=mesh,
        in_specs=placed,
        out_specs=(
            P("stream", "seq", None),
            P("stream", "seq", None),
            P(("seq", "stream")),
            P(("seq", "stream"), None),
            P(("seq", "stream"), None),
            P(("seq", "stream")),
            P(("seq", "stream"), None),
            P(("seq", "stream")),
            P(("seq", "stream"), None),
            P(("seq", "stream")),
        ),
        check_vma=False,
    )
```

```python
from functools import partial
import math

import jax
import jax.numpy as jnp
from jax import lax
from jax.experimental import pallas as pl
from jax.experimental.pallas import tpu as pltpu
from jax.sharding import PartitionSpec as P

HEADS = 12
HEAD_DIM = 64
BLOCK = 16


EPSILON = 1e-05
NEG_FILL = -1e30


ALL = ("seq", "stream")
STREAM_BIT, CORE_BIT, NEAR_BIT = 1, 2, 4


def device_count():
    return lax.axis_size("seq") * lax.axis_size("stream")


def far_groups():
    bits = []
    bit = 2 * NEAR_BIT
    while bit < device_count():
        bits.append(bit)
        bit *= 2
    groups = []
    while bits:
        taken, bits = bits[:2], bits[2:]
        groups.append(taken if len(taken) == 1 else [taken[0], taken[1], taken[0] + taken[1]])
    return groups


def flip(block, mask):
    return lax.ppermute(block, ALL, [(i, i ^ mask) for i in range(device_count())])


def place(pieces, keys, me):
    total = sum(len(key) for key in keys[0])
    rows = pieces[0][0].shape[1]
    widths = [strip[0].shape[2] for strip in pieces]
    shape = (total, rows, sum(widths))
    flat = [p for strip in pieces for p in strip]

    def body(me_ref, *refs):
        out, sem = refs[-2], refs[-1]
        taken, column = 0, 0
        for key_set, width in zip(keys, widths):
            for key in key_set:
                piece = refs[taken]
                taken += 1
                for j, rel in enumerate(key):
                    to = out.at[me_ref[0] ^ rel]
                    if len(widths) > 1:
                        to = to.at[:, pl.ds(column, width)]
                    pltpu.make_async_copy(piece.at[j], to, sem).start()
            column += width
        pltpu.make_async_copy(out, out, sem).wait()

    return pl.pallas_call(
        body,
        out_shape=like(shape, flat[0].dtype),
        in_specs=[SMEM_SPEC] + [pl.BlockSpec(memory_space=pl.ANY)] * len(flat),
        out_specs=VMEM_SPEC,
        scratch_shapes=[pltpu.SemaphoreType.DMA],
        compiler_params=pltpu.CompilerParams(
            vmem_limit_bytes=2 * math.prod(shape) * (16 // min(16, rows)) * 2 + 2**20
        ),
        cost_estimate=SHORT,
    )(me, *flat)


def after(block, *others):
    return lax.optimization_barrier((block,) + others)[0]


def far_gather(shard, key):
    piece = shard[None]
    for group in far_groups():
        got = [piece] + [flip(piece, mask) for mask in group]
        key = [k ^ mask for mask in [0] + group for k in key]
        piece = jnp.concatenate(got, axis=0)
    return piece, key


def near_gather(piece, key, bit):
    return jnp.concatenate([piece, flip(piece, bit)], axis=0), key + [k ^ bit for k in key]


def last_gather(piece, key, bit, *others):
    got = flip(piece, bit)
    if others:
        got = after(got, *others)
    pieces, keys = [piece, got], [key, [k ^ bit for k in key]]
    pieces = pieces + [flip(after(p, got), CORE_BIT) for p in pieces]
    return pieces, keys + [[k ^ CORE_BIT for k in key] for key in keys]


def relative(whole, me):
    pairs = device_count() // 2
    rows = whole.reshape((pairs, 2, -1) + whole.shape[1:]) if whole.ndim < 3 else whole
    rows = rows.reshape((pairs, -1) + whole.shape[-1:])
    bits = pairs.bit_length() - 1
    rows = rows.reshape((2,) * bits + rows.shape[1:])
    for axis in range(bits):
        mine = (me[0] >> (bits - axis)) % 2
        rows = jnp.where(mine == 1, jnp.flip(rows, axis), rows)
    order = (bits - 1, bits - 2) + tuple(range(bits - 2)) + (bits, bits + 1)
    rows = rows.transpose(order).reshape((2, 2, pairs // 4) + rows.shape[-2:])
    return rows[0], rows[1]


def combine_body(bits, counts, stream_ref, *refs):
    ins, outs = refs[: sum(counts)], refs[sum(counts) :]
    stream = stream_ref[0]
    for bit, count in zip(bits, counts):
        terms, ins = ins[:count], ins[count:]
        (send, keep), outs = outs[:2], outs[2:]

        def part(own):
            if bit == STREAM_BIT:
                where = (slice(None), slice(None), pl.ds(stream if own else 1 - stream, 1))
            else:
                where = (slice(0, 1) if own else slice(1, 2),)
            out = terms[0][where].astype(F32)
            for t in terms[1:]:
                out = out + t[where].astype(F32)
            return out

        send[...] = part(False).astype(send.dtype)
        keep[...] = part(True)


def combine(stream, jobs):
    far_count = jobs[0][0][0].shape[1]
    operands, in_specs, out_shape, out_specs = [], [], [], []
    for terms, bit in jobs:
        shape = terms[0].shape
        out = list(shape)
        out[2 if bit == STREAM_BIT else 0] = 1
        out = tuple(out)

        def spec(shape):
            return pl.BlockSpec((shape[0], 1) + shape[2:], lambda j: (0, j, 0, 0, 0))

        operands += terms
        in_specs += [spec(shape)] * len(terms)
        out_shape += [like(out, BF16), like(out, F32)]
        out_specs += [spec(out)] * 2
    outs = pl.pallas_call(
        partial(combine_body, [bit for _, bit in jobs], [len(terms) for terms, _ in jobs]),
        grid=(far_count,),
        out_shape=out_shape,
        in_specs=[SMEM_SPEC] + in_specs,
        out_specs=out_specs,
        compiler_params=pltpu.CompilerParams(vmem_limit_bytes=20 * 2**20),
        cost_estimate=SHORT,
    )(stream, *operands)
    return [(outs[2 * i], outs[2 * i + 1]) for i in range(len(jobs))]


class Sum:
    def __init__(self, parts, me):
        if len(parts) == 1:
            parts = relative(parts[0], me)
        keep, self.send = parts
        self.stream = me % 2
        _, self.far_count, pair_rows, self.columns = keep.shape
        self.shape = (2, self.far_count, 2, pair_rows // 2, self.columns)
        self.terms = [keep.reshape(self.shape)]
        self.shards = None

    def flip(self, bit):
        got = flip(self.send, bit)
        self.got = got
        self.terms.append(got.reshape(self.shape) if bit == CORE_BIT else got)
        return self

    def hold(self, *others):
        self.terms[-1] = after(self.terms[-1], *others)

    def total(self):
        out = self.terms[0].astype(F32)
        for t in self.terms[1:]:
            out = out + t.astype(F32)
        return out

    def far(self):
        total = self.total().reshape(self.far_count, -1, self.columns)
        for group in reversed(far_groups()):
            part = total.shape[0] // (len(group) + 1)
            got = [
                flip(total[(i + 1) * part : (i + 2) * part].astype(BF16), mask)
                for i, mask in enumerate(group)
            ]
            total = total[:part]
            for block in got:
                total = total + block.astype(F32)
        return total[0]


def split(*jobs):
    outs = combine(jobs[0][0].stream, [(s.terms, bit) for s, bit in jobs])
    for (s, _), (send, keep) in zip(jobs, outs):
        s.send, s.terms = send, [keep]


F32, BF16 = jnp.float32, jnp.bfloat16
SHORT = pl.CostEstimate(flops=1, bytes_accessed=1, transcendentals=0)
SMEM_SPEC = pl.BlockSpec(memory_space=pltpu.SMEM)
VMEM_SPEC = pl.BlockSpec(memory_space=pltpu.VMEM)


def like(shape, kind):
    return jax.ShapeDtypeStruct(shape, kind)


def in_hbm(*arrays):
    return [pltpu.with_memory_space_constraint(a, pltpu.HBM) for a in arrays]


def doc_layout(pack_lengths, row_count):
    ends = [pack_lengths[0]]
    for i in range(1, pack_lengths.shape[0]):
        ends.append(ends[-1] + pack_lengths[i])
    seq_ends = jnp.stack(ends)
    row_index = jnp.arange(row_count, dtype=jnp.int32)
    passed = seq_ends[None, :] <= row_index[:, None]
    doc_ids = jnp.sum(passed.astype(jnp.int32), axis=1)
    starts = jnp.max(jnp.where(passed, seq_ends[None, :], 0), axis=1)
    return (doc_ids, row_index - starts)


def rotary_tables(positions, head_size):
    half_size = head_size // 2
    frequency = jnp.exp(
        jnp.arange(half_size, dtype=jnp.float32) * (-2.0 * math.log(10000.0) / head_size)
    )
    angles = positions.astype(jnp.float32)[:, None] * frequency[None, :]
    return (jnp.cos(angles), jnp.sin(angles))


PAIR = 2 * HEAD_DIM
TILE = 128
SMALL = 128
REACH = 16
LOG2_E = math.log2(math.e)
SCORE_SCALE = HEAD_DIM ** (-0.5)
GELU_A = math.sqrt(2.0 / math.pi)
GELU_B = 0.044715


def dot(a, b):
    return lax.dot_general(a, b, (((1,), (0,)), ((), ())), preferred_element_type=F32)


def dot_nt(a, b):
    return lax.dot_general(a, b, (((1,), (1,)), ((), ())), preferred_element_type=F32)


def dot_tn(a, b):
    return lax.dot_general(a, b, (((0,), (0,)), ((), ())), preferred_element_type=F32)


def whole_spec(shape):
    return pl.BlockSpec(shape, lambda *_: (0,) * len(shape))


def normed(values):
    center = values - jnp.mean(values, axis=-1, keepdims=True)
    inverse = lax.rsqrt(jnp.mean(center * center, axis=-1, keepdims=True) + EPSILON)
    return center * inverse, inverse


def norm_term(grad_out, norm, inverse, gain):
    grad_norm = grad_out * gain
    return inverse * (
        grad_norm
        - jnp.mean(grad_norm, axis=-1, keepdims=True)
        - norm * jnp.mean(grad_norm * norm, axis=-1, keepdims=True)
    )


def half_swap(block):
    lane = lax.broadcasted_iota(jnp.int32, block.shape, 1)
    quarter = HEAD_DIM // 2
    return jnp.where(
        (lane & quarter) == 0,
        pltpu.roll(block, PAIR - quarter, 1),
        pltpu.roll(block, quarter, 1),
    )


def small_row(extra, column):
    lane = lax.broadcasted_iota(jnp.int32, (8, extra.shape[1]), 1)
    return dot_nt((lane == column).astype(BF16), extra[...])[0:1, :]


def front_body(noisy_ref, tok, far_tok, extra, weight, cos, sin, first, far_first, q, k, v, kf, vf):
    width = tok.shape[1]
    g = small_row(extra, 0)
    norm, _ = normed(tok[...].astype(F32))
    first[...] = (norm * g).astype(BF16)
    is_noisy = noisy_ref[0] == 1

    @pl.when(is_noisy)
    def _():
        far_norm, _ = normed(far_tok[...].astype(F32))
        far_first[...] = (far_norm * g).astype(BF16)

    @pl.when(jnp.logical_not(is_noisy))
    def _():
        far_first[...] = first[...]

    step = 2 * PAIR
    for rows, outs in ((first, (q, k, v)), (far_first, (None, kf, vf))):
        for part, out in enumerate(outs):
            if out is None:
                continue
            for start in range(0, width, step):
                prod = dot(rows[...], weight[:, part * width + start : part * width + start + step])
                for sub in range(0, step, PAIR):
                    x = prod[:, sub : sub + PAIR]
                    if part < 2:
                        x = x * cos[...] + half_swap(x) * sin[...]
                    out[:, start + sub : start + sub + PAIR] = x.astype(BF16)


def joint_specs(width):
    return (
        pl.BlockSpec((width, SMALL), lambda *_: (0, 4 * width // SMALL)),
        pl.BlockSpec((width, 3 * width), lambda *_: (0, 0)),
        pl.BlockSpec((width, width), lambda *_: (0, 3)),
    )


def front(noisy, tok, far_tok, joint, cos, sin):
    rows, width = tok.shape
    act, table = whole_spec((rows, width)), whole_spec((rows, PAIR))
    extra, qkv, _ = joint_specs(width)
    return pl.pallas_call(
        front_body,
        grid=(1,),
        out_shape=[like((rows, width), BF16)] * 7,
        in_specs=[SMEM_SPEC, act, act, extra, qkv, table, table],
        out_specs=[act] * 7,
        compiler_params=pltpu.CompilerParams(vmem_limit_bytes=20 * 2**20),
        cost_estimate=SHORT,
    )(noisy, tok, far_tok, joint, joint, cos, sin)


def window(i, rows):
    size = TILE + 2 * REACH
    return min(max(i * TILE - REACH, 0), rows - size), size


def far_width(i, rows, noisy):
    return min(rows, (i + 1) * TILE + (0 if noisy else TILE))


def build_masks(lo, hi, code, code_row, far_bias, near_bias):
    rows = far_bias.shape[0]
    for i in range(rows // TILE):
        r = slice(i * TILE, (i + 1) * TILE)
        keys = code_row[...]
        far_bias[r, :] = jnp.where((keys >= lo[r, :]) & (keys <= hi[r, :]), 0.0, NEG_FILL)
        start, size = window(i, rows)
        near_bias[i] = jnp.where(code_row[:, start : start + size] == code[r, :], 0.0, NEG_FILL)


def stack_heads(block):
    lane = lax.broadcasted_iota(jnp.int32, block.shape, 1)
    zero = jnp.zeros_like(block)
    return jnp.concatenate(
        [jnp.where(lane < HEAD_DIM, block, zero), jnp.where(lane < HEAD_DIM, zero, block)], axis=0
    )


def unstack_heads(block):
    half = block.shape[0] // 2
    lane = lax.broadcasted_iota(jnp.int32, (half, block.shape[1]), 1)
    return jnp.where(lane < HEAD_DIM, block[:half], block[half:])


def twice(block):
    return jnp.concatenate([block, block], axis=0)


def attend_body(noisy_ref, lo, hi, code, code_row, q, k, v, kf, vf, o, lse, far_bias, near_bias):
    rows = q.shape[0]

    @pl.when(pl.program_id(0) == 0)
    def _():
        build_masks(lo, hi, code, code_row, far_bias, near_bias)

    def run(noisy):
        for i in range(rows // TILE):
            r = slice(i * TILE, (i + 1) * TILE)
            q2 = stack_heads(q[r, :])
            w = far_width(i, rows, noisy)
            s = dot_nt(q2, kf[:w, :]) * (SCORE_SCALE * LOG2_E) + twice(far_bias[r, :w])
            top = jnp.max(s, axis=-1, keepdims=True)
            if noisy:
                start, size = window(i, rows)
                n = slice(start, start + size)
                sn = dot_nt(q2, k[n, :]) * (SCORE_SCALE * LOG2_E) + twice(near_bias[i])
                top = jnp.maximum(top, jnp.max(sn, axis=-1, keepdims=True))
            e = jnp.exp2(s - top)
            total = jnp.sum(e, axis=-1, keepdims=True)
            mixed = dot(e.astype(BF16), vf[:w, :])
            if noisy:
                en = jnp.exp2(sn - top)
                total = total + jnp.sum(en, axis=-1, keepdims=True)
                mixed = mixed + dot(en.astype(BF16), v[n, :])
            o[r, :] = unstack_heads(mixed * (1.0 / total)).astype(BF16)
            lse[r, :] = unstack_heads(
                jnp.broadcast_to(top + jnp.log2(total), (2 * TILE, PAIR))
            )

    @pl.when(noisy_ref[0] == 1)
    def _():
        run(True)

    @pl.when(noisy_ref[0] == 0)
    def _():
        run(False)


def mask_scratch(rows):
    return [
        pltpu.VMEM((rows, rows), F32),
        pltpu.VMEM((rows // TILE, TILE, TILE + 2 * REACH), F32),
    ]


def attend(noisy, lo, hi, code, code_row, q, k, v, kf, vf):
    rows, width = q.shape
    pair = pl.BlockSpec((rows, PAIR), lambda j: (0, j))
    return pl.pallas_call(
        attend_body,
        grid=(width // PAIR,),
        out_shape=[like((rows, width), BF16), like((rows, width), F32)],
        in_specs=[SMEM_SPEC] + [whole_spec((rows, 1))] * 3 + [whole_spec((1, rows))] + [pair] * 5,
        out_specs=[pair] * 2,
        scratch_shapes=mask_scratch(rows),
        compiler_params=pltpu.CompilerParams(vmem_limit_bytes=12 * 2**20),
        cost_estimate=SHORT,
    )(noisy, lo, hi, code, code_row, q, k, v, kf, vf)


def attend_back_body(
    noisy_ref, lo, hi, code, code_row, q, k, v, kf, vf, o, lse, ga, out_w, cos, sin,
    dq, dk, dv, dkf, dvf, far_bias, near_bias, acc_k, acc_v, acc_kf, acc_vf,
):
    rows = q.shape[0]

    @pl.when(pl.program_id(0) == 0)
    def _():
        build_masks(lo, hi, code, code_row, far_bias, near_bias)

    go = dot_nt(ga[...], out_w[...]).astype(BF16)

    def turn_back(x):
        return (x * cos[...] - half_swap(x) * sin[...]).astype(BF16)

    def run(noisy):
        acc_kf[...] = jnp.zeros_like(acc_kf)
        acc_vf[...] = jnp.zeros_like(acc_vf)
        if noisy:
            acc_k[...] = jnp.zeros_like(acc_k)
            acc_v[...] = jnp.zeros_like(acc_v)
        parts = []
        for i in range(rows // TILE):
            r = slice(i * TILE, (i + 1) * TILE)
            q2 = stack_heads(q[r, :])
            go2 = stack_heads(go[r, :])
            delta = jnp.sum(
                go2.astype(F32) * twice(o[r, :]).astype(F32), axis=-1, keepdims=True
            )
            lse2 = jnp.concatenate([lse[r, 0:1], lse[r, HEAD_DIM : HEAD_DIM + 1]], axis=0)

            def one(keys, values, bias, acc_keys, acc_values, where):
                s = dot_nt(q2, keys) * (SCORE_SCALE * LOG2_E) + twice(bias)
                p = jnp.exp2(s - lse2)
                gp = dot_nt(go2, values)
                ds = (p * (gp - delta)).astype(BF16)
                acc_keys[where, :] += dot_tn(ds, q2)
                acc_values[where, :] += dot_tn(p.astype(BF16), go2)
                return dot(ds, keys)

            w = far_width(i, rows, noisy)
            gq = one(kf[:w, :], vf[:w, :], far_bias[r, :w], acc_kf, acc_vf, slice(0, w))
            if noisy:
                start, size = window(i, rows)
                n = slice(start, start + size)
                gq = gq + one(k[n, :], v[n, :], near_bias[i], acc_k, acc_v, n)
            parts.append(unstack_heads(gq))
        dq[...] = turn_back(jnp.concatenate(parts, axis=0) * SCORE_SCALE)
        dkf[...] = turn_back(acc_kf[...] * SCORE_SCALE)
        dvf[...] = acc_vf[...].astype(BF16)
        if noisy:
            dk[...] = turn_back(acc_k[...] * SCORE_SCALE)
            dv[...] = acc_v[...].astype(BF16)
        else:
            dk[...] = jnp.zeros_like(dk)
            dv[...] = jnp.zeros_like(dv)

    @pl.when(noisy_ref[0] == 1)
    def _():
        run(True)

    @pl.when(noisy_ref[0] == 0)
    def _():
        run(False)


def attend_back(noisy, lo, hi, code, code_row, q, k, v, kf, vf, o, lse, ga, joint, cos, sin):
    rows, width = q.shape
    pair = pl.BlockSpec((rows, PAIR), lambda j: (0, j))
    strip = pl.BlockSpec((PAIR, width), lambda j: (j, 3))
    return pl.pallas_call(
        attend_back_body,
        grid=(width // PAIR,),
        out_shape=[like((rows, width), BF16)] * 5,
        in_specs=[SMEM_SPEC]
        + [whole_spec((rows, 1))] * 3
        + [whole_spec((1, rows))]
        + [pair] * 7
        + [whole_spec((rows, width)), strip]
        + [whole_spec((rows, PAIR))] * 2,
        out_specs=[pair] * 5,
        scratch_shapes=mask_scratch(rows) + [pltpu.VMEM((rows, PAIR), F32)] * 4,
        compiler_params=pltpu.CompilerParams(vmem_limit_bytes=16 * 2**20),
        cost_estimate=SHORT,
    )(noisy, *in_hbm(lo, hi, code, code_row, q, k, v, kf, vf, o, lse, ga, joint, cos, sin))


def store_rows(value, place_ref, outs, columns):
    if len(outs) == 1:
        outs[0][:, columns] = value.astype(BF16)
        return
    keep, send = outs
    _, far_count, pair_rows, _ = keep.shape
    core, near, far = place_ref[0], place_ref[1], place_ref[2]
    for z in range(far_count):
        for y in range(2):
            start = (z * 2 + y) * 2 * pair_rows
            first = value[start : start + pair_rows].astype(BF16)
            second = value[start + pair_rows : start + 2 * pair_rows].astype(BF16)
            keep[y ^ near, z ^ far, :, columns] = jnp.where(core == 0, first, second)
            send[y ^ near, z ^ far, :, columns] = jnp.where(core == 0, second, first)


def mlp_body(n_up, *refs):
    (
        place_ref, tok, o, cot, out_w, extra, up_w, up_b, down_w,
        layer_out, gy, ga, *dups, dup_b, ddown_b, dgain,
        y1, second, out_acc, gsec_acc,
    ) = refs
    dups, ddowns = dups[:n_up], dups[n_up:]
    step = pl.program_id(0)

    @pl.when(step == 0)
    def _():
        rows = tok[...].astype(F32) + dot(o[...], out_w[...])
        y1[...] = rows
        norm, _ = normed(rows)
        second[...] = (norm * small_row(extra, 1)).astype(BF16)
        out_acc[...] = jnp.zeros_like(out_acc)
        gsec_acc[...] = jnp.zeros_like(gsec_acc)
        ddown_b[...] = jnp.sum(cot[...].astype(F32), axis=0, keepdims=True)

    x = dot(second[...], up_w[...]) + up_b[...].astype(F32)
    square = x * x
    t = jnp.tanh(x * (GELU_A + (GELU_A * GELU_B) * square))
    half_t = 0.5 + 0.5 * t
    act = (x * half_t).astype(BF16)
    slope = half_t + (0.5 * x) * (1.0 - t * t) * (GELU_A + (3.0 * GELU_A * GELU_B) * square)
    g_pre = (dot_nt(cot[...], down_w[...]) * slope).astype(BF16)
    dup_b[...] = jnp.sum(g_pre.astype(F32), axis=0, keepdims=True)
    out_acc[...] += dot(act, down_w[...])
    gsec_acc[...] += dot_nt(g_pre, up_w[...])
    down_grad = dot_tn(act, cot[...])
    if len(ddowns) == 1:
        ddowns[0][...] = down_grad.astype(BF16)
    else:
        half = down_grad.shape[0] // 2
        first, other = down_grad[:half].astype(BF16), down_grad[half:].astype(BF16)
        core = place_ref[0]
        ddowns[0][0, 0] = jnp.where(core == 0, first, other)
        ddowns[1][0, 0] = jnp.where(core == 0, other, first)
    store_rows(dot_tn(second[...], g_pre), place_ref, dups, slice(None))

    @pl.when(step == pl.num_programs(0) - 1)
    def _():
        rows = y1[...]
        layer_out[...] = (rows + out_acc[...] + small_row(extra, 2)).astype(BF16)
        norm, inverse = normed(rows)
        gs = gsec_acc[...]
        dgain[...] = jnp.sum(gs * norm, axis=0, keepdims=True)
        g = cot[...].astype(F32) + norm_term(gs, norm, inverse, small_row(extra, 1))
        gy[...] = g
        ga[...] = g.astype(BF16)


def row_grad_shapes(width, columns):
    pair_rows = 2 * (width // device_count())
    if pair_rows % 16:
        return [(width, columns)]
    return [(2, device_count() // 8, pair_rows, columns)] * 2


def mlp(place_in, tok, o, cot, joint, up_w, up_b, down_w):
    rows, width = tok.shape
    hidden = up_w.shape[1]
    ups = row_grad_shapes(width, hidden)
    pair_rows = 2 * (hidden // device_count())
    if len(ups) == 1:
        chunk = 384
        up_specs = [pl.BlockSpec((width, chunk), lambda j, _: (0, j))]
        downs = [(hidden, width)]
        down_specs = [pl.BlockSpec((chunk, width), lambda j, _: (j, 0))]
    else:
        chunk = 2 * pair_rows
        far_count = device_count() // 8
        up_specs = [pl.BlockSpec(ups[0][:3] + (chunk,), lambda j, _: (0, 0, 0, j))] * 2
        downs = [(2, far_count, pair_rows, width)] * 2
        down_specs = [
            pl.BlockSpec(
                (1, 1, pair_rows, width), lambda j, p: ((j % 2) ^ p[1], (j // 2) ^ p[2], 0, 0)
            )
        ] * 2
    act = whole_spec((rows, width))
    line = whole_spec((1, width))
    extra, _, out_w = joint_specs(width)
    up_in = pl.BlockSpec((width, chunk), lambda j, _: (0, j))
    up_line = pl.BlockSpec((1, chunk), lambda j, _: (0, j))
    down_in = pl.BlockSpec((chunk, width), lambda j, _: (j, 0))
    outs = pl.pallas_call(
        partial(mlp_body, len(ups)),
        grid_spec=pltpu.PrefetchScalarGridSpec(
            num_scalar_prefetch=1,
            grid=(hidden // chunk,),
            in_specs=[act, act, act, out_w, extra, up_in, up_line, down_in],
            out_specs=[act, act, act] + up_specs + down_specs + [up_line, line, line],
            scratch_shapes=[
                pltpu.VMEM((rows, width), F32),
                pltpu.VMEM((rows, width), BF16),
                pltpu.VMEM((rows, width), F32),
                pltpu.VMEM((rows, width), F32),
            ],
        ),
        out_shape=[like((rows, width), BF16), like((rows, width), F32), like((rows, width), BF16)]
        + [like(shape, BF16) for shape in ups + downs]
        + [like((1, hidden), F32), like((1, width), F32), like((1, width), F32)],
        compiler_params=pltpu.CompilerParams(vmem_limit_bytes=24 * 2**20),
        cost_estimate=SHORT,
    )(place_in, tok, o, cot, joint, joint, up_w, up_b, down_w)
    n = len(ups)
    return (*outs[:3], outs[3 : 3 + n], outs[3 + n : 3 + 2 * n], *outs[3 + 2 * n :])


def attn_grad_body(parts, has_lines, place_ref, *refs):
    count = sum(2 + 2 * two for two in parts) + has_lines
    ins, outs = refs[:count], refs[count:]
    at = 0
    while parts:
        rows, grads = ins[:2]
        far_rows, far_grads = ins[2:4] if parts[0] else (None, None)
        ins = ins[4:] if parts[0] else ins[2:]
        width = grads.shape[1]
        half = width // 2
        for start in range(0, width, half):
            c = slice(start, start + half)
            value = dot_tn(rows[...], grads[:, c])
            if parts[0]:
                value = value + dot_tn(far_rows[...], far_grads[:, c])
            store_rows(value, place_ref, outs, slice(at + start, at + start + half))
        at += width
        parts = parts[1:]
    if has_lines:
        lines = ins[0][...].astype(BF16)
        row = lax.broadcasted_iota(jnp.int32, (lines.shape[0], SMALL), 0)
        lane = lax.broadcasted_iota(jnp.int32, (lines.shape[0], SMALL), 1)
        store_rows(dot_tn(lines, (row == lane).astype(BF16)), place_ref, outs, slice(at, at + SMALL))


def attn_grad(place_in, pairs, lines=None):
    width = pairs[0][1].shape[1]
    has_lines = lines is not None
    shapes = row_grad_shapes(width, 2 * width + SMALL * has_lines)
    operands = [a for pair in pairs for a in pair if a is not None] + [lines] * has_lines
    return pl.pallas_call(
        partial(attn_grad_body, tuple(pair[2] is not None for pair in pairs), has_lines),
        out_shape=[like(shape, BF16) for shape in shapes],
        in_specs=[SMEM_SPEC] + [VMEM_SPEC] * len(operands),
        out_specs=[VMEM_SPEC] * len(shapes),
        compiler_params=pltpu.CompilerParams(vmem_limit_bytes=16 * 2**20),
        cost_estimate=SHORT,
    )(place_in, *operands)


def input_grad_body(noisy_ref, tok, far_tok, extra, weight, dq, dk, dv, dkf, dvf, gy, part, send, dgain):
    width = tok.shape[1]
    g = small_row(extra, 0)
    norm, inverse = normed(tok[...].astype(F32))
    own = dot_nt(dq[...], weight[:, :width])
    own = own + dot_nt(dk[...], weight[:, width : 2 * width])
    own = own + dot_nt(dv[...], weight[:, 2 * width :])
    far = dot_nt(dkf[...], weight[:, width : 2 * width]) + dot_nt(dvf[...], weight[:, 2 * width :])
    part[...] = gy[...] + norm_term(own, norm, inverse, g)
    gains = jnp.sum(own * norm, axis=0, keepdims=True)

    @pl.when(noisy_ref[0] == 1)
    def _():
        far_norm, far_inverse = normed(far_tok[...].astype(F32))
        send[...] = norm_term(far, far_norm, far_inverse, g).astype(BF16)
        dgain[...] = gains + jnp.sum(far * far_norm, axis=0, keepdims=True)

    @pl.when(noisy_ref[0] == 0)
    def _():
        part[...] += norm_term(far, norm, inverse, g)
        send[...] = jnp.zeros_like(send)
        dgain[...] = gains + jnp.sum(far * norm, axis=0, keepdims=True)


def input_grad(noisy, tok, far_tok, joint, dq, dk, dv, dkf, dvf, gy):
    rows, width = tok.shape
    act, line = whole_spec((rows, width)), whole_spec((1, width))
    extra, qkv, _ = joint_specs(width)
    return pl.pallas_call(
        input_grad_body,
        grid=(1,),
        out_shape=[like((rows, width), F32), like((rows, width), BF16), like((1, width), F32)],
        in_specs=[SMEM_SPEC, act, act, extra, qkv] + [act] * 6,
        out_specs=[act, act, line],
        compiler_params=pltpu.CompilerParams(vmem_limit_bytes=18 * 2**20),
        cost_estimate=SHORT,
    )(noisy, tok, far_tok, joint, joint, dq, dk, dv, dkf, dvf, gy)


def local(
    tokens,
    lengths,
    cotangent,
    attn_gain,
    qkv_weight,
    out_weight,
    mlp_gain,
    up_weight,
    up_bias,
    down_weight,
    down_bias,
):
    rows, width = tokens.shape[1:]
    stream = lax.axis_index("stream").astype(jnp.int32)
    me = (lax.axis_index("seq").astype(jnp.int32) * 2 + stream)[None]
    noisy = stream[None]
    n_dev = device_count()
    tok = tokens[0]
    cot = cotangent[0]

    shard_rows = qkv_weight.shape[0]
    small = [v.reshape(shard_rows, -1) for v in (attn_gain, mlp_gain, down_bias, up_bias)]
    spare = SMALL - sum(v.shape[1] for v in small)
    joint = jnp.concatenate([qkv_weight, out_weight] + small + [jnp.zeros((shard_rows, spare), BF16)], axis=1)
    cut = 2 * width
    j1, jkey = far_gather(joint, [0])
    far_tok = lax.ppermute(tok, "stream", [(0, 1)])
    u1, ukey = far_gather(after(up_weight, j1, far_tok), [0])
    a2, akey = near_gather(after(j1, far_tok)[:, :, :cut], jkey, STREAM_BIT)
    b2, bkey = near_gather(after(j1, far_tok)[:, :, cut:], jkey, NEAR_BIT)
    d1, dkey = far_gather(after(down_weight, u1, a2, b2), [0])
    a2, b2 = after(a2, b2, u1), after(b2, a2, u1)
    a3, akey = last_gather(a2, akey, NEAR_BIT, d1)
    b3, bkey = last_gather(b2, bkey, STREAM_BIT, d1)
    u2, ukey = near_gather(after(u1, d1, a3[1], b3[1]), ukey, NEAR_BIT)
    d2, dkey = near_gather(after(d1, u1, a3[1], b3[1]), dkey, STREAM_BIT)
    joint = place([a3, b3], [akey, bkey], me).reshape(width, -1)
    up_b = joint[:, 4 * width + 3 : 4 * width + 7].reshape(1, -1)

    doc_ids, positions = doc_layout(lengths[0], rows)
    cosine, sine = rotary_tables(positions, HEAD_DIM)
    cos = jnp.concatenate([cosine] * 4, axis=1)
    sin = jnp.concatenate([-sine, sine] * 2, axis=1)
    lo = doc_ids * rows
    code = lo + positions // BLOCK
    masks = (lo[:, None], (code - stream)[:, None], code[:, None], code[None, :])

    joint = after(joint, u2, d2)
    place_in = jnp.stack([(me[0] // bit) % 2 for bit in (CORE_BIT, NEAR_BIT)] + [me[0] // (2 * NEAR_BIT)])
    first, far_first, q, k, v, kf, vf = front(noisy, tok, far_tok, joint, cos, sin)
    o, lse = attend(noisy, *masks, q, k, v, kf, vf)
    u3, ukey = last_gather(u2, ukey, STREAM_BIT, o)
    d3, dkey = last_gather(d2, dkey, NEAR_BIT, o)
    up_full = place([u3], [ukey], me).reshape(width, -1)
    down_full = place([d3], [dkey], me).reshape(-1, width)
    layer_out, gy, ga, dup, ddown, dup_b, ddown_b, dgain_two = mlp(
        place_in, tok, o, cot, joint, up_full, up_b, down_full
    )
    up_sum, down_sum = Sum(dup, me).flip(CORE_BIT), Sum(ddown, me).flip(CORE_BIT)
    split((up_sum, NEAR_BIT), (down_sum, STREAM_BIT))
    up_sum.flip(NEAR_BIT)
    down_sum.flip(STREAM_BIT)
    ga = after(ga, up_sum.send, down_sum.send)
    dq, dk, dv, dkf, dvf = attend_back(
        noisy, *masks, q, k, v, kf, vf, o, lse, ga, joint, cos, sin
    )
    outs = attn_grad(place_in, [(first, dq, None, None), (first, dk, far_first, dkf)])
    front_sum = Sum(outs, me).flip(CORE_BIT)
    gy = after(gy, front_sum.send)
    part, send, dgain_one = input_grad(noisy, tok, far_tok, joint, dq, dk, dv, dkf, dvf, gy)
    up_sum.hold(part)
    down_sum.hold(part)
    split((up_sum, STREAM_BIT), (down_sum, NEAR_BIT))
    up_sum.flip(STREAM_BIT)
    down_sum.flip(NEAR_BIT)
    lines = jnp.concatenate(
        [dgain_one, dgain_two, ddown_b, dup_b.reshape(width, -1).T, jnp.zeros((1, width), F32)], axis=0
    )
    o = after(o, up_sum.send, down_sum.send)
    outs = attn_grad(place_in, [(first, dv, far_first, dvf), (o, ga, None, None)], lines)
    back_sum = Sum(outs, me).flip(CORE_BIT)
    back_sum.hold(up_sum.got, down_sum.got)
    split((front_sum, STREAM_BIT), (back_sum, NEAR_BIT))
    front_sum.flip(STREAM_BIT)
    back_sum.flip(NEAR_BIT)
    up_sum.hold(front_sum.send, back_sum.send)
    owned_up = up_sum.far()
    front_sum.hold(owned_up)
    split((front_sum, NEAR_BIT), (back_sum, STREAM_BIT))
    front_sum.flip(NEAR_BIT)
    back_sum.flip(STREAM_BIT)
    down_sum.hold(front_sum.send, back_sum.send)
    owned_down = down_sum.far()
    send = after(send, front_sum.send, back_sum.send)
    received = lax.ppermute(send, "stream", [(1, 0)])
    front_sum.hold(owned_down)
    back_sum.hold(owned_down)
    owned_front = front_sum.far()
    owned_back = back_sum.far()
    grad_input = part + after(received, owned_front, owned_back).astype(F32)
    owned_small = owned_back[:, 2 * width :]

    def small_owned(start, count):
        return owned_small[:, start : start + count].reshape(-1)

    return (
        layer_out[None],
        grad_input[None],
        small_owned(0, 1),
        jnp.concatenate([owned_front, owned_back[:, :width]], axis=1),
        owned_back[:, width : 2 * width],
        small_owned(1, 1),
        owned_up,
        small_owned(3, 4),
        owned_down,
        small_owned(2, 1),
    )


def solution(mesh):
    placed = (
        P("stream", "seq", None),
        P("seq", None),
        P("stream", "seq", None),
        P(("seq", "stream")),
        P(("seq", "stream"), None),
        P(("seq", "stream"), None),
        P(("seq", "stream")),
        P(("seq", "stream"), None),
        P(("seq", "stream")),
        P(("seq", "stream"), None),
        P(("seq", "stream")),
    )
    return jax.shard_map(
        local,
        mesh=mesh,
        in_specs=placed,
        out_specs=(
            P("stream", "seq", None),
            P("stream", "seq", None),
            P(("seq", "stream")),
            P(("seq", "stream"), None),
            P(("seq", "stream"), None),
            P(("seq", "stream")),
            P(("seq", "stream"), None),
            P(("seq", "stream")),
            P(("seq", "stream"), None),
            P(("seq", "stream")),
        ),
        check_vma=False,
    )
```

```python
from functools import partial
import math

import jax
import jax.numpy as jnp
import numpy as np
from jax import lax
from jax.experimental import pallas as pl
from jax.experimental.pallas import tpu as pltpu
from jax.sharding import PartitionSpec as P

HEADS = 12
HEAD_DIM = 64
BLOCK = 16


EPSILON = 1e-05
NEG_FILL = -1e30


ALL = ("seq", "stream")
STREAM_BIT, CORE_BIT, NEAR_BIT = 1, 2, 4


def device_count():
    return lax.axis_size("seq") * lax.axis_size("stream")


def far_groups():
    bits = []
    bit = 2 * NEAR_BIT
    while bit < device_count():
        bits.append(bit)
        bit *= 2
    groups = []
    while bits:
        taken, bits = bits[:2], bits[2:]
        groups.append(taken if len(taken) == 1 else [taken[0], taken[1], taken[0] + taken[1]])
    return groups


def flip(block, mask):
    return lax.ppermute(block, ALL, [(i, i ^ mask) for i in range(device_count())])


def place(pieces, keys, me):
    total = sum(len(key) for key in keys[0])
    rows = pieces[0][0].shape[1]
    widths = [strip[0].shape[2] for strip in pieces]
    shape = (total, rows, sum(widths))
    flat = [p for strip in pieces for p in strip]

    def body(me_ref, *refs):
        out, sem = refs[-2], refs[-1]
        taken, column = 0, 0
        for key_set, width in zip(keys, widths):
            for key in key_set:
                piece = refs[taken]
                taken += 1
                for j, rel in enumerate(key):
                    to = out.at[me_ref[0] ^ rel]
                    if len(widths) > 1:
                        to = to.at[:, pl.ds(column, width)]
                    pltpu.make_async_copy(piece.at[j], to, sem).start()
            column += width
        pltpu.make_async_copy(out, out, sem).wait()

    return pl.pallas_call(
        body,
        out_shape=like(shape, flat[0].dtype),
        in_specs=[SMEM_SPEC] + [pl.BlockSpec(memory_space=pl.ANY)] * len(flat),
        out_specs=VMEM_SPEC,
        scratch_shapes=[pltpu.SemaphoreType.DMA],
        compiler_params=pltpu.CompilerParams(
            vmem_limit_bytes=2 * math.prod(shape) * (16 // min(16, rows)) * 2 + 2**20
        ),
        cost_estimate=SHORT,
    )(me, *flat)


def after(block, *others):
    return lax.optimization_barrier((block,) + others)[0]


def far_gather(shard, key):
    piece = shard[None]
    for group in far_groups():
        got = [piece] + [flip(piece, mask) for mask in group]
        key = [k ^ mask for mask in [0] + group for k in key]
        piece = jnp.concatenate(got, axis=0)
    return piece, key


def near_gather(piece, key, bit):
    return jnp.concatenate([piece, flip(piece, bit)], axis=0), key + [k ^ bit for k in key]


def last_gather(piece, key, bit, *others):
    got = flip(piece, bit)
    if others:
        got = after(got, *others)
    pieces, keys = [piece, got], [key, [k ^ bit for k in key]]
    pieces = pieces + [flip(after(p, got), CORE_BIT) for p in pieces]
    return pieces, keys + [[k ^ CORE_BIT for k in key] for key in keys]


def relative(whole, me):
    pairs = device_count() // 2
    rows = whole.reshape((pairs, 2, -1) + whole.shape[1:]) if whole.ndim < 3 else whole
    rows = rows.reshape((pairs, -1) + whole.shape[-1:])
    bits = pairs.bit_length() - 1
    rows = rows.reshape((2,) * bits + rows.shape[1:])
    for axis in range(bits):
        mine = (me[0] >> (bits - axis)) % 2
        rows = jnp.where(mine == 1, jnp.flip(rows, axis), rows)
    order = (bits - 1, bits - 2) + tuple(range(bits - 2)) + (bits, bits + 1)
    rows = rows.transpose(order).reshape((2, 2, pairs // 4) + rows.shape[-2:])
    return rows[0], rows[1]


def combine_body(bits, counts, stream_ref, *refs):
    total = sum(sum(groups) for groups in counts)
    ins, outs = refs[:total], refs[total:]
    stream = stream_ref[0]
    for bit, groups in zip(bits, counts):
        (send, keep), outs = outs[:2], outs[2:]
        column = 0
        for count in groups:
            terms, ins = ins[:count], ins[count:]
            columns = slice(column, column + terms[0].shape[-1])
            column = columns.stop

            def part(own):
                if bit == STREAM_BIT:
                    where = (slice(None), slice(None), pl.ds(stream if own else 1 - stream, 1))
                else:
                    where = (slice(0, 1) if own else slice(1, 2),)
                out = terms[0][where].astype(F32)
                for t in terms[1:]:
                    out = out + t[where].astype(F32)
                return out

            send[..., columns] = part(False).astype(send.dtype)
            keep[..., columns] = part(True)


def combine(stream, jobs):
    far_count = jobs[0][0][0][0].shape[1]
    operands, in_specs, out_shape, out_specs = [], [], [], []

    def spec(shape):
        return pl.BlockSpec((shape[0], 1) + shape[2:], lambda j: (0, j, 0, 0, 0))

    for groups, bit in jobs:
        out = list(groups[0][0].shape)
        out[4] = sum(terms[0].shape[4] for terms in groups)
        out[2 if bit == STREAM_BIT else 0] = 1
        out = tuple(out)
        for terms in groups:
            operands += terms
            in_specs += [spec(terms[0].shape)] * len(terms)
        out_shape += [like(out, BF16), like(out, F32)]
        out_specs += [spec(out)] * 2
    outs = pl.pallas_call(
        partial(
            combine_body,
            [bit for _, bit in jobs],
            [[len(terms) for terms in groups] for groups, _ in jobs],
        ),
        grid=(far_count,),
        out_shape=out_shape,
        in_specs=[SMEM_SPEC] + in_specs,
        out_specs=out_specs,
        compiler_params=pltpu.CompilerParams(vmem_limit_bytes=20 * 2**20),
        cost_estimate=SHORT,
    )(stream, *operands)
    return [(outs[2 * i], outs[2 * i + 1]) for i in range(len(jobs))]


class Sum:
    def __init__(self, me, *strips):
        self.me, self.stream = me, me % 2
        self.groups, self.got = [], []
        for parts in strips:
            self.add(parts)

    def add(self, parts):
        if len(parts) == 1:
            parts = relative(parts[0], self.me)
        keep, send = parts
        _, self.far_count, pair_rows, columns = keep.shape
        shape = (2, self.far_count, 2, pair_rows // 2, columns)
        self.got = flip(send, CORE_BIT)
        self.groups.append([keep.reshape(shape), self.got.reshape(shape)])

    def flip(self, bit):
        self.got = flip(self.send, bit)
        self.groups[0].append(self.got)
        return self

    def hold(self, *others):
        self.groups[0][-1] = after(self.groups[0][-1], *others)

    def total(self):
        out = self.groups[0][0].astype(F32)
        for t in self.groups[0][1:]:
            out = out + t.astype(F32)
        return out


def pack_body(far_count, counts, *refs):
    ins, (keep, *sends) = refs[: sum(counts)], refs[sum(counts) :]
    _, rows, _ = keep.shape
    part = far_count // (1 + len(sends))
    column = 0
    for count in counts:
        terms, ins = ins[:count], ins[count:]
        wide, columns = terms[0].shape[-2:]
        for z in range(far_count):
            total = terms[0][0, z, 0].astype(F32)
            for t in terms[1:]:
                total = total + t[0, z, 0].astype(F32)
            out = keep if z < part else sends[z // part - 1]
            for fold in range(wide // rows):
                at = slice(column + fold * columns, column + (fold + 1) * columns)
                value = total[fold * rows : (fold + 1) * rows]
                out[z % part, :, at] = value.astype(out.dtype)
        column += wide // rows * columns


class Far:
    def __init__(self, sums, cost=None):
        groups = [s.groups[0] for s in sums]
        far_count, _, rows, _ = groups[0][0].shape[1:]
        shards = [g[0].shape[3:] for g in groups]
        columns = sum(r // rows * c for r, c in shards)
        self.order = list(reversed(far_groups()))
        part = far_count // (1 + len(self.order[0]))
        shape = (part, rows, columns)
        outs = pl.pallas_call(
            partial(pack_body, far_count, [len(g) for g in groups]),
            out_shape=[like(shape, F32)] + [like(shape, BF16)] * len(self.order[0]),
            in_specs=[VMEM_SPEC] * sum(len(g) for g in groups),
            out_specs=[VMEM_SPEC] * (1 + len(self.order[0])),
            compiler_params=pltpu.CompilerParams(vmem_limit_bytes=16 * 2**20),
            cost_estimate=cost or SHORT,
        )(*[t for g in groups for t in g])
        self.keep, self.sends = outs[0], outs[1:]

    def flip(self):
        self.got = [flip(s, mask) for s, mask in zip(self.sends, self.order[0])]
        return self

    def result(self):
        total = self.keep
        for block in self.got:
            total = total + block.astype(F32)
        for group in self.order[1:]:
            part = total.shape[0] // (len(group) + 1)
            got = [
                flip(total[(i + 1) * part : (i + 2) * part].astype(BF16), mask)
                for i, mask in enumerate(group)
            ]
            total = total[:part]
            for block in got:
                total = total + block.astype(F32)
        return total[0]


def split(*jobs):
    outs = combine(jobs[0][0].stream, [(s.groups, bit) for s, bit in jobs])
    for (s, _), (send, keep) in zip(jobs, outs):
        s.send, s.groups = send, [[keep]]


F32, BF16 = jnp.float32, jnp.bfloat16
SHORT = pl.CostEstimate(flops=1, bytes_accessed=1, transcendentals=0)
LONG = pl.CostEstimate(flops=10**10, bytes_accessed=3 * 10**7, transcendentals=0)
SMEM_SPEC = pl.BlockSpec(memory_space=pltpu.SMEM)
VMEM_SPEC = pl.BlockSpec(memory_space=pltpu.VMEM)


def like(shape, kind):
    return jax.ShapeDtypeStruct(shape, kind)


def in_hbm(*arrays):
    return [pltpu.with_memory_space_constraint(a, pltpu.HBM) for a in arrays]


def doc_layout(pack_lengths, row_count):
    ends = [pack_lengths[0]]
    for i in range(1, pack_lengths.shape[0]):
        ends.append(ends[-1] + pack_lengths[i])
    seq_ends = jnp.stack(ends)
    row_index = jnp.arange(row_count, dtype=jnp.int32)
    passed = seq_ends[None, :] <= row_index[:, None]
    doc_ids = jnp.sum(passed.astype(jnp.int32), axis=1)
    starts = jnp.max(jnp.where(passed, seq_ends[None, :], 0), axis=1)
    return (doc_ids, row_index - starts)


def rotary_tables(positions, head_size):
    half_size = head_size // 2
    frequency = jnp.exp(
        jnp.arange(half_size, dtype=jnp.float32) * (-2.0 * math.log(10000.0) / head_size)
    )
    angles = positions.astype(jnp.float32)[:, None] * frequency[None, :]
    return (jnp.cos(angles), jnp.sin(angles))


PAIR = 2 * HEAD_DIM
TILE = 128
SMALL = 128
REACH = 16
LOG2_E = math.log2(math.e)
SCORE_SCALE = HEAD_DIM ** (-0.5)
GELU_A = math.sqrt(2.0 / math.pi)
GELU_B = 0.044715


def dot(a, b):
    return lax.dot_general(a, b, (((1,), (0,)), ((), ())), preferred_element_type=F32)


def dot_nt(a, b):
    return lax.dot_general(a, b, (((1,), (1,)), ((), ())), preferred_element_type=F32)


def dot_tn(a, b):
    return lax.dot_general(a, b, (((0,), (0,)), ((), ())), preferred_element_type=F32)


def whole_spec(shape):
    return pl.BlockSpec(shape, lambda *_: (0,) * len(shape))


def normed(values):
    center = values - jnp.mean(values, axis=-1, keepdims=True)
    inverse = lax.rsqrt(jnp.mean(center * center, axis=-1, keepdims=True) + EPSILON)
    return center * inverse, inverse


def norm_term(grad_out, norm, inverse, gain):
    grad_norm = grad_out * gain
    return inverse * (
        grad_norm
        - jnp.mean(grad_norm, axis=-1, keepdims=True)
        - norm * jnp.mean(grad_norm * norm, axis=-1, keepdims=True)
    )


def half_swap(block):
    lane = lax.broadcasted_iota(jnp.int32, block.shape, 1)
    quarter = HEAD_DIM // 2
    return jnp.where(
        (lane & quarter) == 0,
        pltpu.roll(block, PAIR - quarter, 1),
        pltpu.roll(block, quarter, 1),
    )


def small_row(extra, column):
    lane = lax.broadcasted_iota(jnp.int32, (8, extra.shape[1]), 1)
    return dot_nt((lane == column).astype(BF16), extra[...])[0:1, :]


def front_body(
    noisy_ref, tok, far_tok, extra, weight, cos, sin,
    first_t, far_first_t, q, k, v, kf, vf, first, far_first,
):
    width = tok.shape[1]
    g = small_row(extra, 0)
    norm, _ = normed(tok[...].astype(F32))
    first[...] = (norm * g).astype(BF16)
    is_noisy = noisy_ref[0] == 1

    @pl.when(is_noisy)
    def _():
        far_norm, _ = normed(far_tok[...].astype(F32))
        far_first[...] = (far_norm * g).astype(BF16)

    @pl.when(jnp.logical_not(is_noisy))
    def _():
        far_first[...] = first[...]

    first_t[...] = first[...].T
    far_first_t[...] = far_first[...].T
    step = 2 * PAIR
    for rows, outs in ((first, (q, k, v)), (far_first, (None, kf, vf))):
        for part, out in enumerate(outs):
            if out is None:
                continue
            for start in range(0, width, step):
                prod = dot(rows[...], weight[:, part * width + start : part * width + start + step])
                for sub in range(0, step, PAIR):
                    x = prod[:, sub : sub + PAIR]
                    if part < 2:
                        x = x * cos[...] + half_swap(x) * sin[...]
                    out[:, start + sub : start + sub + PAIR] = x.astype(BF16)


def joint_specs(width):
    return (
        pl.BlockSpec((width, SMALL), lambda *_: (0, 4 * width // SMALL)),
        pl.BlockSpec((width, 3 * width), lambda *_: (0, 0)),
        pl.BlockSpec((width, width), lambda *_: (0, 3)),
    )


def front(noisy, tok, far_tok, joint, cos, sin):
    rows, width = tok.shape
    act, table = whole_spec((rows, width)), whole_spec((rows, PAIR))
    extra, qkv, _ = joint_specs(width)
    return pl.pallas_call(
        front_body,
        grid=(1,),
        out_shape=[like((width, rows), BF16)] * 2 + [like((rows, width), BF16)] * 5,
        in_specs=[SMEM_SPEC, act, act, extra, qkv, table, table],
        out_specs=[whole_spec((width, rows))] * 2 + [act] * 5,
        scratch_shapes=[pltpu.VMEM((rows, width), BF16)] * 2,
        compiler_params=pltpu.CompilerParams(vmem_limit_bytes=20 * 2**20),
        cost_estimate=SHORT,
    )(noisy, tok, far_tok, joint, joint, cos, sin)


def window(i, rows):
    size = TILE + 2 * REACH
    return min(max(i * TILE - REACH, 0), rows - size), size


def far_width(i, rows, noisy):
    return min(rows, (i + 1) * TILE + (0 if noisy else TILE))


def build_masks(lo, hi, code, code_row, far_bias, near_bias):
    rows = far_bias.shape[0]
    for i in range(rows // TILE):
        r = slice(i * TILE, (i + 1) * TILE)
        keys = code_row[...]
        far_bias[r, :] = jnp.where((keys >= lo[r, :]) & (keys <= hi[r, :]), 0.0, NEG_FILL)
        start, size = window(i, rows)
        near_bias[i] = jnp.where(code_row[:, start : start + size] == code[r, :], 0.0, NEG_FILL)


def build_turned_masks(code, lo_row, hi_row, code_row, far_bias, near_bias):
    rows = far_bias.shape[0]
    for i in range(rows // TILE):
        r = slice(i * TILE, (i + 1) * TILE)
        keys = code[r, :]
        far_bias[r, :] = jnp.where((keys >= lo_row[...]) & (keys <= hi_row[...]), 0.0, NEG_FILL)
        start, size = window(i, rows)
        near = code[start : start + size, :] == code_row[:, r]
        near_bias[i] = jnp.where(near, 0.0, NEG_FILL)


def beside(block):
    return jnp.concatenate([block, block], axis=1)


def stack_heads(block):
    lane = lax.broadcasted_iota(jnp.int32, block.shape, 1)
    zero = jnp.zeros_like(block)
    return jnp.concatenate(
        [jnp.where(lane < HEAD_DIM, block, zero), jnp.where(lane < HEAD_DIM, zero, block)], axis=0
    )


def unstack_heads(block):
    half = block.shape[0] // 2
    lane = lax.broadcasted_iota(jnp.int32, (half, block.shape[1]), 1)
    return jnp.where(lane < HEAD_DIM, block[:half], block[half:])


def twice(block):
    return jnp.concatenate([block, block], axis=0)


def attend_body(noisy_ref, lo, hi, code, code_row, q, k, v, kf, vf, o, lse, far_bias, near_bias):
    rows = q.shape[0]

    @pl.when(pl.program_id(0) == 0)
    def _():
        build_masks(lo, hi, code, code_row, far_bias, near_bias)

    def run(noisy):
        for i in range(rows // TILE):
            r = slice(i * TILE, (i + 1) * TILE)
            q2 = stack_heads(q[r, :])
            w = far_width(i, rows, noisy)
            s = dot_nt(q2, kf[:w, :]) * (SCORE_SCALE * LOG2_E) + twice(far_bias[r, :w])
            top = jnp.max(s, axis=-1, keepdims=True)
            if noisy:
                start, size = window(i, rows)
                n = slice(start, start + size)
                sn = dot_nt(q2, k[n, :]) * (SCORE_SCALE * LOG2_E) + twice(near_bias[i])
                top = jnp.maximum(top, jnp.max(sn, axis=-1, keepdims=True))
            e = jnp.exp2(s - top)
            total = jnp.sum(e, axis=-1, keepdims=True)
            mixed = dot(e.astype(BF16), vf[:w, :])
            if noisy:
                en = jnp.exp2(sn - top)
                total = total + jnp.sum(en, axis=-1, keepdims=True)
                mixed = mixed + dot(en.astype(BF16), v[n, :])
            o[r, :] = unstack_heads(mixed * (1.0 / total)).astype(BF16)
            log_sum = jnp.broadcast_to(top + jnp.log2(total), (2 * TILE, PAIR))
            lse[:, 2 * TILE * i : 2 * TILE * (i + 1)] = log_sum.T[:8]

    @pl.when(noisy_ref[0] == 1)
    def _():
        run(True)

    @pl.when(noisy_ref[0] == 0)
    def _():
        run(False)


def mask_scratch(rows):
    return [
        pltpu.VMEM((rows, rows), F32),
        pltpu.VMEM((rows // TILE, TILE, TILE + 2 * REACH), F32),
    ]


def attend(noisy, lo, hi, code, code_row, q, k, v, kf, vf):
    rows, width = q.shape
    pair = pl.BlockSpec((rows, PAIR), lambda j: (0, j))
    return pl.pallas_call(
        attend_body,
        grid=(width // PAIR,),
        out_shape=[like((rows, width), BF16), like((8 * (width // PAIR), 2 * rows), F32)],
        in_specs=[SMEM_SPEC] + [whole_spec((rows, 1))] * 3 + [whole_spec((1, rows))] + [pair] * 5,
        out_specs=[pair, pl.BlockSpec((8, 2 * rows), lambda j: (j, 0))],
        scratch_shapes=mask_scratch(rows),
        compiler_params=pltpu.CompilerParams(vmem_limit_bytes=12 * 2**20),
        cost_estimate=SHORT,
    )(noisy, lo, hi, code, code_row, q, k, v, kf, vf)


def attend_back_body(
    early, noisy_ref, place_ref, code, lo_row, hi_row, code_row, q, k, v, kf, vf, o, lse, ga, out_w, wq, wk, wv,
    first_t, far_first_t, cos, sin, own, far, *refs,
):
    outs, (far_bias, near_bias, acc_k, acc_v, acc_kf, acc_vf, dw_own, dw_rest) = refs[:-8], refs[-8:]
    rows = q.shape[0]

    @pl.when(pl.program_id(0) == 0)
    def _():
        build_turned_masks(code, lo_row, hi_row, code_row, far_bias, near_bias)
        own[...] = jnp.zeros_like(own)
        far[...] = jnp.zeros_like(far)

    go = dot_nt(ga[...], out_w[...]).astype(BF16)

    def turn_back(x):
        return (x * cos[...] - half_swap(x) * sin[...]).astype(BF16)

    def run(noisy):
        acc_kf[...] = jnp.zeros_like(acc_kf)
        acc_vf[...] = jnp.zeros_like(acc_vf)
        if noisy:
            acc_k[...] = jnp.zeros_like(acc_k)
            acc_v[...] = jnp.zeros_like(acc_v)
        parts = []
        for i in range(rows // TILE):
            r = slice(i * TILE, (i + 1) * TILE)
            q2 = stack_heads(q[r, :])
            go2 = stack_heads(go[r, :])
            delta = jnp.sum(
                (go2.astype(F32) * twice(o[r, :]).astype(F32)).T, axis=0, keepdims=True
            )
            log_sum = lse[0:1, 2 * TILE * i : 2 * TILE * (i + 1)]

            def one(keys, values, bias, acc_keys, acc_values, where):
                s = dot_nt(keys, q2) * (SCORE_SCALE * LOG2_E) + beside(bias)
                p = jnp.exp2(s - log_sum)
                gp = dot_nt(values, go2)
                ds = (p * (gp - delta)).astype(BF16)
                acc_keys[where, :] += dot(ds, q2)
                acc_values[where, :] += dot(p.astype(BF16), go2)
                return dot_tn(keys, ds)

            w = far_width(i, rows, noisy)
            gq = one(kf[:w, :], vf[:w, :], far_bias[:w, r], acc_kf, acc_vf, slice(0, w))
            if noisy:
                start, size = window(i, rows)
                n = slice(start, start + size)
                gq = gq + one(k[n, :], v[n, :], near_bias[i], acc_k, acc_v, n)
            parts.append(unstack_heads(gq.T))
        dq = turn_back(jnp.concatenate(parts, axis=0) * SCORE_SCALE)
        dkf = turn_back(acc_kf[...] * SCORE_SCALE)
        dvf = acc_vf[...].astype(BF16)
        g_far = jnp.concatenate([dkf, dvf], axis=1)
        w_far = jnp.concatenate([wk[...], wv[...]], axis=1)
        far[...] += dot_nt(g_far, w_far)
        dw_far = dot(far_first_t[...], g_far)
        if noisy:
            dk = turn_back(acc_k[...] * SCORE_SCALE)
            dv = acc_v[...].astype(BF16)
            g_own = jnp.concatenate([dq, dk, dv], axis=1)
            own[...] += dot_nt(g_own, jnp.concatenate([wq[...], w_far], axis=1))
            dw = dot(first_t[...], g_own)
            dw_far = dw[:, PAIR:] + dw_far
        else:
            own[...] += dot_nt(dq, wq[...])
            dw = dot(first_t[...], dq)
        dw_own[...] = dw[:, :PAIR].astype(BF16)
        dw_rest[...] = dw_far.astype(BF16)

    @pl.when(noisy_ref[0] == 1)
    def _():
        run(True)

    @pl.when(noisy_ref[0] == 0)
    def _():
        run(False)

    def store(some):
        store_rows(dw_own[...], place_ref, some, slice(0, PAIR))
        store_rows(dw_rest[...], place_ref, some, slice(PAIR, 3 * PAIR))

    half = len(outs) // 2

    @pl.when(pl.program_id(0) < early)
    def _():
        store(outs[:half])

    @pl.when(pl.program_id(0) >= early)
    def _():
        store(outs[half:])


def attend_back(noisy, place_in, masks, heads, ga, joint, first_t, far_first_t, cos, sin, early):
    rows, width = ga.shape
    pairs = width // PAIR
    pair = pl.BlockSpec((rows, PAIR), lambda j: (0, j))

    def strip(part):
        return pl.BlockSpec((width, PAIR), lambda j: (0, part * pairs + j))

    shapes, out_specs = [], []
    for first, last in ((0, early), (early, pairs)):
        for shape in row_grad_shapes(width, 3 * PAIR * (last - first)):
            shapes.append(shape)
            out_specs.append(
                pl.BlockSpec(
                    shape[:-1] + (3 * PAIR,),
                    lambda j, first=first, last=last, n=len(shape): (0,) * (n - 1)
                    + (jnp.clip(j, first, last - 1) - first,),
                )
            )
    act = whole_spec((rows, width))
    turned = whole_spec((width, rows))
    outs = pl.pallas_call(
        partial(attend_back_body, early),
        grid=(pairs,),
        out_shape=[like((rows, width), F32)] * 2 + [like(shape, BF16) for shape in shapes],
        in_specs=[SMEM_SPEC] * 2
        + [whole_spec((rows, 1))]
        + [whole_spec((1, rows))] * 3
        + [pair] * 6
        + [pl.BlockSpec((8, 2 * rows), lambda j: (j, 0))]
        + [act, pl.BlockSpec((PAIR, width), lambda j: (j, 3))]
        + [strip(0), strip(1), strip(2), turned, turned]
        + [whole_spec((rows, PAIR))] * 2,
        out_specs=[act] * 2 + out_specs,
        scratch_shapes=[
            pltpu.VMEM((rows, rows), F32),
            pltpu.VMEM((rows // TILE, TILE + 2 * REACH, TILE), F32),
        ]
        + [pltpu.VMEM((rows, PAIR), F32)] * 4
        + [pltpu.VMEM((width, PAIR), BF16), pltpu.VMEM((width, 2 * PAIR), BF16)],
        compiler_params=pltpu.CompilerParams(vmem_limit_bytes=32 * 2**20),
        cost_estimate=SHORT,
    )(
        noisy,
        place_in,
        *in_hbm(*masks, *heads, ga, joint, joint, joint, joint, first_t, far_first_t, cos, sin),
    )
    half = len(shapes) // 2
    return outs[0], outs[1], outs[2 : 2 + half], outs[2 + half :]


def store_rows(value, place_ref, outs, columns):
    if len(outs) == 1:
        outs[0][:, columns] = value.astype(BF16)
        return
    keep, send = outs
    _, far_count, pair_rows, _ = keep.shape
    core, near, far = place_ref[0], place_ref[1], place_ref[2]
    for z in range(far_count):
        for y in range(2):
            start = (z * 2 + y) * 2 * pair_rows
            first = value[start : start + pair_rows].astype(BF16)
            second = value[start + pair_rows : start + 2 * pair_rows].astype(BF16)
            keep[y ^ near, z ^ far, :, columns] = jnp.where(core == 0, first, second)
            send[y ^ near, z ^ far, :, columns] = jnp.where(core == 0, second, first)


def mlp_body(n_up, *refs):
    (
        place_ref, tok, o, cot, out_w, extra, up_w, down_w, within, which,
        layer_out, gy, ga, *dups, lines, up_lines,
        y1, second, out_acc, gsec_acc, up_line, grad_line,
    ) = refs
    dups, ddowns = dups[:n_up], dups[n_up:]
    step = pl.program_id(0)

    @pl.when(step == 0)
    def _():
        rows = tok[...].astype(F32) + dot(o[...], out_w[...])
        y1[...] = rows
        norm, _ = normed(rows)
        second[...] = (norm * small_row(extra, 1)).astype(BF16)
        out_acc[...] = jnp.zeros_like(out_acc)
        gsec_acc[...] = jnp.zeros_like(gsec_acc)
        lines[...] = jnp.zeros_like(lines)
        lines[2:3, :] = jnp.sum(cot[...].astype(F32), axis=0, keepdims=True)
        chunk = up_w.shape[1]
        quarter = chunk // 4
        row = lax.broadcasted_iota(jnp.int32, (8, SMALL), 0)
        lane = lax.broadcasted_iota(jnp.int32, (8, SMALL), 1)
        pick = (lane == row + 3).astype(BF16)
        line = lax.broadcasted_iota(jnp.int32, (8, chunk), 0)
        for j in range(up_line.shape[0]):
            four = dot_nt(pick, extra[j * quarter : (j + 1) * quarter, :]).astype(BF16)
            values = jnp.where(line == which[...], dot_nt(four, within[...]), 0.0)
            up_line[j : j + 1, :] = jnp.sum(values, axis=0, keepdims=True)

    up_b = up_line[pl.ds(step, 1), :]
    x = dot(second[...], up_w[...]) + up_b
    square = x * x
    t = jnp.tanh(x * (GELU_A + (GELU_A * GELU_B) * square))
    half_t = 0.5 + 0.5 * t
    act = (x * half_t).astype(BF16)
    slope = half_t + (0.5 * x) * (1.0 - t * t) * (GELU_A + (3.0 * GELU_A * GELU_B) * square)
    g_pre = (dot_nt(cot[...], down_w[...]) * slope).astype(BF16)
    dup_b = jnp.sum(g_pre.astype(F32), axis=0, keepdims=True)
    grad_line[pl.ds(step, 1), :] = dup_b
    out_acc[...] += dot(act, down_w[...])
    gsec_acc[...] += dot_nt(g_pre, up_w[...])
    down_grad = dot_tn(act, cot[...])
    if len(ddowns) == 1:
        ddowns[0][...] = down_grad.astype(BF16)
    else:
        pair_rows = down_grad.shape[0] // 4
        core, near = place_ref[0], place_ref[1]
        for y in range(2):
            start = 2 * y * pair_rows
            first = down_grad[start : start + pair_rows].astype(BF16)
            other = down_grad[start + pair_rows : start + 2 * pair_rows].astype(BF16)
            ddowns[0][y ^ near, 0] = jnp.where(core == 0, first, other)
            ddowns[1][y ^ near, 0] = jnp.where(core == 0, other, first)
    store_rows(dot_tn(second[...], g_pre), place_ref, dups, slice(None))

    @pl.when(step == pl.num_programs(0) - 1)
    def _():
        up_lines[...] = jnp.zeros_like(up_lines)
        for j in range(4):
            up_lines[j] = dot(jnp.where(which[...] == j, grad_line[...], 0.0).astype(BF16), within[...])
        rows = y1[...]
        layer_out[...] = (rows + out_acc[...] + small_row(extra, 2)).astype(BF16)
        norm, inverse = normed(rows)
        gs = gsec_acc[...]
        lines[1:2, :] = jnp.sum(gs * norm, axis=0, keepdims=True)
        g = cot[...].astype(F32) + norm_term(gs, norm, inverse, small_row(extra, 1))
        gy[...] = g
        ga[...] = g.astype(BF16)


def row_grad_shapes(width, columns):
    pair_rows = 2 * (width // device_count())
    if pair_rows % 16:
        return [(width, columns)]
    return [(2, device_count() // 8, pair_rows, columns)] * 2


def mlp(place_in, tok, o, cot, joint, up_w, down_w):
    rows, width = tok.shape
    hidden = up_w.shape[1]
    ups = row_grad_shapes(width, hidden)
    pair_rows = 2 * (hidden // device_count())
    if len(ups) == 1:
        chunk = hidden // 4
        up_specs = [pl.BlockSpec((width, chunk), lambda j, _: (0, j))]
        downs = [(hidden, width)]
        down_specs = [pl.BlockSpec((chunk, width), lambda j, _: (j, 0))]
    else:
        chunk = 4 * pair_rows
        far_count = device_count() // 8
        up_specs = [pl.BlockSpec(ups[0][:3] + (chunk,), lambda j, _: (0, 0, 0, j))] * 2
        downs = [(2, far_count, pair_rows, width)] * 2
        down_specs = [
            pl.BlockSpec((2, 1, pair_rows, width), lambda j, p: (0, j ^ p[2], 0, 0))
        ] * 2
    act = whole_spec((rows, width))
    extra, _, out_w = joint_specs(width)
    up_in = pl.BlockSpec((width, chunk), lambda j, _: (0, j))
    shard = hidden // device_count()
    unit = np.arange(chunk)
    within = (unit // shard) * (shard // 4) + unit % (shard // 4)
    which = (unit % shard) // (shard // 4)
    within = jnp.asarray(within[:, None] == np.arange(chunk // 4)[None, :], BF16)
    which = jnp.asarray(which[None], jnp.int32)
    down_in = pl.BlockSpec((chunk, width), lambda j, _: (j, 0))
    outs = pl.pallas_call(
        partial(mlp_body, len(ups)),
        grid_spec=pltpu.PrefetchScalarGridSpec(
            num_scalar_prefetch=1,
            grid=(hidden // chunk,),
            in_specs=[act, act, act, out_w, extra, up_in, down_in]
            + [whole_spec((chunk, chunk // 4)), whole_spec((1, chunk))],
            out_specs=[act, act, act]
            + up_specs
            + down_specs
            + [whole_spec((8, width)), whole_spec((8, hidden // chunk, chunk // 4))],
            scratch_shapes=[
                pltpu.VMEM((rows, width), F32),
                pltpu.VMEM((rows, width), BF16),
                pltpu.VMEM((rows, width), F32),
                pltpu.VMEM((rows, width), F32),
                pltpu.VMEM((hidden // chunk, chunk), F32),
                pltpu.VMEM((hidden // chunk, chunk), F32),
            ],
        ),
        out_shape=[like((rows, width), BF16), like((rows, width), F32), like((rows, width), BF16)]
        + [like(shape, BF16) for shape in ups + downs]
        + [like((8, width), F32), like((8, hidden // chunk, chunk // 4), F32)],
        compiler_params=pltpu.CompilerParams(vmem_limit_bytes=32 * 2**20),
        cost_estimate=SHORT,
    )(place_in, tok, o, cot, joint, joint, up_w, down_w, within, which)
    n = len(ups)
    return (*outs[:3], outs[3 : 3 + n], outs[3 + n : 3 + 2 * n], outs[-2], outs[-1])


def finish_body(
    noisy_ref, place_ref, tok, far_tok, extra, own, far, gy, o, ga, lines, up_lines,
    part, send, *outs
):
    width = tok.shape[1]
    g = small_row(extra, 0)
    norm, inverse = normed(tok[...].astype(F32))
    own, far = own[...], far[...]

    def put_lines(gains):
        row = lax.broadcasted_iota(jnp.int32, (8, width), 0)
        values = jnp.where(row == 0, gains, lines[...]).astype(BF16)
        row = lax.broadcasted_iota(jnp.int32, (8, SMALL), 0)
        lane = lax.broadcasted_iota(jnp.int32, (8, SMALL), 1)
        small = dot_tn(values, (row == lane).astype(BF16))
        later = (row + 3 == lane).astype(BF16)
        biases = [dot_tn(up_lines[:, j, :].astype(BF16), later) for j in range(up_lines.shape[1])]
        small = small + jnp.concatenate(biases, axis=0)
        store_rows(small, place_ref, outs, slice(width, width + SMALL))

    half = width // 2
    for start in (0, half):
        c = slice(start, start + half)
        store_rows(dot_tn(o[...], ga[:, c]), place_ref, outs, c)

    @pl.when(noisy_ref[0] == 1)
    def _():
        part[...] = gy[...] + norm_term(own, norm, inverse, g)
        far_norm, far_inverse = normed(far_tok[...].astype(F32))
        send[...] = norm_term(far, far_norm, far_inverse, g).astype(BF16)
        put_lines(jnp.sum(own * norm + far * far_norm, axis=0, keepdims=True))

    @pl.when(noisy_ref[0] == 0)
    def _():
        both = own + far
        part[...] = gy[...] + norm_term(both, norm, inverse, g)
        send[...] = jnp.zeros_like(send)
        put_lines(jnp.sum(both * norm, axis=0, keepdims=True))


def finish(noisy, place_in, tok, far_tok, joint, own, far, gy, o, ga, lines, up_lines):
    rows, width = tok.shape
    act = whole_spec((rows, width))
    extra, _, _ = joint_specs(width)
    shapes = row_grad_shapes(width, width + SMALL)
    outs = pl.pallas_call(
        finish_body,
        grid=(1,),
        out_shape=[like((rows, width), F32), like((rows, width), BF16)]
        + [like(shape, BF16) for shape in shapes],
        in_specs=[SMEM_SPEC] * 2 + [act, act, extra] + [act] * 5
        + [whole_spec((8, width)), whole_spec(up_lines.shape)],
        out_specs=[act, act] + [whole_spec(shape) for shape in shapes],
        compiler_params=pltpu.CompilerParams(vmem_limit_bytes=32 * 2**20),
        cost_estimate=SHORT,
    )(noisy, place_in, tok, far_tok, joint, own, far, gy, o, ga, lines, up_lines)
    return outs[0], outs[1], outs[2:]


def local(
    tokens,
    lengths,
    cotangent,
    attn_gain,
    qkv_weight,
    out_weight,
    mlp_gain,
    up_weight,
    up_bias,
    down_weight,
    down_bias,
):
    rows, width = tokens.shape[1:]
    stream = lax.axis_index("stream").astype(jnp.int32)
    me = (lax.axis_index("seq").astype(jnp.int32) * 2 + stream)[None]
    noisy = stream[None]
    n_dev = device_count()
    tok = tokens[0]
    cot = cotangent[0]

    shard_rows = qkv_weight.shape[0]
    small = [v.reshape(shard_rows, 1) for v in (attn_gain, mlp_gain, down_bias)]
    small.append(up_bias.reshape(4, shard_rows).T)
    spare = SMALL - sum(v.shape[1] for v in small)
    joint = jnp.concatenate([qkv_weight, out_weight] + small + [jnp.zeros((shard_rows, spare), BF16)], axis=1)
    cut = 2 * width
    j1, jkey = far_gather(joint, [0])
    far_tok = lax.ppermute(tok, "stream", [(0, 1)])
    u1, ukey = far_gather(after(up_weight, j1, far_tok), [0])
    a2, akey = near_gather(after(j1, far_tok)[:, :, :cut], jkey, STREAM_BIT)
    b2, bkey = near_gather(after(j1, far_tok)[:, :, cut:], jkey, NEAR_BIT)
    d1, dkey = far_gather(after(down_weight, u1, a2, b2), [0])
    a2, b2 = after(a2, b2, u1), after(b2, a2, u1)
    a3, akey = last_gather(a2, akey, NEAR_BIT, d1)
    b3, bkey = last_gather(b2, bkey, STREAM_BIT, d1)
    u2, ukey = near_gather(after(u1, d1, a3[1], b3[1]), ukey, NEAR_BIT)
    d2, dkey = near_gather(after(d1, u1, a3[1], b3[1]), dkey, STREAM_BIT)
    joint = place([a3, b3], [akey, bkey], me).reshape(width, -1)

    doc_ids, positions = doc_layout(lengths[0], rows)
    cosine, sine = rotary_tables(positions, HEAD_DIM)
    cos = jnp.concatenate([cosine] * 4, axis=1)
    sin = jnp.concatenate([-sine, sine] * 2, axis=1)
    lo = doc_ids * rows
    code = lo + positions // BLOCK
    masks = (lo[:, None], (code - stream)[:, None], code[:, None], code[None, :])

    joint = after(joint, u2, d2)
    place_in = jnp.stack([(me[0] // bit) % 2 for bit in (CORE_BIT, NEAR_BIT)] + [me[0] // (2 * NEAR_BIT)])
    first_t, far_first_t, q, k, v, kf, vf = front(noisy, tok, far_tok, joint, cos, sin)
    o, lse = attend(noisy, *masks, q, k, v, kf, vf)
    u3, ukey = last_gather(u2, ukey, STREAM_BIT, o)
    d3, dkey = last_gather(d2, dkey, NEAR_BIT, o)
    up_full = place([u3], [ukey], me).reshape(width, -1)
    down_full = place([d3], [dkey], me).reshape(-1, width)
    layer_out, gy, ga, dup, ddown, lines, up_lines = mlp(place_in, tok, o, cot, joint, up_full, down_full)

    up_sum, down_sum = Sum(me, dup), Sum(me, ddown)
    split((up_sum, NEAR_BIT), (down_sum, STREAM_BIT))
    up_sum.flip(NEAR_BIT)
    down_sum.flip(STREAM_BIT)
    ga_next = after(ga, up_sum.send, down_sum.send)
    heads = (q, k, v, kf, vf, o, lse)
    turned_masks = (code[:, None], lo[None], (code - stream)[None], code[None])
    pairs = width // PAIR
    early = 2 * pairs // 3
    own, far, front_outs, back_outs = attend_back(
        noisy, place_in, turned_masks, heads, ga_next, joint, first_t, far_first_t, cos, sin, early
    )
    up_sum.hold(*front_outs)
    down_sum.hold(*front_outs)
    split((up_sum, STREAM_BIT), (down_sum, NEAR_BIT))
    up_sum.flip(STREAM_BIT)
    down_sum.flip(NEAR_BIT)
    front_sum = Sum(me, [after(a, up_sum.send, down_sum.send) for a in front_outs])
    back_sum = Sum(me, [after(a, up_sum.send, down_sum.send) for a in back_outs])
    up_sum.hold(front_sum.got, back_sum.got)
    down_sum.hold(front_sum.got, back_sum.got)
    gy = after(gy, up_sum.send, down_sum.send)
    part, send, outs = finish(
        noisy, place_in, tok, far_tok, joint, own, far, gy, o, ga, lines, up_lines
    )
    back_sum.add(outs)
    half = rows // 2
    received = [lax.ppermute(send[:half], "stream", [(1, 0)])]
    mlp_far = Far([up_sum, down_sum], LONG)
    back_sum.hold(*mlp_far.sends)
    split((front_sum, STREAM_BIT), (back_sum, NEAR_BIT))
    front_sum.flip(STREAM_BIT)
    back_sum.flip(NEAR_BIT)
    mlp_far.flip()
    back_sum.hold(received[0])
    split((front_sum, NEAR_BIT), (back_sum, STREAM_BIT))
    front_sum.flip(NEAR_BIT)
    back_sum.flip(STREAM_BIT)
    back_sum.hold(*mlp_far.got)
    attn_far = Far([front_sum, back_sum])
    later = after(send[half:], *attn_far.sends)
    received.append(lax.ppermute(later, "stream", [(1, 0)]))
    owned_mlp = mlp_far.result()
    owned_attn = attn_far.flip().result()
    grad_input = part + jnp.concatenate(received, axis=0).astype(F32)

    hidden = up_weight.shape[1]
    owned_up = owned_mlp[:, :hidden]
    owned_down = owned_mlp[:, hidden:].reshape(shard_rows, -1, width)
    owned_down = owned_down.transpose(1, 0, 2).reshape(-1, width)
    owned_front = owned_attn[:, : 3 * PAIR * early]
    owned_back = owned_attn[:, 3 * PAIR * early :]
    strips = [owned_front[:, i * PAIR : (i + 1) * PAIR] for i in range(3 * early)]
    strips += [owned_back[:, i * PAIR : (i + 1) * PAIR] for i in range(3 * (pairs - early))]
    owned_qkv = jnp.concatenate([s for p in range(3) for s in strips[p::3]], axis=1)
    owned_out = owned_back[:, 3 * PAIR * (pairs - early) :]
    owned_small = owned_out[:, width:]

    def small_owned(i):
        return owned_small[:, i]

    return (
        layer_out[None],
        grad_input[None],
        small_owned(0),
        owned_qkv,
        owned_out[:, :width],
        small_owned(1),
        owned_up,
        owned_small[:, 3:7].T.reshape(-1),
        owned_down,
        small_owned(2),
    )


def solution(mesh):
    placed = (
        P("stream", "seq", None),
        P("seq", None),
        P("stream", "seq", None),
        P(("seq", "stream")),
        P(("seq", "stream"), None),
        P(("seq", "stream"), None),
        P(("seq", "stream")),
        P(("seq", "stream"), None),
        P(("seq", "stream")),
        P(("seq", "stream"), None),
        P(("seq", "stream")),
    )
    return jax.shard_map(
        local,
        mesh=mesh,
        in_specs=placed,
        out_specs=(
            P("stream", "seq", None),
            P("stream", "seq", None),
            P(("seq", "stream")),
            P(("seq", "stream"), None),
            P(("seq", "stream"), None),
            P(("seq", "stream")),
            P(("seq", "stream"), None),
            P(("seq", "stream")),
            P(("seq", "stream"), None),
            P(("seq", "stream")),
        ),
        check_vma=False,
    )
```

```python
from functools import partial
import math

import jax
import jax.numpy as jnp
import numpy as np
from jax import lax
from jax.experimental import pallas as pl
from jax.experimental.pallas import tpu as pltpu
from jax.sharding import PartitionSpec as P

HEADS = 12
HEAD_DIM = 64
BLOCK = 16


EPSILON = 1e-05
NEG_FILL = -1e30


ALL = ("seq", "stream")
STREAM_BIT, CORE_BIT, NEAR_BIT = 1, 2, 4


def device_count():
    return lax.axis_size("seq") * lax.axis_size("stream")


def far_groups():
    bits = []
    bit = 2 * NEAR_BIT
    while bit < device_count():
        bits.append(bit)
        bit *= 2
    groups = []
    while bits:
        taken, bits = bits[:2], bits[2:]
        groups.append(taken if len(taken) == 1 else [taken[0], taken[1], taken[0] + taken[1]])
    return groups


def flip(block, mask):
    return lax.ppermute(block, ALL, [(i, i ^ mask) for i in range(device_count())])


def place(pieces, keys, me):
    total = sum(len(key) for key in keys[0])
    rows = pieces[0][0].shape[1]
    widths = [strip[0].shape[2] for strip in pieces]
    shape = (total, rows, sum(widths))
    flat = [p for strip in pieces for p in strip]

    def body(me_ref, *refs):
        out, sem = refs[-2], refs[-1]
        taken, column = 0, 0
        for key_set, width in zip(keys, widths):
            for key in key_set:
                piece = refs[taken]
                taken += 1
                for j, rel in enumerate(key):
                    to = out.at[me_ref[0] ^ rel]
                    if len(widths) > 1:
                        to = to.at[:, pl.ds(column, width)]
                    pltpu.make_async_copy(piece.at[j], to, sem).start()
            column += width
        pltpu.make_async_copy(out, out, sem).wait()

    return pl.pallas_call(
        body,
        out_shape=like(shape, flat[0].dtype),
        in_specs=[SMEM_SPEC] + [pl.BlockSpec(memory_space=pl.ANY)] * len(flat),
        out_specs=VMEM_SPEC,
        scratch_shapes=[pltpu.SemaphoreType.DMA],
        compiler_params=pltpu.CompilerParams(
            vmem_limit_bytes=2 * math.prod(shape) * (16 // min(16, rows)) * 2 + 2**20
        ),
        cost_estimate=SHORT,
    )(me, *flat)


def place_pair(up, up_keys, down, down_keys, me):
    total, (rows, hidden) = sum(len(key) for key in up_keys), up[0].shape[1:]
    width = total * rows
    folds = down[0].shape[2] // width

    def body(me_ref, *refs):
        up_out, down_out, up_sem, down_sem = refs[-4:]
        for piece, key in zip(refs, up_keys):
            for j, rel in enumerate(key):
                pltpu.make_async_copy(piece.at[j], up_out.at[me_ref[0] ^ rel], up_sem).start()
        for piece, key in zip(refs[len(up) :], down_keys):
            for j, rel in enumerate(key):
                for f in range(folds):
                    part = piece.at[j, :, pl.ds(f * width, width)]
                    pltpu.make_async_copy(part, down_out.at[me_ref[0] ^ rel, f], down_sem).start()
        pltpu.make_async_copy(up_out, up_out, up_sem).wait()
        pltpu.make_async_copy(down_out, down_out, down_sem).wait()

    return pl.pallas_call(
        body,
        out_shape=[like((total, rows, hidden), BF16), like((total, folds, rows, width), BF16)],
        in_specs=[SMEM_SPEC] + [pl.BlockSpec(memory_space=pl.ANY)] * len(up + down),
        out_specs=[VMEM_SPEC] * 2,
        scratch_shapes=[pltpu.SemaphoreType.DMA] * 2,
        compiler_params=pltpu.CompilerParams(
            vmem_limit_bytes=4 * total * rows * hidden * (16 // min(16, rows)) + 2**20
        ),
        cost_estimate=SHORT,
    )(me, *up, *down)


def after(block, *others):
    return lax.optimization_barrier((block,) + others)[0]


def stack_body(count, widths, *refs):
    ins, outs = refs[:count], refs[count:]
    column = 0
    for out, width in zip(outs, widths):
        at = 0
        for piece in ins:
            out[at : at + piece.shape[0]] = piece[:, :, column : column + width]
            at += piece.shape[0]
        column += width


def stack(pieces, widths, cost):
    total, rows = sum(p.shape[0] for p in pieces), pieces[0].shape[1]
    return pl.pallas_call(
        partial(stack_body, len(pieces), widths),
        out_shape=[like((total, rows, width), BF16) for width in widths],
        in_specs=[VMEM_SPEC] * len(pieces),
        out_specs=[VMEM_SPEC] * len(widths),
        compiler_params=pltpu.CompilerParams(vmem_limit_bytes=16 * 2**20),
        cost_estimate=cost,
    )(*pieces)


def far_gather(shard, widths, cost, *others):
    piece, key = shard[None], [0]
    groups = far_groups()
    for group in groups:
        got = [piece] + [flip(piece, mask) for mask in group]
        key = [k ^ mask for mask in [0] + group for k in key]
        if group != groups[-1]:
            piece = jnp.concatenate(got, axis=0)
    if others:
        got[-1] = after(got[-1], *others)
    return stack(got, widths, cost), key


def near_gather(piece, key, bit):
    return jnp.concatenate([piece, flip(piece, bit)], axis=0), key + [k ^ bit for k in key]


def last_gather(piece, key, bit, *others):
    got = flip(piece, bit)
    if others:
        got = after(got, *others)
    pieces, keys = [piece, got], [key, [k ^ bit for k in key]]
    pieces = pieces + [flip(p, CORE_BIT) for p in pieces]
    return pieces, keys + [[k ^ CORE_BIT for k in key] for key in keys]


def relative(whole, me):
    pairs = device_count() // 2
    rows = whole.reshape((pairs, 2, -1) + whole.shape[1:]) if whole.ndim < 3 else whole
    rows = rows.reshape((pairs, -1) + whole.shape[-1:])
    bits = pairs.bit_length() - 1
    rows = rows.reshape((2,) * bits + rows.shape[1:])
    for axis in range(bits):
        mine = (me[0] >> (bits - axis)) % 2
        rows = jnp.where(mine == 1, jnp.flip(rows, axis), rows)
    order = (bits - 1, bits - 2) + tuple(range(bits - 2)) + (bits, bits + 1)
    rows = rows.transpose(order).reshape((2, 2, pairs // 4) + rows.shape[-2:])
    return rows[0], rows[1]


def combine_body(bits, counts, stream_ref, *refs):
    total = sum(sum(groups) for groups in counts)
    ins, outs = refs[:total], refs[total:]
    stream = stream_ref[0]
    for bit, groups in zip(bits, counts):
        (send, keep), outs = outs[:2], outs[2:]
        column = 0
        for count in groups:
            terms, ins = ins[:count], ins[count:]
            columns = slice(column, column + terms[0].shape[-1])
            column = columns.stop

            def part(own):
                if bit == STREAM_BIT:
                    where = (slice(None), slice(None), pl.ds(stream if own else 1 - stream, 1))
                else:
                    where = (slice(0, 1) if own else slice(1, 2),)
                out = terms[0][where].astype(F32)
                for t in terms[1:]:
                    out = out + t[where].astype(F32)
                return out

            send[..., columns] = part(False).astype(send.dtype)
            keep[..., columns] = part(True)


def combine(stream, jobs):
    far_count = jobs[0][0][0][0].shape[1]
    operands, in_specs, out_shape, out_specs = [], [], [], []

    def spec(shape):
        return pl.BlockSpec((shape[0], 1) + shape[2:], lambda j: (0, j, 0, 0, 0))

    for groups, bit in jobs:
        out = list(groups[0][0].shape)
        out[4] = sum(terms[0].shape[4] for terms in groups)
        out[2 if bit == STREAM_BIT else 0] = 1
        out = tuple(out)
        for terms in groups:
            operands += terms
            in_specs += [spec(terms[0].shape)] * len(terms)
        out_shape += [like(out, BF16), like(out, F32)]
        out_specs += [spec(out)] * 2
    outs = pl.pallas_call(
        partial(
            combine_body,
            [bit for _, bit in jobs],
            [[len(terms) for terms in groups] for groups, _ in jobs],
        ),
        grid=(far_count,),
        out_shape=out_shape,
        in_specs=[SMEM_SPEC] + in_specs,
        out_specs=out_specs,
        compiler_params=pltpu.CompilerParams(vmem_limit_bytes=20 * 2**20),
        cost_estimate=SHORT,
    )(stream, *operands)
    return [(outs[2 * i], outs[2 * i + 1]) for i in range(len(jobs))]


class Sum:
    def __init__(self, me, *strips):
        self.me, self.stream = me, me % 2
        self.groups, self.got = [], []
        for parts in strips:
            self.add(parts)

    def add(self, parts):
        if len(parts) == 1:
            parts = relative(parts[0], self.me)
        keep, send = parts
        _, self.far_count, pair_rows, columns = keep.shape
        shape = (2, self.far_count, 2, pair_rows // 2, columns)
        self.got = flip(send, CORE_BIT)
        self.groups.append([keep.reshape(shape), self.got.reshape(shape)])

    def flip(self, bit):
        self.got = flip(self.send, bit)
        self.groups[0].append(self.got)
        return self

    def hold(self, *others):
        self.groups[0][-1] = after(self.groups[0][-1], *others)

    def total(self):
        out = self.groups[0][0].astype(F32)
        for t in self.groups[0][1:]:
            out = out + t.astype(F32)
        return out


def pack_body(far_count, counts, *refs):
    ins, (keep, *sends) = refs[: sum(counts)], refs[sum(counts) :]
    _, rows, _ = keep.shape
    part = far_count // (1 + len(sends))
    column = 0
    for count in counts:
        terms, ins = ins[:count], ins[count:]
        wide, columns = terms[0].shape[-2:]
        for z in range(far_count):
            total = terms[0][0, z, 0].astype(F32)
            for t in terms[1:]:
                total = total + t[0, z, 0].astype(F32)
            out = keep if z < part else sends[z // part - 1]
            for fold in range(wide // rows):
                at = slice(column + fold * columns, column + (fold + 1) * columns)
                value = total[fold * rows : (fold + 1) * rows]
                out[z % part, :, at] = value.astype(out.dtype)
        column += wide // rows * columns


class Far:
    def __init__(self, sums, cost=None):
        groups = [s.groups[0] for s in sums]
        far_count, _, rows, _ = groups[0][0].shape[1:]
        shards = [g[0].shape[3:] for g in groups]
        columns = sum(r // rows * c for r, c in shards)
        self.order = list(reversed(far_groups()))
        part = far_count // (1 + len(self.order[0]))
        shape = (part, rows, columns)
        outs = pl.pallas_call(
            partial(pack_body, far_count, [len(g) for g in groups]),
            out_shape=[like(shape, F32)] + [like(shape, BF16)] * len(self.order[0]),
            in_specs=[VMEM_SPEC] * sum(len(g) for g in groups),
            out_specs=[VMEM_SPEC] * (1 + len(self.order[0])),
            compiler_params=pltpu.CompilerParams(vmem_limit_bytes=16 * 2**20),
            cost_estimate=cost or SHORT,
        )(*[t for g in groups for t in g])
        self.keep, self.sends = outs[0], outs[1:]

    def flip(self):
        self.got = [flip(s, mask) for s, mask in zip(self.sends, self.order[0])]
        return self.advance()

    def advance(self):
        for group in self.order[1:]:
            total = self.keep
            for block in self.got:
                total = total + block.astype(F32)
            part = total.shape[0] // (len(group) + 1)
            got = [
                flip(total[(i + 1) * part : (i + 2) * part].astype(BF16), mask)
                for i, mask in enumerate(group)
            ]
            self.keep, self.got = total[:part], got
        return self


def split(*jobs):
    outs = combine(jobs[0][0].stream, [(s.groups, bit) for s, bit in jobs])
    for (s, _), (send, keep) in zip(jobs, outs):
        s.send, s.groups = send, [[keep]]


F32, BF16 = jnp.float32, jnp.bfloat16
SHORT = pl.CostEstimate(flops=1, bytes_accessed=1, transcendentals=0)
LONG = pl.CostEstimate(flops=10**10, bytes_accessed=3 * 10**7, transcendentals=0)
SMEM_SPEC = pl.BlockSpec(memory_space=pltpu.SMEM)
VMEM_SPEC = pl.BlockSpec(memory_space=pltpu.VMEM)


def like(shape, kind):
    return jax.ShapeDtypeStruct(shape, kind)


def in_hbm(*arrays):
    return [pltpu.with_memory_space_constraint(a, pltpu.HBM) for a in arrays]


def doc_layout(pack_lengths, row_count):
    ends = [pack_lengths[0]]
    for i in range(1, pack_lengths.shape[0]):
        ends.append(ends[-1] + pack_lengths[i])
    seq_ends = jnp.stack(ends)
    row_index = jnp.arange(row_count, dtype=jnp.int32)
    passed = seq_ends[None, :] <= row_index[:, None]
    doc_ids = jnp.sum(passed.astype(jnp.int32), axis=1)
    starts = jnp.max(jnp.where(passed, seq_ends[None, :], 0), axis=1)
    return (doc_ids, row_index - starts)


def rotary_tables(positions, head_size):
    half_size = head_size // 2
    frequency = jnp.exp(
        jnp.arange(half_size, dtype=jnp.float32) * (-2.0 * math.log(10000.0) / head_size)
    )
    angles = positions.astype(jnp.float32)[:, None] * frequency[None, :]
    return (jnp.cos(angles), jnp.sin(angles))


PAIR = 2 * HEAD_DIM
TILE = 128
SMALL = 128
REACH = 16
LOG2_E = math.log2(math.e)
SCORE_SCALE = HEAD_DIM ** (-0.5)
GELU_A = math.sqrt(2.0 / math.pi)
GELU_B = 0.044715


def dot(a, b):
    return lax.dot_general(a, b, (((1,), (0,)), ((), ())), preferred_element_type=F32)


def dot_nt(a, b):
    return lax.dot_general(a, b, (((1,), (1,)), ((), ())), preferred_element_type=F32)


def dot_tn(a, b):
    return lax.dot_general(a, b, (((0,), (0,)), ((), ())), preferred_element_type=F32)


def whole_spec(shape):
    return pl.BlockSpec(shape, lambda *_: (0,) * len(shape))


def normed(values):
    center = values - jnp.mean(values, axis=-1, keepdims=True)
    inverse = lax.rsqrt(jnp.mean(center * center, axis=-1, keepdims=True) + EPSILON)
    return center * inverse, inverse


def norm_term(grad_out, norm, inverse, gain):
    grad_norm = grad_out * gain
    return inverse * (
        grad_norm
        - jnp.mean(grad_norm, axis=-1, keepdims=True)
        - norm * jnp.mean(grad_norm * norm, axis=-1, keepdims=True)
    )


def half_swap(block):
    lane = lax.broadcasted_iota(jnp.int32, block.shape, 1)
    quarter = HEAD_DIM // 2
    return jnp.where(
        (lane & quarter) == 0,
        pltpu.roll(block, PAIR - quarter, 1),
        pltpu.roll(block, quarter, 1),
    )


def prepare_body(qkv, out, up, down, attn_gain, mlp_gain, down_bias, up_bias, joint, pair_weights):
    rows, hidden = up.shape
    width = out.shape[1]
    joint[:, : 3 * width] = qkv[...]
    joint[:, 3 * width : 4 * width] = out[...]
    lane = lax.broadcasted_iota(jnp.int32, (rows, SMALL), 1)
    small = jnp.zeros((rows, SMALL), F32)
    column = 0
    for line in (attn_gain, mlp_gain, down_bias, up_bias):
        values = line[...].astype(F32)
        for start in range(0, line.shape[1], rows):
            row = lax.broadcasted_iota(jnp.int32, (rows, line.shape[1]), 0)
            item = lax.broadcasted_iota(jnp.int32, (rows, line.shape[1]), 1)
            picked = jnp.sum(jnp.where(item == row + start, values, 0.0), axis=1, keepdims=True)
            small = jnp.where(lane == column, picked, small)
            column += 1
    joint[:, 4 * width :] = small.astype(BF16)
    pair_weights[:, :hidden] = up[...]
    tall = down[...].astype(F32)
    for fold in range(down.shape[0] // rows):
        at = hidden + fold * width
        pair_weights[:, at : at + width] = tall[fold * rows : (fold + 1) * rows].astype(BF16)


def prepare(qkv, out, up, down, *lines):
    rows, width = out.shape
    shapes = ((rows, 4 * width + SMALL), (rows, up.shape[1] + down.size // rows))
    return pl.pallas_call(
        prepare_body,
        out_shape=[like(shape, BF16) for shape in shapes],
        in_specs=[VMEM_SPEC] * 8,
        out_specs=[VMEM_SPEC] * 2,
        compiler_params=pltpu.CompilerParams(vmem_limit_bytes=8 * 2**20),
        cost_estimate=SHORT,
    )(*in_hbm(qkv, out, up, down, *(v[None] for v in lines)))


def small_row(extra, column):
    lane = lax.broadcasted_iota(jnp.int32, (8, extra.shape[1]), 1)
    return dot_nt((lane == column).astype(BF16), extra[...])[0:1, :]


def both(begin, end):
    return jnp.concatenate([begin[...], end[...]], axis=0).astype(F32)


def front_body(
    noisy_ref, tok, far_tok, far_tok_end, extra, weight, cos, sin,
    first_t, far_first_t, q, k, v, kf, vf, first, far_first,
):
    width = tok.shape[1]
    g = small_row(extra, 0)
    norm, _ = normed(tok[...].astype(F32))
    first[...] = (norm * g).astype(BF16)
    is_noisy = noisy_ref[0] == 1

    @pl.when(is_noisy)
    def _():
        far_norm, _ = normed(both(far_tok, far_tok_end))
        far_first[...] = (far_norm * g).astype(BF16)

    @pl.when(jnp.logical_not(is_noisy))
    def _():
        far_first[...] = first[...]

    first_t[...] = first[...].T
    far_first_t[...] = far_first[...].T
    step = 2 * PAIR
    for rows, outs in ((first, (q, k, v)), (far_first, (None, kf, vf))):
        for part, out in enumerate(outs):
            if out is None:
                continue
            for start in range(0, width, step):
                prod = dot(rows[...], weight[:, part * width + start : part * width + start + step])
                for sub in range(0, step, PAIR):
                    x = prod[:, sub : sub + PAIR]
                    if part < 2:
                        x = x * cos[...] + half_swap(x) * sin[...]
                    out[:, start + sub : start + sub + PAIR] = x.astype(BF16)


def joint_specs(width):
    return (
        pl.BlockSpec((width, SMALL), lambda *_: (0, 4 * width // SMALL)),
        pl.BlockSpec((width, 3 * width), lambda *_: (0, 0)),
        pl.BlockSpec((width, width), lambda *_: (0, 3)),
    )


def front(noisy, tok, far_tok, far_tok_end, joint, cos, sin):
    rows, width = tok.shape
    act, table = whole_spec((rows, width)), whole_spec((rows, PAIR))
    extra, qkv, _ = joint_specs(width)
    return pl.pallas_call(
        front_body,
        grid=(1,),
        out_shape=[pltpu.HBM((width, rows), BF16)] * 2 + [pltpu.HBM((rows, width), BF16)] * 5,
        in_specs=[SMEM_SPEC, act] + [whole_spec((rows // 2, width))] * 2 + [extra, qkv, table, table],
        out_specs=[whole_spec((width, rows))] * 2 + [act] * 5,
        scratch_shapes=[pltpu.VMEM((rows, width), BF16)] * 2,
        compiler_params=pltpu.CompilerParams(vmem_limit_bytes=20 * 2**20),
        cost_estimate=SHORT,
    )(noisy, tok, far_tok, far_tok_end, joint, joint, cos, sin)


def window(i, rows):
    size = TILE + 2 * REACH
    return min(max(i * TILE - REACH, 0), rows - size), size


def far_width(i, rows, noisy):
    return min(rows, (i + 1) * TILE + (0 if noisy else TILE))


def build_masks(lo, hi, code, code_row, far_bias, near_bias):
    rows = far_bias.shape[0]
    for i in range(rows // TILE):
        r = slice(i * TILE, (i + 1) * TILE)
        keys = code_row[...]
        far_bias[r, :] = jnp.where((keys >= lo[r, :]) & (keys <= hi[r, :]), 0.0, NEG_FILL)
        start, size = window(i, rows)
        near_bias[i] = jnp.where(code_row[:, start : start + size] == code[r, :], 0.0, NEG_FILL)


def build_turned_masks(code, lo_row, hi_row, code_row, far_bias, near_bias):
    rows = far_bias.shape[0]
    for i in range(rows // TILE):
        r = slice(i * TILE, (i + 1) * TILE)
        keys = code[r, :]
        far_bias[r, :] = jnp.where((keys >= lo_row[...]) & (keys <= hi_row[...]), 0.0, NEG_FILL)
        start, size = window(i, rows)
        near = code[start : start + size, :] == code_row[:, r]
        near_bias[i] = jnp.where(near, 0.0, NEG_FILL)


def beside(block):
    return jnp.concatenate([block, block], axis=1)


def stack_heads(block):
    lane = lax.broadcasted_iota(jnp.int32, block.shape, 1)
    zero = jnp.zeros_like(block)
    return jnp.concatenate(
        [jnp.where(lane < HEAD_DIM, block, zero), jnp.where(lane < HEAD_DIM, zero, block)], axis=0
    )


def unstack_heads(block):
    half = block.shape[0] // 2
    lane = lax.broadcasted_iota(jnp.int32, (half, block.shape[1]), 1)
    return jnp.where(lane < HEAD_DIM, block[:half], block[half:])


def twice(block):
    return jnp.concatenate([block, block], axis=0)


def attend_body(noisy_ref, lo, hi, code, code_row, q, k, v, kf, vf, o, lse, far_bias, near_bias):
    rows = q.shape[0]

    @pl.when(pl.program_id(0) == 0)
    def _():
        build_masks(lo, hi, code, code_row, far_bias, near_bias)

    def run(noisy):
        for i in range(rows // TILE):
            r = slice(i * TILE, (i + 1) * TILE)
            q2 = stack_heads(q[r, :])
            w = far_width(i, rows, noisy)
            s = dot_nt(q2, kf[:w, :]) * (SCORE_SCALE * LOG2_E) + twice(far_bias[r, :w])
            top = jnp.max(s, axis=-1, keepdims=True)
            if noisy:
                start, size = window(i, rows)
                n = slice(start, start + size)
                sn = dot_nt(q2, k[n, :]) * (SCORE_SCALE * LOG2_E) + twice(near_bias[i])
                top = jnp.maximum(top, jnp.max(sn, axis=-1, keepdims=True))
            e = jnp.exp2(s - top)
            total = jnp.sum(e, axis=-1, keepdims=True)
            mixed = dot(e.astype(BF16), vf[:w, :])
            if noisy:
                en = jnp.exp2(sn - top)
                total = total + jnp.sum(en, axis=-1, keepdims=True)
                mixed = mixed + dot(en.astype(BF16), v[n, :])
            o[r, :] = unstack_heads(mixed * (1.0 / total)).astype(BF16)
            log_sum = jnp.broadcast_to(top + jnp.log2(total), (2 * TILE, PAIR))
            lse[:, 2 * TILE * i : 2 * TILE * (i + 1)] = log_sum.T[:8]

    @pl.when(noisy_ref[0] == 1)
    def _():
        run(True)

    @pl.when(noisy_ref[0] == 0)
    def _():
        run(False)


def mask_scratch(rows):
    return [
        pltpu.VMEM((rows, rows), F32),
        pltpu.VMEM((rows // TILE, TILE, TILE + 2 * REACH), F32),
    ]


def attend(noisy, lo, hi, code, code_row, q, k, v, kf, vf):
    rows, width = q.shape
    pair = pl.BlockSpec((rows, PAIR), lambda j: (0, j))
    return pl.pallas_call(
        attend_body,
        grid=(width // PAIR,),
        out_shape=[like((rows, width), BF16), like((8 * (width // PAIR), 2 * rows), F32)],
        in_specs=[SMEM_SPEC] + [whole_spec((rows, 1))] * 3 + [whole_spec((1, rows))] + [pair] * 5,
        out_specs=[pair, pl.BlockSpec((8, 2 * rows), lambda j: (j, 0))],
        scratch_shapes=mask_scratch(rows),
        compiler_params=pltpu.CompilerParams(vmem_limit_bytes=12 * 2**20),
        cost_estimate=SHORT,
    )(noisy, *in_hbm(lo, hi, code, code_row, q, k, v, kf, vf))


def attend_back_body(
    early, noisy_ref, place_ref, code, lo_row, hi_row, code_row, q, k, v, kf, vf, o, lse, ga, out_w, wq, wk, wv,
    first_t, far_first_t, cos, sin, own, far, *refs,
):
    outs, (far_bias, near_bias, acc_k, acc_v, acc_kf, acc_vf, dw_own, dw_rest) = refs[:-8], refs[-8:]
    rows = q.shape[0]

    @pl.when(pl.program_id(0) == 0)
    def _():
        build_turned_masks(code, lo_row, hi_row, code_row, far_bias, near_bias)
        own[...] = jnp.zeros_like(own)
        far[...] = jnp.zeros_like(far)

    go = dot_nt(ga[...], out_w[...]).astype(BF16)

    def turn_back(x):
        return (x * cos[...] - half_swap(x) * sin[...]).astype(BF16)

    def run(noisy):
        acc_kf[...] = jnp.zeros_like(acc_kf)
        acc_vf[...] = jnp.zeros_like(acc_vf)
        if noisy:
            acc_k[...] = jnp.zeros_like(acc_k)
            acc_v[...] = jnp.zeros_like(acc_v)
        parts = []
        for i in range(rows // TILE):
            r = slice(i * TILE, (i + 1) * TILE)
            q2 = stack_heads(q[r, :])
            go2 = stack_heads(go[r, :])
            delta = jnp.sum(
                (go2.astype(F32) * twice(o[r, :]).astype(F32)).T, axis=0, keepdims=True
            )
            log_sum = lse[0:1, 2 * TILE * i : 2 * TILE * (i + 1)]

            def one(keys, values, bias, acc_keys, acc_values, where):
                s = dot_nt(keys, q2) * (SCORE_SCALE * LOG2_E) + beside(bias)
                p = jnp.exp2(s - log_sum)
                gp = dot_nt(values, go2)
                ds = (p * (gp - delta)).astype(BF16)
                acc_keys[where, :] += dot(ds, q2)
                acc_values[where, :] += dot(p.astype(BF16), go2)
                return dot_tn(keys, ds)

            w = far_width(i, rows, noisy)
            gq = one(kf[:w, :], vf[:w, :], far_bias[:w, r], acc_kf, acc_vf, slice(0, w))
            if noisy:
                start, size = window(i, rows)
                n = slice(start, start + size)
                gq = gq + one(k[n, :], v[n, :], near_bias[i], acc_k, acc_v, n)
            parts.append(unstack_heads(gq.T))
        dq = turn_back(jnp.concatenate(parts, axis=0) * SCORE_SCALE)
        dkf = turn_back(acc_kf[...] * SCORE_SCALE)
        dvf = acc_vf[...].astype(BF16)
        g_far = jnp.concatenate([dkf, dvf], axis=1)
        w_far = jnp.concatenate([wk[...], wv[...]], axis=1)
        far[...] += dot_nt(g_far, w_far)
        dw_far = dot(far_first_t[...], g_far)
        if noisy:
            dk = turn_back(acc_k[...] * SCORE_SCALE)
            dv = acc_v[...].astype(BF16)
            g_own = jnp.concatenate([dq, dk, dv], axis=1)
            own[...] += dot_nt(g_own, jnp.concatenate([wq[...], w_far], axis=1))
            dw = dot(first_t[...], g_own)
            dw_far = dw[:, PAIR:] + dw_far
        else:
            own[...] += dot_nt(dq, wq[...])
            dw = dot(first_t[...], dq)
        dw_own[...] = dw[:, :PAIR].astype(BF16)
        dw_rest[...] = dw_far.astype(BF16)

    @pl.when(noisy_ref[0] == 1)
    def _():
        run(True)

    @pl.when(noisy_ref[0] == 0)
    def _():
        run(False)

    def store(some):
        store_rows(dw_own[...], place_ref, some, slice(0, PAIR))
        store_rows(dw_rest[...], place_ref, some, slice(PAIR, 3 * PAIR))

    half = len(outs) // 2

    @pl.when(pl.program_id(0) < early)
    def _():
        store(outs[:half])

    @pl.when(pl.program_id(0) >= early)
    def _():
        store(outs[half:])


def attend_back(noisy, place_in, masks, heads, ga, joint, first_t, far_first_t, cos, sin, early):
    rows, width = ga.shape
    pairs = width // PAIR
    pair = pl.BlockSpec((rows, PAIR), lambda j: (0, j))

    def strip(part):
        return pl.BlockSpec((width, PAIR), lambda j: (0, part * pairs + j))

    shapes, out_specs = [], []
    for first, last in ((0, early), (early, pairs)):
        for shape in row_grad_shapes(width, 3 * PAIR * (last - first)):
            shapes.append(shape)
            out_specs.append(
                pl.BlockSpec(
                    shape[:-1] + (3 * PAIR,),
                    lambda j, first=first, last=last, n=len(shape): (0,) * (n - 1)
                    + (jnp.clip(j, first, last - 1) - first,),
                )
            )
    act = whole_spec((rows, width))
    turned = whole_spec((width, rows))
    outs = pl.pallas_call(
        partial(attend_back_body, early),
        grid=(pairs,),
        out_shape=[like((rows, width), F32)] * 2 + [like(shape, BF16) for shape in shapes],
        in_specs=[SMEM_SPEC] * 2
        + [whole_spec((rows, 1))]
        + [whole_spec((1, rows))] * 3
        + [pair] * 6
        + [pl.BlockSpec((8, 2 * rows), lambda j: (j, 0))]
        + [act, pl.BlockSpec((PAIR, width), lambda j: (j, 3))]
        + [strip(0), strip(1), strip(2), turned, turned]
        + [whole_spec((rows, PAIR))] * 2,
        out_specs=[act] * 2 + out_specs,
        scratch_shapes=[
            pltpu.VMEM((rows, rows), F32),
            pltpu.VMEM((rows // TILE, TILE + 2 * REACH, TILE), F32),
        ]
        + [pltpu.VMEM((rows, PAIR), F32)] * 4
        + [pltpu.VMEM((width, PAIR), BF16), pltpu.VMEM((width, 2 * PAIR), BF16)],
        compiler_params=pltpu.CompilerParams(vmem_limit_bytes=32 * 2**20),
        cost_estimate=SHORT,
    )(
        noisy,
        place_in,
        *in_hbm(*masks, *heads, ga, joint, joint, joint, joint, first_t, far_first_t, cos, sin),
    )
    half = len(shapes) // 2
    return outs[0], outs[1], outs[2 : 2 + half], outs[2 + half :]


def store_rows(value, place_ref, outs, columns):
    if len(outs) == 1:
        outs[0][:, columns] = value.astype(BF16)
        return
    keep, send = outs
    _, far_count, pair_rows, _ = keep.shape
    core, near, far = place_ref[0], place_ref[1], place_ref[2]
    for z in range(far_count):
        for y in range(2):
            start = (z * 2 + y) * 2 * pair_rows
            first = value[start : start + pair_rows].astype(BF16)
            second = value[start + pair_rows : start + 2 * pair_rows].astype(BF16)
            keep[y ^ near, z ^ far, :, columns] = jnp.where(core == 0, first, second)
            send[y ^ near, z ^ far, :, columns] = jnp.where(core == 0, second, first)


def mlp_body(n_up, *refs):
    (
        place_ref, tok, o, cot, out_w, extra, up_w, down_w, within, which,
        layer_out, gy, ga, *dups, lines, up_lines,
        y1, second, out_acc, gsec_acc, up_line, grad_line,
    ) = refs
    dups, ddowns = dups[:n_up], dups[n_up:]
    step = pl.program_id(0)

    @pl.when(step == 0)
    def _():
        rows = tok[...].astype(F32) + dot(o[...], out_w[...])
        y1[...] = rows
        norm, _ = normed(rows)
        second[...] = (norm * small_row(extra, 1)).astype(BF16)
        out_acc[...] = jnp.zeros_like(out_acc)
        gsec_acc[...] = jnp.zeros_like(gsec_acc)
        lines[...] = jnp.zeros_like(lines)
        lines[2:3, :] = jnp.sum(cot[...].astype(F32), axis=0, keepdims=True)
        chunk = up_w.shape[1]
        quarter = chunk // 4
        row = lax.broadcasted_iota(jnp.int32, (8, SMALL), 0)
        lane = lax.broadcasted_iota(jnp.int32, (8, SMALL), 1)
        pick = (lane == row + 3).astype(BF16)
        line = lax.broadcasted_iota(jnp.int32, (8, chunk), 0)
        for j in range(up_line.shape[0]):
            four = dot_nt(pick, extra[j * quarter : (j + 1) * quarter, :]).astype(BF16)
            values = jnp.where(line == which[...], dot_nt(four, within[...]), 0.0)
            up_line[j : j + 1, :] = jnp.sum(values, axis=0, keepdims=True)

    up_b = up_line[pl.ds(step, 1), :]
    x = dot(second[...], up_w[...]) + up_b
    square = x * x
    t = jnp.tanh(x * (GELU_A + (GELU_A * GELU_B) * square))
    half_t = 0.5 + 0.5 * t
    act = (x * half_t).astype(BF16)
    slope = half_t + (0.5 * x) * (1.0 - t * t) * (GELU_A + (3.0 * GELU_A * GELU_B) * square)
    g_pre = (dot_nt(cot[...], down_w[...]) * slope).astype(BF16)
    dup_b = jnp.sum(g_pre.astype(F32), axis=0, keepdims=True)
    grad_line[pl.ds(step, 1), :] = dup_b
    out_acc[...] += dot(act, down_w[...])
    gsec_acc[...] += dot_nt(g_pre, up_w[...])
    down_grad = dot_tn(act, cot[...])
    if len(ddowns) == 1:
        ddowns[0][...] = down_grad.astype(BF16)
    else:
        pair_rows = down_grad.shape[0] // 4
        core, near = place_ref[0], place_ref[1]
        for y in range(2):
            start = 2 * y * pair_rows
            first = down_grad[start : start + pair_rows].astype(BF16)
            other = down_grad[start + pair_rows : start + 2 * pair_rows].astype(BF16)
            ddowns[0][y ^ near, 0] = jnp.where(core == 0, first, other)
            ddowns[1][y ^ near, 0] = jnp.where(core == 0, other, first)
    store_rows(dot_tn(second[...], g_pre), place_ref, dups, slice(None))

    @pl.when(step == pl.num_programs(0) - 1)
    def _():
        up_lines[...] = jnp.zeros_like(up_lines)
        for j in range(4):
            up_lines[j] = dot(jnp.where(which[...] == j, grad_line[...], 0.0).astype(BF16), within[...])
        rows = y1[...]
        layer_out[...] = (rows + out_acc[...] + small_row(extra, 2)).astype(BF16)
        norm, inverse = normed(rows)
        gs = gsec_acc[...]
        lines[1:2, :] = jnp.sum(gs * norm, axis=0, keepdims=True)
        g = cot[...].astype(F32) + norm_term(gs, norm, inverse, small_row(extra, 1))
        gy[...] = g
        ga[...] = g.astype(BF16)


def row_grad_shapes(width, columns):
    pair_rows = 2 * (width // device_count())
    if pair_rows % 16:
        return [(width, columns)]
    return [(2, device_count() // 8, pair_rows, columns)] * 2


def mlp(place_in, tok, o, cot, joint, up_w, down_w):
    rows, width = tok.shape
    hidden = up_w.shape[1]
    ups = row_grad_shapes(width, hidden)
    pair_rows = 2 * (hidden // device_count())
    if len(ups) == 1:
        chunk = hidden // 4
        up_specs = [pl.BlockSpec((width, chunk), lambda j, _: (0, j))]
        downs = [(hidden, width)]
        down_specs = [pl.BlockSpec((chunk, width), lambda j, _: (j, 0))]
    else:
        chunk = 4 * pair_rows
        far_count = device_count() // 8
        up_specs = [pl.BlockSpec(ups[0][:3] + (chunk,), lambda j, _: (0, 0, 0, j))] * 2
        downs = [(2, far_count, pair_rows, width)] * 2
        down_specs = [
            pl.BlockSpec((2, 1, pair_rows, width), lambda j, p: (0, j ^ p[2], 0, 0))
        ] * 2
    act = whole_spec((rows, width))
    extra, _, out_w = joint_specs(width)
    up_in = pl.BlockSpec((width, chunk), lambda j, _: (0, j))
    shard = hidden // device_count()
    unit = np.arange(chunk)
    within = (unit // shard) * (shard // 4) + unit % (shard // 4)
    which = (unit % shard) // (shard // 4)
    within = jnp.asarray(within[:, None] == np.arange(chunk // 4)[None, :], BF16)
    which = jnp.asarray(which[None], jnp.int32)
    down_in = pl.BlockSpec((chunk, width), lambda j, _: (j, 0))
    outs = pl.pallas_call(
        partial(mlp_body, len(ups)),
        grid_spec=pltpu.PrefetchScalarGridSpec(
            num_scalar_prefetch=1,
            grid=(hidden // chunk,),
            in_specs=[act, act, act, out_w, extra, up_in, down_in]
            + [whole_spec((chunk, chunk // 4)), whole_spec((1, chunk))],
            out_specs=[act, act, act]
            + up_specs
            + down_specs
            + [whole_spec((8, width)), whole_spec((8, hidden // chunk, chunk // 4))],
            scratch_shapes=[
                pltpu.VMEM((rows, width), F32),
                pltpu.VMEM((rows, width), BF16),
                pltpu.VMEM((rows, width), F32),
                pltpu.VMEM((rows, width), F32),
                pltpu.VMEM((hidden // chunk, chunk), F32),
                pltpu.VMEM((hidden // chunk, chunk), F32),
            ],
        ),
        out_shape=[like((rows, width), BF16), like((rows, width), F32), like((rows, width), BF16)]
        + [like(shape, BF16) for shape in ups + downs]
        + [like((8, width), F32), like((8, hidden // chunk, chunk // 4), F32)],
        compiler_params=pltpu.CompilerParams(vmem_limit_bytes=32 * 2**20),
        cost_estimate=SHORT,
    )(place_in, *in_hbm(tok), o, *in_hbm(cot), joint, joint, up_w, down_w, *in_hbm(within, which))
    n = len(ups)
    return (*outs[:3], outs[3 : 3 + n], outs[3 + n : 3 + 2 * n], outs[-2], outs[-1])


def finish_body(
    noisy_ref, place_ref, tok, far_tok, far_tok_end, extra, own, far, gy, o, ga, lines, up_lines,
    part, send, *outs
):
    width = tok.shape[1]
    g = small_row(extra, 0)
    norm, inverse = normed(tok[...].astype(F32))
    own, far = own[...], far[...]

    def put_lines(gains):
        row = lax.broadcasted_iota(jnp.int32, (8, width), 0)
        values = jnp.where(row == 0, gains, lines[...]).astype(BF16)
        row = lax.broadcasted_iota(jnp.int32, (8, SMALL), 0)
        lane = lax.broadcasted_iota(jnp.int32, (8, SMALL), 1)
        small = dot_tn(values, (row == lane).astype(BF16))
        later = (row + 3 == lane).astype(BF16)
        biases = [dot_tn(up_lines[:, j, :].astype(BF16), later) for j in range(up_lines.shape[1])]
        small = small + jnp.concatenate(biases, axis=0)
        store_rows(small, place_ref, outs, slice(width, width + SMALL))

    half = width // 2
    for start in (0, half):
        c = slice(start, start + half)
        store_rows(dot_tn(o[...], ga[:, c]), place_ref, outs, c)

    @pl.when(noisy_ref[0] == 1)
    def _():
        part[...] = gy[...] + norm_term(own, norm, inverse, g)
        far_norm, far_inverse = normed(both(far_tok, far_tok_end))
        send[...] = norm_term(far, far_norm, far_inverse, g).astype(BF16)
        put_lines(jnp.sum(own * norm + far * far_norm, axis=0, keepdims=True))

    @pl.when(noisy_ref[0] == 0)
    def _():
        both = own + far
        part[...] = gy[...] + norm_term(both, norm, inverse, g)
        send[...] = jnp.zeros_like(send)
        put_lines(jnp.sum(both * norm, axis=0, keepdims=True))


def finish(noisy, place_in, tok, far_tok, far_tok_end, joint, own, far, gy, o, ga, lines, up_lines):
    rows, width = tok.shape
    act = whole_spec((rows, width))
    extra, _, _ = joint_specs(width)
    shapes = row_grad_shapes(width, width + SMALL)
    outs = pl.pallas_call(
        finish_body,
        grid=(1,),
        out_shape=[like((rows, width), F32)]
        + [like((rows, width), BF16)]
        + [like(shape, BF16) for shape in shapes],
        in_specs=[SMEM_SPEC] * 2
        + [act]
        + [whole_spec((rows // 2, width))] * 2
        + [extra]
        + [act] * 5
        + [whole_spec((8, width)), whole_spec(up_lines.shape)],
        out_specs=[act, act] + [whole_spec(shape) for shape in shapes],
        compiler_params=pltpu.CompilerParams(vmem_limit_bytes=32 * 2**20),
        cost_estimate=SHORT,
    )(noisy, place_in, tok, far_tok, far_tok_end, joint, own, far, gy, o, ga, lines, up_lines)
    return outs[0], outs[1], outs[2:]


def last_sum_body(pairs, keep, *refs):
    got, (qkv, out, small) = refs[:-3], refs[-3:]
    total = keep[0]
    for g in got:
        total = total + g[0].astype(F32)
    width = out.shape[1]
    for i in range(pairs):
        at = 3 * PAIR * i
        for p in range(3):
            qkv[:, p * width + i * PAIR : p * width + (i + 1) * PAIR] = total[
                :, at + p * PAIR : at + (p + 1) * PAIR
            ]
    out[...] = total[:, 3 * width : 4 * width]
    small[...] = total[:, 4 * width :]


def last_sum(keep, got, width):
    rows = keep.shape[1]
    shapes = ((rows, 3 * width), (rows, width), (rows, SMALL))
    return pl.pallas_call(
        partial(last_sum_body, width // PAIR),
        out_shape=[like(shape, F32) for shape in shapes],
        in_specs=[VMEM_SPEC] * (1 + len(got)),
        out_specs=[VMEM_SPEC] * 3,
        compiler_params=pltpu.CompilerParams(vmem_limit_bytes=8 * 2**20),
        cost_estimate=SHORT,
    )(keep, *got)


def mlp_sum_body(keep, *refs):
    got, (up, down) = refs[:-2], refs[-2:]
    total = keep[0]
    for g in got:
        total = total + g[0].astype(F32)
    rows, hidden = up.shape
    width = down.shape[1]
    up[...] = total[:, :hidden]
    for f in range(down.shape[0] // rows):
        at = hidden + f * width
        down[f * rows : (f + 1) * rows, :] = total[:, at : at + width]


def mlp_sum(keep, got, hidden, width):
    _, rows, columns = keep.shape
    return pl.pallas_call(
        mlp_sum_body,
        out_shape=[like((rows, hidden), F32), like(((columns - hidden) // width * rows, width), F32)],
        in_specs=[VMEM_SPEC] * (1 + len(got)),
        out_specs=[VMEM_SPEC] * 2,
        compiler_params=pltpu.CompilerParams(vmem_limit_bytes=8 * 2**20),
        cost_estimate=LONG,
    )(keep, *got)


def add_body(part, got, out):
    out[...] = part[...] + got[...].astype(F32)


def add(part, got):
    rows, width = part.shape
    block = pl.BlockSpec((rows // 4, width), lambda j: (j, 0))
    return pl.pallas_call(
        add_body,
        grid=(4,),
        out_shape=like((rows, width), F32),
        in_specs=[block] * 2,
        out_specs=block,
        compiler_params=pltpu.CompilerParams(vmem_limit_bytes=8 * 2**20),
        cost_estimate=LONG,
    )(part, got)


def local(
    tokens,
    lengths,
    cotangent,
    attn_gain,
    qkv_weight,
    out_weight,
    mlp_gain,
    up_weight,
    up_bias,
    down_weight,
    down_bias,
):
    rows, width = tokens.shape[1:]
    stream = lax.axis_index("stream").astype(jnp.int32)
    me = (lax.axis_index("seq").astype(jnp.int32) * 2 + stream)[None]
    noisy = stream[None]
    n_dev = device_count()
    tok = tokens[0]
    cot = cotangent[0]

    shard_rows, hidden = up_weight.shape
    joint, pair_weights = prepare(
        qkv_weight, out_weight, up_weight, down_weight, attn_gain, mlp_gain, down_bias, up_bias
    )
    cut = 2 * width
    half = rows // 2
    far_tok = [lax.ppermute(tok[:half], "stream", [(0, 1)])]
    far_tok.append(lax.ppermute(after(tok[half:], far_tok[0]), "stream", [(0, 1)]))
    (a1, b1), jkey = far_gather(joint, (cut, joint.shape[1] - cut), SHORT, far_tok[0])
    (u1, d1), ukey = far_gather(after(pair_weights, a1), (hidden, hidden), LONG)
    a2, akey = near_gather(a1, jkey, STREAM_BIT)
    b2, bkey = near_gather(b1, jkey, NEAR_BIT)
    a2, b2 = after(a2, far_tok[1]), after(b2, far_tok[1])
    a3, akey = last_gather(a2, akey, NEAR_BIT, u1, d1)
    b3, bkey = last_gather(b2, bkey, STREAM_BIT, u1, d1)
    u1, d1 = after(u1, a3[1], b3[1]), after(d1, a3[1], b3[1])
    u_got, d_got = flip(u1, NEAR_BIT), flip(d1, STREAM_BIT)
    joint = place([a3, b3], [akey, bkey], me).reshape(width, -1)

    doc_ids, positions = doc_layout(lengths[0], rows)
    cosine, sine = rotary_tables(positions, HEAD_DIM)
    cos = jnp.concatenate([cosine] * 4, axis=1)
    sin = jnp.concatenate([-sine, sine] * 2, axis=1)
    lo = doc_ids * rows
    code = lo + positions // BLOCK
    masks = (lo[:, None], (code - stream)[:, None], code[:, None], code[None, :])

    place_in = jnp.stack([(me[0] // bit) % 2 for bit in (CORE_BIT, NEAR_BIT)] + [me[0] // (2 * NEAR_BIT)])
    first_t, far_first_t, q, k, v, kf, vf = front(noisy, tok, *far_tok, joint, cos, sin)
    u_got, d_got = after(u_got, q), after(d_got, q)
    u2, d2 = jnp.concatenate([u1, u_got], axis=0), jnp.concatenate([d1, d_got], axis=0)
    u_got, d_got = flip(u2, STREAM_BIT), flip(d2, NEAR_BIT)
    u_core, d_core = flip(u2, CORE_BIT), flip(d2, CORE_BIT)
    o, lse = attend(noisy, *masks, after(q, u2, d2), k, v, kf, vf)
    u_got, d_got = after(u_got, o), after(d_got, o)
    u3 = [u2, u_got, u_core, flip(u_got, CORE_BIT)]
    d3 = [d2, d_got, d_core, flip(d_got, CORE_BIT)]

    def keys(*bits):
        out = [ukey]
        for bit in bits:
            out = out + [[key ^ bit for key in line] for line in out]
        return [out[0] + out[1], out[2] + out[3], out[4] + out[5], out[6] + out[7]]

    ukey, dkey = keys(NEAR_BIT, STREAM_BIT, CORE_BIT), keys(STREAM_BIT, NEAR_BIT, CORE_BIT)
    up_full, down_full = place_pair(u3, ukey, d3, dkey, me)
    layer_out, gy, ga, dup, ddown, lines, up_lines = mlp(
        place_in, tok, o, cot, joint, up_full.reshape(width, -1), down_full.reshape(-1, width)
    )

    up_sum, down_sum = Sum(me, dup), Sum(me, ddown)
    split((up_sum, NEAR_BIT), (down_sum, STREAM_BIT))
    up_sum.flip(NEAR_BIT)
    down_sum.flip(STREAM_BIT)
    ga_next = after(ga, up_sum.send, down_sum.send)
    heads = (q, k, v, kf, vf, o, lse)
    turned_masks = (code[:, None], lo[None], (code - stream)[None], code[None])
    pairs = width // PAIR
    early = 2 * pairs // 3
    own, far, front_outs, back_outs = attend_back(
        noisy, place_in, turned_masks, heads, ga_next, joint, first_t, far_first_t, cos, sin, early
    )
    up_sum.hold(*front_outs)
    down_sum.hold(*front_outs)
    split((up_sum, STREAM_BIT), (down_sum, NEAR_BIT))
    up_sum.flip(STREAM_BIT)
    down_sum.flip(NEAR_BIT)
    front_sum = Sum(me, [after(a, up_sum.send, down_sum.send) for a in front_outs])
    back_sum = Sum(me, [after(a, up_sum.send, down_sum.send) for a in back_outs])
    up_sum.hold(front_sum.got, back_sum.got)
    down_sum.hold(front_sum.got, back_sum.got)
    gy = after(gy, up_sum.send, down_sum.send)
    part, send, outs = finish(
        noisy, place_in, tok, *far_tok, joint, own, far, gy, o, ga, lines, up_lines
    )
    back_sum.add(outs)
    mlp_far = Far([up_sum, down_sum], LONG)
    back_sum.hold(*mlp_far.sends)
    split((front_sum, STREAM_BIT), (back_sum, NEAR_BIT))
    front_sum.flip(STREAM_BIT)
    back_sum.flip(NEAR_BIT)
    mlp_far.flip()
    split((front_sum, NEAR_BIT), (back_sum, STREAM_BIT))
    front_sum.flip(NEAR_BIT)
    back_sum.flip(STREAM_BIT)
    owned_up, owned_down = mlp_sum(mlp_far.keep, mlp_far.got, hidden, width)
    back_sum.hold(owned_up, owned_down)
    received = lax.ppermute(after(send, front_sum.send, back_sum.send), "stream", [(1, 0)])
    attn_far = Far([front_sum, back_sum])
    attn_far.flip()
    grad_input = add(part, received)
    attn_far.got[0] = after(attn_far.got[0], grad_input)
    owned_qkv, owned_out, owned_small = last_sum(attn_far.keep, attn_far.got, width)

    def small_owned(i):
        return owned_small[:, i]

    return (
        layer_out[None],
        grad_input[None],
        small_owned(0),
        owned_qkv,
        owned_out,
        small_owned(1),
        owned_up,
        owned_small[:, 3:7].T.reshape(-1),
        owned_down,
        small_owned(2),
    )


def solution(mesh):
    placed = (
        P("stream", "seq", None),
        P("seq", None),
        P("stream", "seq", None),
        P(("seq", "stream")),
        P(("seq", "stream"), None),
        P(("seq", "stream"), None),
        P(("seq", "stream")),
        P(("seq", "stream"), None),
        P(("seq", "stream")),
        P(("seq", "stream"), None),
        P(("seq", "stream")),
    )
    return jax.shard_map(
        local,
        mesh=mesh,
        in_specs=placed,
        out_specs=(
            P("stream", "seq", None),
            P("stream", "seq", None),
            P(("seq", "stream")),
            P(("seq", "stream"), None),
            P(("seq", "stream"), None),
            P(("seq", "stream")),
            P(("seq", "stream"), None),
            P(("seq", "stream")),
            P(("seq", "stream"), None),
            P(("seq", "stream")),
        ),
        check_vma=False,
    )
```

```python
from functools import partial
import math

import jax
import jax.numpy as jnp
import numpy as np
from jax import lax
from jax.experimental import pallas as pl
from jax.experimental.pallas import tpu as pltpu
from jax.sharding import PartitionSpec as P

HEADS = 12
HEAD_DIM = 64
BLOCK = 16


EPSILON = 1e-05
NEG_FILL = -1e30


ALL = ("seq", "stream")
STREAM_BIT, CORE_BIT, NEAR_BIT = 1, 2, 4


def device_count():
    return lax.axis_size("seq") * lax.axis_size("stream")


def far_groups():
    bits = []
    bit = 2 * NEAR_BIT
    while bit < device_count():
        bits.append(bit)
        bit *= 2
    groups = []
    while bits:
        taken, bits = bits[:2], bits[2:]
        groups.append(taken if len(taken) == 1 else [taken[0], taken[1], taken[0] + taken[1]])
    return groups


def flip(block, mask):
    return lax.ppermute(block, ALL, [(i, i ^ mask) for i in range(device_count())])


def place(pieces, keys, me):
    total = sum(len(key) for key in keys[0])
    rows = pieces[0][0].shape[1]
    widths = [strip[0].shape[2] for strip in pieces]
    shape = (total, rows, sum(widths))
    flat = [p for strip in pieces for p in strip]

    def body(me_ref, *refs):
        out, sem = refs[-2], refs[-1]
        taken, column = 0, 0
        for key_set, width in zip(keys, widths):
            for key in key_set:
                piece = refs[taken]
                taken += 1
                for j, rel in enumerate(key):
                    to = out.at[me_ref[0] ^ rel]
                    if len(widths) > 1:
                        to = to.at[:, pl.ds(column, width)]
                    pltpu.make_async_copy(piece.at[j], to, sem).start()
            column += width
        pltpu.make_async_copy(out, out, sem).wait()

    return pl.pallas_call(
        body,
        out_shape=like(shape, flat[0].dtype),
        in_specs=[SMEM_SPEC] + [pl.BlockSpec(memory_space=pl.ANY)] * len(flat),
        out_specs=VMEM_SPEC,
        scratch_shapes=[pltpu.SemaphoreType.DMA],
        compiler_params=pltpu.CompilerParams(
            vmem_limit_bytes=2 * math.prod(shape) * (16 // min(16, rows)) * 2 + 2**20
        ),
        cost_estimate=SHORT,
    )(me, *flat)


def place_pair(up, up_keys, down, down_keys, me):
    total, (rows, hidden) = sum(len(key) for key in up_keys), up[0].shape[1:]
    width = total * rows
    folds = down[0].shape[2] // width

    def body(me_ref, *refs):
        up_out, down_out, up_sem, down_sem = refs[-4:]
        for piece, key in zip(refs, up_keys):
            for j, rel in enumerate(key):
                pltpu.make_async_copy(piece.at[j], up_out.at[me_ref[0] ^ rel], up_sem).start()
        for piece, key in zip(refs[len(up) :], down_keys):
            for j, rel in enumerate(key):
                for f in range(folds):
                    part = piece.at[j, :, pl.ds(f * width, width)]
                    pltpu.make_async_copy(part, down_out.at[me_ref[0] ^ rel, f], down_sem).start()
        pltpu.make_async_copy(up_out, up_out, up_sem).wait()
        pltpu.make_async_copy(down_out, down_out, down_sem).wait()

    return pl.pallas_call(
        body,
        out_shape=[like((total, rows, hidden), BF16), like((total, folds, rows, width), BF16)],
        in_specs=[SMEM_SPEC] + [pl.BlockSpec(memory_space=pl.ANY)] * len(up + down),
        out_specs=[VMEM_SPEC] * 2,
        scratch_shapes=[pltpu.SemaphoreType.DMA] * 2,
        compiler_params=pltpu.CompilerParams(
            vmem_limit_bytes=4 * total * rows * hidden * (16 // min(16, rows)) + 2**20
        ),
        cost_estimate=SHORT,
    )(me, *up, *down)


def after(block, *others):
    return lax.optimization_barrier((block,) + others)[0]


def stack_body(count, widths, *refs):
    ins, outs = refs[:count], refs[count:]
    column = 0
    for out, width in zip(outs, widths):
        at = 0
        for piece in ins:
            out[at : at + piece.shape[0]] = piece[:, :, column : column + width]
            at += piece.shape[0]
        column += width


def stack(pieces, widths, cost):
    total, rows = sum(p.shape[0] for p in pieces), pieces[0].shape[1]
    return pl.pallas_call(
        partial(stack_body, len(pieces), widths),
        out_shape=[like((total, rows, width), BF16) for width in widths],
        in_specs=[VMEM_SPEC] * len(pieces),
        out_specs=[VMEM_SPEC] * len(widths),
        compiler_params=pltpu.CompilerParams(vmem_limit_bytes=16 * 2**20),
        cost_estimate=cost,
    )(*pieces)


def far_gather(shard, widths, cost, *others):
    piece, key = shard[None], [0]
    groups = far_groups()
    for group in groups:
        got = [piece] + [flip(piece, mask) for mask in group]
        key = [k ^ mask for mask in [0] + group for k in key]
        if group != groups[-1]:
            piece = jnp.concatenate(got, axis=0)
    if others:
        got[-1] = after(got[-1], *others)
    return stack(got, widths, cost), key


def near_gather(piece, key, bit):
    return jnp.concatenate([piece, flip(piece, bit)], axis=0), key + [k ^ bit for k in key]


def last_gather(piece, key, bit, *others):
    got = flip(piece, bit)
    if others:
        got = after(got, *others)
    pieces, keys = [piece, got], [key, [k ^ bit for k in key]]
    pieces = pieces + [flip(after(piece, *others), CORE_BIT), flip(got, CORE_BIT)]
    return pieces, keys + [[k ^ CORE_BIT for k in key] for key in keys]


def relative(whole, me):
    pairs = device_count() // 2
    rows = whole.reshape((pairs, 2, -1) + whole.shape[1:]) if whole.ndim < 3 else whole
    rows = rows.reshape((pairs, -1) + whole.shape[-1:])
    bits = pairs.bit_length() - 1
    rows = rows.reshape((2,) * bits + rows.shape[1:])
    for axis in range(bits):
        mine = (me[0] >> (bits - axis)) % 2
        rows = jnp.where(mine == 1, jnp.flip(rows, axis), rows)
    order = (bits - 1, bits - 2) + tuple(range(bits - 2)) + (bits, bits + 1)
    rows = rows.transpose(order).reshape((2, 2, pairs // 4) + rows.shape[-2:])
    return rows[0], rows[1]


def combine_body(bits, counts, stream_ref, *refs):
    total = sum(sum(groups) for groups in counts)
    ins, outs = refs[:total], refs[total:]
    stream = stream_ref[0]
    for bit, groups in zip(bits, counts):
        (send, keep), outs = outs[:2], outs[2:]
        column = 0
        for count in groups:
            terms, ins = ins[:count], ins[count:]
            columns = slice(column, column + terms[0].shape[-1])
            column = columns.stop

            def part(own):
                if bit == STREAM_BIT:
                    where = (slice(None), slice(None), pl.ds(stream if own else 1 - stream, 1))
                else:
                    where = (slice(0, 1) if own else slice(1, 2),)
                out = terms[0][where].astype(F32)
                for t in terms[1:]:
                    out = out + t[where].astype(F32)
                return out

            send[..., columns] = part(False).astype(send.dtype)
            keep[..., columns] = part(True)


def combine(stream, jobs):
    far_count = jobs[0][0][0][0].shape[1]
    operands, in_specs, out_shape, out_specs = [], [], [], []

    def spec(shape):
        return pl.BlockSpec((shape[0], 1) + shape[2:], lambda j: (0, j, 0, 0, 0))

    for groups, bit in jobs:
        out = list(groups[0][0].shape)
        out[4] = sum(terms[0].shape[4] for terms in groups)
        out[2 if bit == STREAM_BIT else 0] = 1
        out = tuple(out)
        for terms in groups:
            operands += terms
            in_specs += [spec(terms[0].shape)] * len(terms)
        out_shape += [like(out, BF16), like(out, F32)]
        out_specs += [spec(out)] * 2
    outs = pl.pallas_call(
        partial(
            combine_body,
            [bit for _, bit in jobs],
            [[len(terms) for terms in groups] for groups, _ in jobs],
        ),
        grid=(far_count,),
        out_shape=out_shape,
        in_specs=[SMEM_SPEC] + in_specs,
        out_specs=out_specs,
        compiler_params=pltpu.CompilerParams(vmem_limit_bytes=20 * 2**20),
        cost_estimate=SHORT,
    )(stream, *operands)
    return [(outs[2 * i], outs[2 * i + 1]) for i in range(len(jobs))]


class Sum:
    def __init__(self, me, *strips):
        self.me, self.stream = me, me % 2
        self.groups, self.got = [], []
        for parts in strips:
            self.add(parts)

    def add(self, parts):
        if len(parts) == 1:
            parts = relative(parts[0], self.me)
        keep, send = parts
        _, self.far_count, pair_rows, columns = keep.shape
        shape = (2, self.far_count, 2, pair_rows // 2, columns)
        self.got = flip(send, CORE_BIT)
        self.groups.append([keep.reshape(shape), self.got.reshape(shape)])

    def flip(self, bit):
        self.got = flip(self.send, bit)
        self.groups[0].append(self.got)
        return self

    def hold(self, *others):
        self.groups[0][-1] = after(self.groups[0][-1], *others)

    def total(self):
        out = self.groups[0][0].astype(F32)
        for t in self.groups[0][1:]:
            out = out + t.astype(F32)
        return out


def pack_body(far_count, counts, *refs):
    ins, (keep, *sends) = refs[: sum(counts)], refs[sum(counts) :]
    _, rows, _ = keep.shape
    part = far_count // (1 + len(sends))
    column = 0
    for count in counts:
        terms, ins = ins[:count], ins[count:]
        wide, columns = terms[0].shape[-2:]
        for z in range(far_count):
            total = terms[0][0, z, 0].astype(F32)
            for t in terms[1:]:
                total = total + t[0, z, 0].astype(F32)
            out = keep if z < part else sends[z // part - 1]
            for fold in range(wide // rows):
                at = slice(column + fold * columns, column + (fold + 1) * columns)
                value = total[fold * rows : (fold + 1) * rows]
                out[z % part, :, at] = value.astype(out.dtype)
        column += wide // rows * columns


class Far:
    def __init__(self, sums, cost=None):
        groups = [s.groups[0] for s in sums]
        far_count, _, rows, _ = groups[0][0].shape[1:]
        shards = [g[0].shape[3:] for g in groups]
        columns = sum(r // rows * c for r, c in shards)
        self.order = list(reversed(far_groups()))
        part = far_count // (1 + len(self.order[0]))
        shape = (part, rows, columns)
        outs = pl.pallas_call(
            partial(pack_body, far_count, [len(g) for g in groups]),
            out_shape=[like(shape, F32)] + [like(shape, BF16)] * len(self.order[0]),
            in_specs=[VMEM_SPEC] * sum(len(g) for g in groups),
            out_specs=[VMEM_SPEC] * (1 + len(self.order[0])),
            compiler_params=pltpu.CompilerParams(vmem_limit_bytes=16 * 2**20),
            cost_estimate=cost or SHORT,
        )(*[t for g in groups for t in g])
        self.keep, self.sends = outs[0], outs[1:]

    def flip(self):
        self.got = [flip(s, mask) for s, mask in zip(self.sends, self.order[0])]
        return self.advance()

    def advance(self):
        for group in self.order[1:]:
            total = self.keep
            for block in self.got:
                total = total + block.astype(F32)
            part = total.shape[0] // (len(group) + 1)
            got = [
                flip(total[(i + 1) * part : (i + 2) * part].astype(BF16), mask)
                for i, mask in enumerate(group)
            ]
            self.keep, self.got = total[:part], got
        return self


def split(*jobs):
    outs = combine(jobs[0][0].stream, [(s.groups, bit) for s, bit in jobs])
    for (s, _), (send, keep) in zip(jobs, outs):
        s.send, s.groups = send, [[keep]]


F32, BF16 = jnp.float32, jnp.bfloat16
SHORT = pl.CostEstimate(flops=1, bytes_accessed=1, transcendentals=0)
LONG = pl.CostEstimate(flops=10**10, bytes_accessed=3 * 10**7, transcendentals=0)
SMEM_SPEC = pl.BlockSpec(memory_space=pltpu.SMEM)
VMEM_SPEC = pl.BlockSpec(memory_space=pltpu.VMEM)


def like(shape, kind):
    return jax.ShapeDtypeStruct(shape, kind)


def in_hbm(*arrays):
    return [pltpu.with_memory_space_constraint(a, pltpu.HBM) for a in arrays]


def doc_layout(pack_lengths, row_count):
    ends = [pack_lengths[0]]
    for i in range(1, pack_lengths.shape[0]):
        ends.append(ends[-1] + pack_lengths[i])
    seq_ends = jnp.stack(ends)
    row_index = jnp.arange(row_count, dtype=jnp.int32)
    passed = seq_ends[None, :] <= row_index[:, None]
    doc_ids = jnp.sum(passed.astype(jnp.int32), axis=1)
    starts = jnp.max(jnp.where(passed, seq_ends[None, :], 0), axis=1)
    return (doc_ids, row_index - starts)


def rotary_tables(positions, head_size):
    half_size = head_size // 2
    frequency = jnp.exp(
        jnp.arange(half_size, dtype=jnp.float32) * (-2.0 * math.log(10000.0) / head_size)
    )
    angles = positions.astype(jnp.float32)[:, None] * frequency[None, :]
    return (jnp.cos(angles), jnp.sin(angles))


PAIR = 2 * HEAD_DIM
TILE = 128
SMALL = 128
REACH = 16
LOG2_E = math.log2(math.e)
SCORE_SCALE = HEAD_DIM ** (-0.5)
GELU_A = math.sqrt(2.0 / math.pi)
GELU_B = 0.044715


def dot(a, b):
    return lax.dot_general(a, b, (((1,), (0,)), ((), ())), preferred_element_type=F32)


def dot_nt(a, b):
    return lax.dot_general(a, b, (((1,), (1,)), ((), ())), preferred_element_type=F32)


def dot_tn(a, b):
    return lax.dot_general(a, b, (((0,), (0,)), ((), ())), preferred_element_type=F32)


def whole_spec(shape):
    return pl.BlockSpec(shape, lambda *_: (0,) * len(shape))


def normed(values):
    center = values - jnp.mean(values, axis=-1, keepdims=True)
    inverse = lax.rsqrt(jnp.mean(center * center, axis=-1, keepdims=True) + EPSILON)
    return center * inverse, inverse


def norm_term(grad_out, norm, inverse, gain):
    grad_norm = grad_out * gain
    return inverse * (
        grad_norm
        - jnp.mean(grad_norm, axis=-1, keepdims=True)
        - norm * jnp.mean(grad_norm * norm, axis=-1, keepdims=True)
    )


def half_swap(block):
    lane = lax.broadcasted_iota(jnp.int32, block.shape, 1)
    quarter = HEAD_DIM // 2
    return jnp.where(
        (lane & quarter) == 0,
        pltpu.roll(block, PAIR - quarter, 1),
        pltpu.roll(block, quarter, 1),
    )


def prepare_body(qkv, out, up, down, attn_gain, mlp_gain, down_bias, up_bias, joint, pair_weights):
    rows, hidden = up.shape
    width = out.shape[1]
    joint[:, : 3 * width] = qkv[...]
    joint[:, 3 * width : 4 * width] = out[...]
    lane = lax.broadcasted_iota(jnp.int32, (rows, SMALL), 1)
    small = jnp.zeros((rows, SMALL), F32)
    column = 0
    for line in (attn_gain, mlp_gain, down_bias, up_bias):
        values = line[...].astype(F32)
        for start in range(0, line.shape[1], rows):
            row = lax.broadcasted_iota(jnp.int32, (rows, line.shape[1]), 0)
            item = lax.broadcasted_iota(jnp.int32, (rows, line.shape[1]), 1)
            picked = jnp.sum(jnp.where(item == row + start, values, 0.0), axis=1, keepdims=True)
            small = jnp.where(lane == column, picked, small)
            column += 1
    joint[:, 4 * width :] = small.astype(BF16)
    pair_weights[:, :hidden] = up[...]
    tall = down[...].astype(F32)
    for fold in range(down.shape[0] // rows):
        at = hidden + fold * width
        pair_weights[:, at : at + width] = tall[fold * rows : (fold + 1) * rows].astype(BF16)


def prepare(qkv, out, up, down, *lines):
    rows, width = out.shape
    shapes = ((rows, 4 * width + SMALL), (rows, up.shape[1] + down.size // rows))
    return pl.pallas_call(
        prepare_body,
        out_shape=[like(shape, BF16) for shape in shapes],
        in_specs=[VMEM_SPEC] * 8,
        out_specs=[VMEM_SPEC] * 2,
        compiler_params=pltpu.CompilerParams(vmem_limit_bytes=8 * 2**20),
        cost_estimate=SHORT,
    )(*in_hbm(qkv, out, up, down, *(v[None] for v in lines)))


def small_row(extra, column):
    lane = lax.broadcasted_iota(jnp.int32, (8, extra.shape[1]), 1)
    return dot_nt((lane == column).astype(BF16), extra[...])[0:1, :]


def both(begin, end):
    return jnp.concatenate([begin[...], end[...]], axis=0).astype(F32)


def front_body(
    noisy_ref, tok, far_tok, far_tok_end, extra, weight, cos, sin,
    first_t, far_first_t, q, k, v, kf, vf, first, far_first,
):
    width = tok.shape[1]
    g = small_row(extra, 0)
    norm, _ = normed(tok[...].astype(F32))
    first[...] = (norm * g).astype(BF16)
    is_noisy = noisy_ref[0] == 1

    @pl.when(is_noisy)
    def _():
        far_norm, _ = normed(both(far_tok, far_tok_end))
        far_first[...] = (far_norm * g).astype(BF16)

    @pl.when(jnp.logical_not(is_noisy))
    def _():
        far_first[...] = first[...]

    first_t[...] = first[...].T
    far_first_t[...] = far_first[...].T
    step = 2 * PAIR
    for rows, outs in ((first, (q, k, v)), (far_first, (None, kf, vf))):
        for part, out in enumerate(outs):
            if out is None:
                continue
            for start in range(0, width, step):
                prod = dot(rows[...], weight[:, part * width + start : part * width + start + step])
                for sub in range(0, step, PAIR):
                    x = prod[:, sub : sub + PAIR]
                    if part < 2:
                        x = x * cos[...] + half_swap(x) * sin[...]
                    out[:, start + sub : start + sub + PAIR] = x.astype(BF16)


def joint_specs(width):
    return (
        pl.BlockSpec((width, SMALL), lambda *_: (0, 4 * width // SMALL)),
        pl.BlockSpec((width, 3 * width), lambda *_: (0, 0)),
        pl.BlockSpec((width, width), lambda *_: (0, 3)),
    )


def front(noisy, tok, far_tok, far_tok_end, joint, cos, sin):
    rows, width = tok.shape
    act, table = whole_spec((rows, width)), whole_spec((rows, PAIR))
    extra, qkv, _ = joint_specs(width)
    return pl.pallas_call(
        front_body,
        grid=(1,),
        out_shape=[pltpu.HBM((width, rows), BF16)] * 2 + [pltpu.HBM((rows, width), BF16)] * 5,
        in_specs=[SMEM_SPEC, act] + [whole_spec((rows // 2, width))] * 2 + [extra, qkv, table, table],
        out_specs=[whole_spec((width, rows))] * 2 + [act] * 5,
        scratch_shapes=[pltpu.VMEM((rows, width), BF16)] * 2,
        compiler_params=pltpu.CompilerParams(vmem_limit_bytes=20 * 2**20),
        cost_estimate=SHORT,
    )(noisy, tok, far_tok, far_tok_end, joint, joint, cos, sin)


def window(i, rows):
    size = TILE + 2 * REACH
    return min(max(i * TILE - REACH, 0), rows - size), size


def far_width(i, rows, noisy):
    return min(rows, (i + 1) * TILE + (0 if noisy else TILE))


def build_masks(lo, hi, code, code_row, far_bias, near_bias):
    rows = far_bias.shape[0]
    for i in range(rows // TILE):
        r = slice(i * TILE, (i + 1) * TILE)
        keys = code_row[...]
        far_bias[r, :] = jnp.where((keys >= lo[r, :]) & (keys <= hi[r, :]), 0.0, NEG_FILL)
        start, size = window(i, rows)
        near_bias[i] = jnp.where(code_row[:, start : start + size] == code[r, :], 0.0, NEG_FILL)


def build_turned_masks(code, lo_row, hi_row, code_row, far_bias, near_bias):
    rows = far_bias.shape[0]
    for i in range(rows // TILE):
        r = slice(i * TILE, (i + 1) * TILE)
        keys = code[r, :]
        far_bias[r, :] = jnp.where((keys >= lo_row[...]) & (keys <= hi_row[...]), 0.0, NEG_FILL)
        start, size = window(i, rows)
        near = code[start : start + size, :] == code_row[:, r]
        near_bias[i] = jnp.where(near, 0.0, NEG_FILL)


def beside(block):
    return jnp.concatenate([block, block], axis=1)


def stack_heads(block):
    lane = lax.broadcasted_iota(jnp.int32, block.shape, 1)
    zero = jnp.zeros_like(block)
    return jnp.concatenate(
        [jnp.where(lane < HEAD_DIM, block, zero), jnp.where(lane < HEAD_DIM, zero, block)], axis=0
    )


def unstack_heads(block):
    half = block.shape[0] // 2
    lane = lax.broadcasted_iota(jnp.int32, (half, block.shape[1]), 1)
    return jnp.where(lane < HEAD_DIM, block[:half], block[half:])


def twice(block):
    return jnp.concatenate([block, block], axis=0)


def attend_body(noisy_ref, lo, hi, code, code_row, q, k, v, kf, vf, o, lse, far_bias, near_bias):
    rows = q.shape[0]

    @pl.when(pl.program_id(0) == 0)
    def _():
        build_masks(lo, hi, code, code_row, far_bias, near_bias)

    def run(noisy):
        for i in range(rows // TILE):
            r = slice(i * TILE, (i + 1) * TILE)
            q2 = stack_heads(q[r, :])
            w = far_width(i, rows, noisy)
            s = dot_nt(q2, kf[:w, :]) * (SCORE_SCALE * LOG2_E) + twice(far_bias[r, :w])
            top = jnp.max(s, axis=-1, keepdims=True)
            if noisy:
                start, size = window(i, rows)
                n = slice(start, start + size)
                sn = dot_nt(q2, k[n, :]) * (SCORE_SCALE * LOG2_E) + twice(near_bias[i])
                top = jnp.maximum(top, jnp.max(sn, axis=-1, keepdims=True))
            e = jnp.exp2(s - top)
            total = jnp.sum(e, axis=-1, keepdims=True)
            mixed = dot(e.astype(BF16), vf[:w, :])
            if noisy:
                en = jnp.exp2(sn - top)
                total = total + jnp.sum(en, axis=-1, keepdims=True)
                mixed = mixed + dot(en.astype(BF16), v[n, :])
            o[r, :] = unstack_heads(mixed * (1.0 / total)).astype(BF16)
            log_sum = jnp.broadcast_to(top + jnp.log2(total), (2 * TILE, PAIR))
            lse[:, 2 * TILE * i : 2 * TILE * (i + 1)] = log_sum.T[:8]

    @pl.when(noisy_ref[0] == 1)
    def _():
        run(True)

    @pl.when(noisy_ref[0] == 0)
    def _():
        run(False)


def mask_scratch(rows):
    return [
        pltpu.VMEM((rows, rows), F32),
        pltpu.VMEM((rows // TILE, TILE, TILE + 2 * REACH), F32),
    ]


def attend(noisy, lo, hi, code, code_row, q, k, v, kf, vf):
    rows, width = q.shape
    pair = pl.BlockSpec((rows, PAIR), lambda j: (0, j))
    return pl.pallas_call(
        attend_body,
        grid=(width // PAIR,),
        out_shape=[like((rows, width), BF16), like((8 * (width // PAIR), 2 * rows), F32)],
        in_specs=[SMEM_SPEC] + [whole_spec((rows, 1))] * 3 + [whole_spec((1, rows))] + [pair] * 5,
        out_specs=[pair, pl.BlockSpec((8, 2 * rows), lambda j: (j, 0))],
        scratch_shapes=mask_scratch(rows),
        compiler_params=pltpu.CompilerParams(vmem_limit_bytes=12 * 2**20),
        cost_estimate=SHORT,
    )(noisy, *in_hbm(lo, hi, code, code_row, q, k, v, kf, vf))


def attend_back_body(
    early, noisy_ref, place_ref, code, lo_row, hi_row, code_row, q, k, v, kf, vf, o, lse, ga, out_w, wq, wk, wv,
    first_t, far_first_t, cos, sin, own, far, *refs,
):
    outs, (far_bias, near_bias, acc_k, acc_v, acc_kf, acc_vf, dw_own, dw_rest) = refs[:-8], refs[-8:]
    rows = q.shape[0]

    @pl.when(pl.program_id(0) == 0)
    def _():
        build_turned_masks(code, lo_row, hi_row, code_row, far_bias, near_bias)
        own[...] = jnp.zeros_like(own)
        far[...] = jnp.zeros_like(far)

    go = dot_nt(ga[...], out_w[...]).astype(BF16)

    def turn_back(x):
        return (x * cos[...] - half_swap(x) * sin[...]).astype(BF16)

    def run(noisy):
        acc_kf[...] = jnp.zeros_like(acc_kf)
        acc_vf[...] = jnp.zeros_like(acc_vf)
        if noisy:
            acc_k[...] = jnp.zeros_like(acc_k)
            acc_v[...] = jnp.zeros_like(acc_v)
        parts = []
        for i in range(rows // TILE):
            r = slice(i * TILE, (i + 1) * TILE)
            q2 = stack_heads(q[r, :])
            go2 = stack_heads(go[r, :])
            delta = jnp.sum(
                (go2.astype(F32) * twice(o[r, :]).astype(F32)).T, axis=0, keepdims=True
            )
            log_sum = lse[0:1, 2 * TILE * i : 2 * TILE * (i + 1)]

            w = far_width(i, rows, noisy)
            keys, values, bias = kf[:w, :], vf[:w, :], far_bias[:w, r]
            if noisy:
                start, size = window(i, rows)
                n = slice(start, start + size)
                keys = jnp.concatenate([keys, k[n, :]], axis=0)
                values = jnp.concatenate([values, v[n, :]], axis=0)
                bias = jnp.concatenate([bias, near_bias[i]], axis=0)
            s = dot_nt(keys, q2) * (SCORE_SCALE * LOG2_E) + beside(bias)
            p = jnp.exp2(s - log_sum)
            gp = dot_nt(values, go2)
            ds = (p * (gp - delta)).astype(BF16)
            g_keys, g_values = dot(ds, q2), dot(p.astype(BF16), go2)
            acc_kf[:w, :] += g_keys[:w]
            acc_vf[:w, :] += g_values[:w]
            if noisy:
                acc_k[n, :] += g_keys[w:]
                acc_v[n, :] += g_values[w:]
            gq = dot_tn(keys, ds)
            parts.append(unstack_heads(gq.T))
        dq = turn_back(jnp.concatenate(parts, axis=0) * SCORE_SCALE)
        dkf = turn_back(acc_kf[...] * SCORE_SCALE)
        dvf = acc_vf[...].astype(BF16)
        g_far = jnp.concatenate([dkf, dvf], axis=1)
        w_far = jnp.concatenate([wk[...], wv[...]], axis=1)
        far[...] += dot_nt(g_far, w_far)
        dw_far = dot(far_first_t[...], g_far)
        if noisy:
            dk = turn_back(acc_k[...] * SCORE_SCALE)
            dv = acc_v[...].astype(BF16)
            g_own = jnp.concatenate([dq, dk, dv], axis=1)
            own[...] += dot_nt(g_own, jnp.concatenate([wq[...], w_far], axis=1))
            dw = dot(first_t[...], g_own)
            dw_far = dw[:, PAIR:] + dw_far
        else:
            own[...] += dot_nt(dq, wq[...])
            dw = dot(first_t[...], dq)
        dw_own[...] = dw[:, :PAIR].astype(BF16)
        dw_rest[...] = dw_far.astype(BF16)

    @pl.when(noisy_ref[0] == 1)
    def _():
        run(True)

    @pl.when(noisy_ref[0] == 0)
    def _():
        run(False)

    def store(some):
        store_rows(dw_own[...], place_ref, some, slice(0, PAIR))
        store_rows(dw_rest[...], place_ref, some, slice(PAIR, 3 * PAIR))

    half = len(outs) // 2

    @pl.when(pl.program_id(0) < early)
    def _():
        store(outs[:half])

    @pl.when(pl.program_id(0) >= early)
    def _():
        store(outs[half:])


def attend_back(noisy, place_in, masks, heads, ga, joint, first_t, far_first_t, cos, sin, early):
    rows, width = ga.shape
    pairs = width // PAIR
    pair = pl.BlockSpec((rows, PAIR), lambda j: (0, j))

    def strip(part):
        return pl.BlockSpec((width, PAIR), lambda j: (0, part * pairs + j))

    shapes, out_specs = [], []
    for first, last in ((0, early), (early, pairs)):
        for shape in row_grad_shapes(width, 3 * PAIR * (last - first)):
            shapes.append(shape)
            out_specs.append(
                pl.BlockSpec(
                    shape[:-1] + (3 * PAIR,),
                    lambda j, first=first, last=last, n=len(shape): (0,) * (n - 1)
                    + (jnp.clip(j, first, last - 1) - first,),
                )
            )
    act = whole_spec((rows, width))
    turned = whole_spec((width, rows))
    outs = pl.pallas_call(
        partial(attend_back_body, early),
        grid=(pairs,),
        out_shape=[like((rows, width), F32)] * 2 + [like(shape, BF16) for shape in shapes],
        in_specs=[SMEM_SPEC] * 2
        + [whole_spec((rows, 1))]
        + [whole_spec((1, rows))] * 3
        + [pair] * 6
        + [pl.BlockSpec((8, 2 * rows), lambda j: (j, 0))]
        + [act, pl.BlockSpec((PAIR, width), lambda j: (j, 3))]
        + [strip(0), strip(1), strip(2), turned, turned]
        + [whole_spec((rows, PAIR))] * 2,
        out_specs=[act] * 2 + out_specs,
        scratch_shapes=[
            pltpu.VMEM((rows, rows), F32),
            pltpu.VMEM((rows // TILE, TILE + 2 * REACH, TILE), F32),
        ]
        + [pltpu.VMEM((rows, PAIR), F32)] * 4
        + [pltpu.VMEM((width, PAIR), BF16), pltpu.VMEM((width, 2 * PAIR), BF16)],
        compiler_params=pltpu.CompilerParams(vmem_limit_bytes=32 * 2**20),
        cost_estimate=SHORT,
    )(
        noisy,
        place_in,
        *in_hbm(*masks, *heads, ga, joint, joint, joint, joint, first_t, far_first_t, cos, sin),
    )
    half = len(shapes) // 2
    return outs[0], outs[1], outs[2 : 2 + half], outs[2 + half :]


def store_rows(value, place_ref, outs, columns):
    if len(outs) == 1:
        outs[0][:, columns] = value.astype(BF16)
        return
    keep, send = outs
    _, far_count, pair_rows, _ = keep.shape
    core, near, far = place_ref[0], place_ref[1], place_ref[2]
    for z in range(far_count):
        for y in range(2):
            start = (z * 2 + y) * 2 * pair_rows
            first = value[start : start + pair_rows].astype(BF16)
            second = value[start + pair_rows : start + 2 * pair_rows].astype(BF16)
            keep[y ^ near, z ^ far, :, columns] = jnp.where(core == 0, first, second)
            send[y ^ near, z ^ far, :, columns] = jnp.where(core == 0, second, first)


def mlp_body(n_up, *refs):
    (
        place_ref, tok, o, cot, out_w, extra, up_w, down_w, within, which,
        layer_out, gy, ga, *dups, lines, up_lines,
        y1, second, out_acc, gsec_acc, up_line, grad_line,
    ) = refs
    dups, ddowns = dups[:n_up], dups[n_up:]
    step = pl.program_id(0)

    @pl.when(step == 0)
    def _():
        rows = tok[...].astype(F32) + dot(o[...], out_w[...])
        y1[...] = rows
        norm, _ = normed(rows)
        second[...] = (norm * small_row(extra, 1)).astype(BF16)
        out_acc[...] = jnp.zeros_like(out_acc)
        gsec_acc[...] = jnp.zeros_like(gsec_acc)
        lines[...] = jnp.zeros_like(lines)
        lines[2:3, :] = jnp.sum(cot[...].astype(F32), axis=0, keepdims=True)
        chunk = up_w.shape[1]
        quarter = chunk // 4
        row = lax.broadcasted_iota(jnp.int32, (8, SMALL), 0)
        lane = lax.broadcasted_iota(jnp.int32, (8, SMALL), 1)
        pick = (lane == row + 3).astype(BF16)
        line = lax.broadcasted_iota(jnp.int32, (8, chunk), 0)
        for j in range(up_line.shape[0]):
            four = dot_nt(pick, extra[j * quarter : (j + 1) * quarter, :]).astype(BF16)
            values = jnp.where(line == which[...], dot_nt(four, within[...]), 0.0)
            up_line[j : j + 1, :] = jnp.sum(values, axis=0, keepdims=True)

    up_b = up_line[pl.ds(step, 1), :]
    x = dot(second[...], up_w[...]) + up_b
    square = x * x
    t = jnp.tanh(x * (GELU_A + (GELU_A * GELU_B) * square))
    half_t = 0.5 + 0.5 * t
    act = (x * half_t).astype(BF16)
    slope = half_t + (0.5 * x) * (1.0 - t * t) * (GELU_A + (3.0 * GELU_A * GELU_B) * square)
    g_pre = (dot_nt(cot[...], down_w[...]) * slope).astype(BF16)
    dup_b = jnp.sum(g_pre.astype(F32), axis=0, keepdims=True)
    grad_line[pl.ds(step, 1), :] = dup_b
    out_acc[...] += dot(act, down_w[...])
    gsec_acc[...] += dot_nt(g_pre, up_w[...])
    down_grad = dot_tn(act, cot[...])
    if len(ddowns) == 1:
        ddowns[0][...] = down_grad.astype(BF16)
    else:
        pair_rows = down_grad.shape[0] // 4
        core, near = place_ref[0], place_ref[1]
        for y in range(2):
            start = 2 * y * pair_rows
            first = down_grad[start : start + pair_rows].astype(BF16)
            other = down_grad[start + pair_rows : start + 2 * pair_rows].astype(BF16)
            ddowns[0][y ^ near, 0] = jnp.where(core == 0, first, other)
            ddowns[1][y ^ near, 0] = jnp.where(core == 0, other, first)
    store_rows(dot_tn(second[...], g_pre), place_ref, dups, slice(None))

    @pl.when(step == pl.num_programs(0) - 1)
    def _():
        up_lines[...] = jnp.zeros_like(up_lines)
        for j in range(4):
            up_lines[j] = dot(jnp.where(which[...] == j, grad_line[...], 0.0).astype(BF16), within[...])
        rows = y1[...]
        layer_out[...] = (rows + out_acc[...] + small_row(extra, 2)).astype(BF16)
        norm, inverse = normed(rows)
        gs = gsec_acc[...]
        lines[1:2, :] = jnp.sum(gs * norm, axis=0, keepdims=True)
        g = cot[...].astype(F32) + norm_term(gs, norm, inverse, small_row(extra, 1))
        gy[...] = g
        ga[...] = g.astype(BF16)


def row_grad_shapes(width, columns):
    pair_rows = 2 * (width // device_count())
    if pair_rows % 16:
        return [(width, columns)]
    return [(2, device_count() // 8, pair_rows, columns)] * 2


def mlp(place_in, tok, o, cot, joint, up_w, down_w):
    rows, width = tok.shape
    hidden = up_w.shape[1]
    ups = row_grad_shapes(width, hidden)
    pair_rows = 2 * (hidden // device_count())
    if len(ups) == 1:
        chunk = hidden // 4
        up_specs = [pl.BlockSpec((width, chunk), lambda j, _: (0, j))]
        downs = [(hidden, width)]
        down_specs = [pl.BlockSpec((chunk, width), lambda j, _: (j, 0))]
    else:
        chunk = 4 * pair_rows
        far_count = device_count() // 8
        up_specs = [pl.BlockSpec(ups[0][:3] + (chunk,), lambda j, _: (0, 0, 0, j))] * 2
        downs = [(2, far_count, pair_rows, width)] * 2
        down_specs = [
            pl.BlockSpec((2, 1, pair_rows, width), lambda j, p: (0, j ^ p[2], 0, 0))
        ] * 2
    act = whole_spec((rows, width))
    extra, _, out_w = joint_specs(width)
    up_in = pl.BlockSpec((width, chunk), lambda j, _: (0, j))
    shard = hidden // device_count()
    unit = np.arange(chunk)
    within = (unit // shard) * (shard // 4) + unit % (shard // 4)
    which = (unit % shard) // (shard // 4)
    within = jnp.asarray(within[:, None] == np.arange(chunk // 4)[None, :], BF16)
    which = jnp.asarray(which[None], jnp.int32)
    down_in = pl.BlockSpec((chunk, width), lambda j, _: (j, 0))
    outs = pl.pallas_call(
        partial(mlp_body, len(ups)),
        grid_spec=pltpu.PrefetchScalarGridSpec(
            num_scalar_prefetch=1,
            grid=(hidden // chunk,),
            in_specs=[act, act, act, out_w, extra, up_in, down_in]
            + [whole_spec((chunk, chunk // 4)), whole_spec((1, chunk))],
            out_specs=[act, act, act]
            + up_specs
            + down_specs
            + [whole_spec((8, width)), whole_spec((8, hidden // chunk, chunk // 4))],
            scratch_shapes=[
                pltpu.VMEM((rows, width), F32),
                pltpu.VMEM((rows, width), BF16),
                pltpu.VMEM((rows, width), F32),
                pltpu.VMEM((rows, width), F32),
                pltpu.VMEM((hidden // chunk, chunk), F32),
                pltpu.VMEM((hidden // chunk, chunk), F32),
            ],
        ),
        out_shape=[like((rows, width), BF16), like((rows, width), F32), like((rows, width), BF16)]
        + [like(shape, BF16) for shape in ups + downs]
        + [like((8, width), F32), like((8, hidden // chunk, chunk // 4), F32)],
        compiler_params=pltpu.CompilerParams(vmem_limit_bytes=32 * 2**20),
        cost_estimate=SHORT,
    )(place_in, *in_hbm(tok), o, *in_hbm(cot), joint, joint, up_w, down_w, *in_hbm(within, which))
    n = len(ups)
    return (*outs[:3], outs[3 : 3 + n], outs[3 + n : 3 + 2 * n], outs[-2], outs[-1])


def finish_body(
    noisy_ref, place_ref, tok, far_tok, far_tok_end, extra, own, far, gy, o, ga, lines, up_lines,
    part, send, *outs
):
    width = tok.shape[1]
    g = small_row(extra, 0)
    norm, inverse = normed(tok[...].astype(F32))
    own, far = own[...], far[...]

    def put_lines(gains):
        row = lax.broadcasted_iota(jnp.int32, (8, width), 0)
        values = jnp.where(row == 0, gains, lines[...]).astype(BF16)
        row = lax.broadcasted_iota(jnp.int32, (8, SMALL), 0)
        lane = lax.broadcasted_iota(jnp.int32, (8, SMALL), 1)
        small = dot_tn(values, (row == lane).astype(BF16))
        later = (row + 3 == lane).astype(BF16)
        biases = [dot_tn(up_lines[:, j, :].astype(BF16), later) for j in range(up_lines.shape[1])]
        small = small + jnp.concatenate(biases, axis=0)
        store_rows(small, place_ref, outs, slice(width, width + SMALL))

    half = width // 2
    for start in (0, half):
        c = slice(start, start + half)
        store_rows(dot_tn(o[...], ga[:, c]), place_ref, outs, c)

    @pl.when(noisy_ref[0] == 1)
    def _():
        part[...] = gy[...] + norm_term(own, norm, inverse, g)
        far_norm, far_inverse = normed(both(far_tok, far_tok_end))
        send[...] = norm_term(far, far_norm, far_inverse, g).astype(BF16)
        put_lines(jnp.sum(own * norm + far * far_norm, axis=0, keepdims=True))

    @pl.when(noisy_ref[0] == 0)
    def _():
        both = own + far
        part[...] = gy[...] + norm_term(both, norm, inverse, g)
        send[...] = jnp.zeros_like(send)
        put_lines(jnp.sum(both * norm, axis=0, keepdims=True))


def finish(noisy, place_in, tok, far_tok, far_tok_end, joint, own, far, gy, o, ga, lines, up_lines):
    rows, width = tok.shape
    act = whole_spec((rows, width))
    extra, _, _ = joint_specs(width)
    shapes = row_grad_shapes(width, width + SMALL)
    outs = pl.pallas_call(
        finish_body,
        grid=(1,),
        out_shape=[like((rows, width), F32)]
        + [like((rows, width), BF16)]
        + [like(shape, BF16) for shape in shapes],
        in_specs=[SMEM_SPEC] * 2
        + [act]
        + [whole_spec((rows // 2, width))] * 2
        + [extra]
        + [act] * 5
        + [whole_spec((8, width)), whole_spec(up_lines.shape)],
        out_specs=[act, act] + [whole_spec(shape) for shape in shapes],
        compiler_params=pltpu.CompilerParams(vmem_limit_bytes=32 * 2**20),
        cost_estimate=SHORT,
    )(noisy, place_in, tok, far_tok, far_tok_end, joint, own, far, gy, o, ga, lines, up_lines)
    return outs[0], outs[1], outs[2:]


def last_sum_body(pairs, keep, *refs):
    got, (qkv, out, small) = refs[:-3], refs[-3:]
    total = keep[0]
    for g in got:
        total = total + g[0].astype(F32)
    width = out.shape[1]
    for i in range(pairs):
        at = 3 * PAIR * i
        for p in range(3):
            qkv[:, p * width + i * PAIR : p * width + (i + 1) * PAIR] = total[
                :, at + p * PAIR : at + (p + 1) * PAIR
            ]
    out[...] = total[:, 3 * width : 4 * width]
    small[...] = total[:, 4 * width :]


def last_sum(keep, got, width):
    rows = keep.shape[1]
    shapes = ((rows, 3 * width), (rows, width), (rows, SMALL))
    return pl.pallas_call(
        partial(last_sum_body, width // PAIR),
        out_shape=[like(shape, F32) for shape in shapes],
        in_specs=[VMEM_SPEC] * (1 + len(got)),
        out_specs=[VMEM_SPEC] * 3,
        compiler_params=pltpu.CompilerParams(vmem_limit_bytes=8 * 2**20),
        cost_estimate=SHORT,
    )(keep, *got)


def mlp_sum_body(keep, *refs):
    got, (up, down) = refs[:-2], refs[-2:]
    total = keep[0]
    for g in got:
        total = total + g[0].astype(F32)
    rows, hidden = up.shape
    width = down.shape[1]
    up[...] = total[:, :hidden]
    for f in range(down.shape[0] // rows):
        at = hidden + f * width
        down[f * rows : (f + 1) * rows, :] = total[:, at : at + width]


def mlp_sum(keep, got, hidden, width):
    _, rows, columns = keep.shape
    return pl.pallas_call(
        mlp_sum_body,
        out_shape=[like((rows, hidden), F32), like(((columns - hidden) // width * rows, width), F32)],
        in_specs=[VMEM_SPEC] * (1 + len(got)),
        out_specs=[VMEM_SPEC] * 2,
        compiler_params=pltpu.CompilerParams(vmem_limit_bytes=8 * 2**20),
        cost_estimate=LONG,
    )(keep, *got)


def add_body(part, got, out):
    out[...] = part[...] + got[...].astype(F32)


def add(part, got):
    rows, width = part.shape
    block = pl.BlockSpec((rows // 4, width), lambda j: (j, 0))
    return pl.pallas_call(
        add_body,
        grid=(4,),
        out_shape=like((rows, width), F32),
        in_specs=[block] * 2,
        out_specs=block,
        compiler_params=pltpu.CompilerParams(vmem_limit_bytes=8 * 2**20),
        cost_estimate=LONG,
    )(part, got)


def local(
    tokens,
    lengths,
    cotangent,
    attn_gain,
    qkv_weight,
    out_weight,
    mlp_gain,
    up_weight,
    up_bias,
    down_weight,
    down_bias,
):
    rows, width = tokens.shape[1:]
    stream = lax.axis_index("stream").astype(jnp.int32)
    me = (lax.axis_index("seq").astype(jnp.int32) * 2 + stream)[None]
    noisy = stream[None]
    n_dev = device_count()
    tok = tokens[0]
    cot = cotangent[0]

    shard_rows, hidden = up_weight.shape
    joint, pair_weights = prepare(
        qkv_weight, out_weight, up_weight, down_weight, attn_gain, mlp_gain, down_bias, up_bias
    )
    cut = 2 * width
    half = rows // 2
    far_tok = [lax.ppermute(tok[:half], "stream", [(0, 1)])]
    far_tok.append(lax.ppermute(after(tok[half:], far_tok[0]), "stream", [(0, 1)]))
    (a1, b1), jkey = far_gather(joint, (cut, joint.shape[1] - cut), SHORT, far_tok[0])
    (u1, d1), ukey = far_gather(after(pair_weights, a1), (hidden, hidden), LONG, far_tok[1])
    a2, akey = near_gather(a1, jkey, STREAM_BIT)
    b2, bkey = near_gather(b1, jkey, NEAR_BIT)
    a3, akey = last_gather(a2, akey, NEAR_BIT, u1, d1)
    b3, bkey = last_gather(b2, bkey, STREAM_BIT, u1, d1)
    u1, d1 = after(u1, a3[1], b3[1]), after(d1, a3[1], b3[1])
    u_got, d_got = flip(u1, NEAR_BIT), flip(d1, STREAM_BIT)
    joint = place([a3, b3], [akey, bkey], me).reshape(width, -1)

    doc_ids, positions = doc_layout(lengths[0], rows)
    cosine, sine = rotary_tables(positions, HEAD_DIM)
    cos = jnp.concatenate([cosine] * 4, axis=1)
    sin = jnp.concatenate([-sine, sine] * 2, axis=1)
    lo = doc_ids * rows
    code = lo + positions // BLOCK
    masks = (lo[:, None], (code - stream)[:, None], code[:, None], code[None, :])

    place_in = jnp.stack([(me[0] // bit) % 2 for bit in (CORE_BIT, NEAR_BIT)] + [me[0] // (2 * NEAR_BIT)])
    first_t, far_first_t, q, k, v, kf, vf = front(noisy, tok, *far_tok, joint, cos, sin)
    u_got, d_got = after(u_got, q), after(d_got, q)
    u2, d2 = jnp.concatenate([u1, u_got], axis=0), jnp.concatenate([d1, d_got], axis=0)
    u_got, d_got = flip(u2, STREAM_BIT), flip(d2, NEAR_BIT)
    u_core, d_core = flip(u2, CORE_BIT), flip(d2, CORE_BIT)
    o, lse = attend(noisy, *masks, after(q, u2, d2), k, v, kf, vf)
    u_got, d_got = after(u_got, o), after(d_got, o)
    u3 = [u2, u_got, u_core, flip(u_got, CORE_BIT)]
    d3 = [d2, d_got, d_core, flip(d_got, CORE_BIT)]

    def keys(*bits):
        out = [ukey]
        for bit in bits:
            out = out + [[key ^ bit for key in line] for line in out]
        return [out[0] + out[1], out[2] + out[3], out[4] + out[5], out[6] + out[7]]

    ukey, dkey = keys(NEAR_BIT, STREAM_BIT, CORE_BIT), keys(STREAM_BIT, NEAR_BIT, CORE_BIT)
    up_full, down_full = place_pair(u3, ukey, d3, dkey, me)
    layer_out, gy, ga, dup, ddown, lines, up_lines = mlp(
        place_in, tok, o, cot, joint, up_full.reshape(width, -1), down_full.reshape(-1, width)
    )

    up_sum, down_sum = Sum(me, dup), Sum(me, ddown)
    split((up_sum, NEAR_BIT), (down_sum, STREAM_BIT))
    up_sum.flip(NEAR_BIT)
    down_sum.flip(STREAM_BIT)
    ga_next = after(ga, up_sum.send, down_sum.send)
    heads = (q, k, v, kf, vf, o, lse)
    turned_masks = (code[:, None], lo[None], (code - stream)[None], code[None])
    pairs = width // PAIR
    early = 2 * pairs // 3
    own, far, front_outs, back_outs = attend_back(
        noisy, place_in, turned_masks, heads, ga_next, joint, first_t, far_first_t, cos, sin, early
    )
    up_sum.hold(*front_outs)
    down_sum.hold(*front_outs)
    split((up_sum, STREAM_BIT), (down_sum, NEAR_BIT))
    up_sum.flip(STREAM_BIT)
    down_sum.flip(NEAR_BIT)
    front_sum = Sum(me, [after(a, up_sum.send, down_sum.send) for a in front_outs])
    back_sum = Sum(me, [after(a, up_sum.send, down_sum.send) for a in back_outs])
    up_sum.hold(front_sum.got, back_sum.got)
    down_sum.hold(front_sum.got, back_sum.got)
    gy = after(gy, up_sum.send, down_sum.send)
    part, send, outs = finish(
        noisy, place_in, tok, *far_tok, joint, own, far, gy, o, ga, lines, up_lines
    )
    back_sum.add(outs)
    mlp_far = Far([up_sum, down_sum], LONG)
    back_sum.hold(*mlp_far.sends)
    split((front_sum, STREAM_BIT), (back_sum, NEAR_BIT))
    front_sum.flip(STREAM_BIT)
    back_sum.flip(NEAR_BIT)
    mlp_far.flip()
    split((front_sum, NEAR_BIT), (back_sum, STREAM_BIT))
    front_sum.flip(NEAR_BIT)
    back_sum.flip(STREAM_BIT)
    owned_up, owned_down = mlp_sum(mlp_far.keep, mlp_far.got, hidden, width)
    back_sum.hold(owned_up, owned_down)
    received = lax.ppermute(after(send, front_sum.send, back_sum.send), "stream", [(1, 0)])
    attn_far = Far([front_sum, back_sum])
    attn_far.flip()
    grad_input = add(part, received)
    attn_far.got[0] = after(attn_far.got[0], grad_input)
    owned_qkv, owned_out, owned_small = last_sum(attn_far.keep, attn_far.got, width)

    def small_owned(i):
        return owned_small[:, i]

    return (
        layer_out[None],
        grad_input[None],
        small_owned(0),
        owned_qkv,
        owned_out,
        small_owned(1),
        owned_up,
        owned_small[:, 3:7].T.reshape(-1),
        owned_down,
        small_owned(2),
    )


def solution(mesh):
    placed = (
        P("stream", "seq", None),
        P("seq", None),
        P("stream", "seq", None),
        P(("seq", "stream")),
        P(("seq", "stream"), None),
        P(("seq", "stream"), None),
        P(("seq", "stream")),
        P(("seq", "stream"), None),
        P(("seq", "stream")),
        P(("seq", "stream"), None),
        P(("seq", "stream")),
    )
    return jax.shard_map(
        local,
        mesh=mesh,
        in_specs=placed,
        out_specs=(
            P("stream", "seq", None),
            P("stream", "seq", None),
            P(("seq", "stream")),
            P(("seq", "stream"), None),
            P(("seq", "stream"), None),
            P(("seq", "stream")),
            P(("seq", "stream"), None),
            P(("seq", "stream")),
            P(("seq", "stream"), None),
            P(("seq", "stream")),
        ),
        check_vma=False,
    )
```

```python
from functools import partial
import math

import jax
import jax.numpy as jnp
import numpy as np
from jax import lax
from jax.experimental import pallas as pl
from jax.experimental.pallas import tpu as pltpu
from jax.sharding import PartitionSpec as P

HEADS = 12
HEAD_DIM = 64
BLOCK = 16


EPSILON = 1e-05
NEG_FILL = -1e30


ALL = ("seq", "stream")
STREAM_BIT, CORE_BIT, NEAR_BIT = 1, 2, 4


def device_count():
    return lax.axis_size("seq") * lax.axis_size("stream")


def far_groups():
    bits = []
    bit = 2 * NEAR_BIT
    while bit < device_count():
        bits.append(bit)
        bit *= 2
    groups = []
    while bits:
        taken, bits = bits[:2], bits[2:]
        groups.append(taken if len(taken) == 1 else [taken[0], taken[1], taken[0] + taken[1]])
    return groups


def flip(block, mask):
    return lax.ppermute(block, ALL, [(i, i ^ mask) for i in range(device_count())])


def place(pieces, keys, me):
    total = sum(len(key) for key in keys[0])
    rows = pieces[0][0].shape[1]
    widths = [strip[0].shape[2] for strip in pieces]
    shape = (total, rows, sum(widths))
    flat = [p for strip in pieces for p in strip]

    def body(me_ref, *refs):
        out, sem = refs[-2], refs[-1]
        taken, column = 0, 0
        for key_set, width in zip(keys, widths):
            for key in key_set:
                piece = refs[taken]
                taken += 1
                for j, rel in enumerate(key):
                    to = out.at[me_ref[0] ^ rel]
                    if len(widths) > 1:
                        to = to.at[:, pl.ds(column, width)]
                    pltpu.make_async_copy(piece.at[j], to, sem).start()
            column += width
        pltpu.make_async_copy(out, out, sem).wait()

    return pl.pallas_call(
        body,
        out_shape=like(shape, flat[0].dtype),
        in_specs=[SMEM_SPEC] + [pl.BlockSpec(memory_space=pl.ANY)] * len(flat),
        out_specs=VMEM_SPEC,
        scratch_shapes=[pltpu.SemaphoreType.DMA],
        compiler_params=pltpu.CompilerParams(
            vmem_limit_bytes=2 * math.prod(shape) * (16 // min(16, rows)) * 2 + 2**20
        ),
        cost_estimate=SHORT,
    )(me, *flat)


def place_pair(up, up_keys, down, down_keys, total, me, begun=()):
    rows, hidden = up[0].shape[1:]
    width = total * rows
    folds = down[0].shape[2] // width

    def body(me_ref, *refs):
        up_out, down_out, up_sem, down_sem = refs[-4:]
        pieces = refs[len(begun) : -4]
        copies = []
        for piece, key in zip(pieces, up_keys):
            for j, rel in enumerate(key):
                copies.append((piece.at[j], up_out.at[me_ref[0] ^ rel], up_sem))
        for piece, key in zip(pieces[len(up) :], down_keys):
            for j, rel in enumerate(key):
                for f in range(folds):
                    part = piece.at[j, :, pl.ds(f * width, width)]
                    copies.append((part, down_out.at[me_ref[0] ^ rel, f], down_sem))
        for source, target, sem in copies:
            pltpu.make_async_copy(source, target, sem).start()
        count = sum(len(key) for key in up_keys)
        for out, sem in ((up_out, up_sem), (down_out, down_sem)):
            some = out.at[pl.ds(0, count)]
            pltpu.make_async_copy(some, some, sem).wait()

    shapes = ((total, rows, hidden), (total, folds, rows, width))
    return pl.pallas_call(
        body,
        out_shape=[pltpu.VMEM(shape, BF16) for shape in shapes],
        in_specs=[SMEM_SPEC]
        + [VMEM_SPEC] * len(begun)
        + [pl.BlockSpec(memory_space=pl.ANY)] * len(up + down),
        out_specs=[VMEM_SPEC] * 2,
        scratch_shapes=[pltpu.SemaphoreType.DMA] * 2,
        input_output_aliases={1: 0, 2: 1} if begun else {},
        compiler_params=pltpu.CompilerParams(
            vmem_limit_bytes=4 * total * rows * hidden * (16 // min(16, rows)) + 2**20
        ),
        cost_estimate=SHORT,
    )(me, *(pltpu.with_memory_space_constraint(b, pltpu.VMEM) for b in begun), *up, *down)


def after(block, *others):
    return lax.optimization_barrier((block,) + others)[0]


def stack_body(count, widths, *refs):
    ins, outs = refs[:count], refs[count:]
    column = 0
    for out, width in zip(outs, widths):
        at = 0
        for piece in ins:
            out[at : at + piece.shape[0]] = piece[:, :, column : column + width]
            at += piece.shape[0]
        column += width


def stack(pieces, widths, cost):
    total, rows = sum(p.shape[0] for p in pieces), pieces[0].shape[1]
    return pl.pallas_call(
        partial(stack_body, len(pieces), widths),
        out_shape=[like((total, rows, width), BF16) for width in widths],
        in_specs=[VMEM_SPEC] * len(pieces),
        out_specs=[VMEM_SPEC] * len(widths),
        compiler_params=pltpu.CompilerParams(vmem_limit_bytes=6 * 2**20),
        cost_estimate=cost,
    )(*pieces)


def far_gather(shard, widths, cost, *others):
    piece, key = shard[None], [0]
    groups = far_groups()
    for group in groups:
        got = [piece] + [flip(piece, mask) for mask in group]
        key = [k ^ mask for mask in [0] + group for k in key]
        if group != groups[-1]:
            piece = jnp.concatenate(got, axis=0)
    if others:
        got[-1] = after(got[-1], *others)
    return stack(got, widths, cost), key


def near_gather(piece, key, bit):
    return jnp.concatenate([piece, flip(piece, bit)], axis=0), key + [k ^ bit for k in key]


def last_gather(piece, key, bit, *others):
    got = flip(piece, bit)
    if others:
        got = after(got, *others)
    pieces, keys = [piece, got], [key, [k ^ bit for k in key]]
    pieces = pieces + [flip(after(piece, *others), CORE_BIT), flip(got, CORE_BIT)]
    return pieces, keys + [[k ^ CORE_BIT for k in key] for key in keys]


def relative(whole, me):
    pairs = device_count() // 2
    rows = whole.reshape((pairs, 2, -1) + whole.shape[1:]) if whole.ndim < 3 else whole
    rows = rows.reshape((pairs, -1) + whole.shape[-1:])
    bits = pairs.bit_length() - 1
    rows = rows.reshape((2,) * bits + rows.shape[1:])
    for axis in range(bits):
        mine = (me[0] >> (bits - axis)) % 2
        rows = jnp.where(mine == 1, jnp.flip(rows, axis), rows)
    order = (bits - 1, bits - 2) + tuple(range(bits - 2)) + (bits, bits + 1)
    rows = rows.transpose(order).reshape((2, 2, pairs // 4) + rows.shape[-2:])
    return rows[0], rows[1]


def combine_body(bits, counts, stream_ref, *refs):
    total = sum(sum(groups) for groups in counts)
    ins, outs = refs[:total], refs[total:]
    stream = stream_ref[0]
    for bit, groups in zip(bits, counts):
        (send, keep), outs = outs[:2], outs[2:]
        column = 0
        for count in groups:
            terms, ins = ins[:count], ins[count:]
            columns = slice(column, column + terms[0].shape[-1])
            column = columns.stop

            def part(own):
                if bit == STREAM_BIT:
                    where = (slice(None), slice(None), pl.ds(stream if own else 1 - stream, 1))
                else:
                    where = (slice(0, 1) if own else slice(1, 2),)
                out = terms[0][where].astype(F32)
                for t in terms[1:]:
                    out = out + t[where].astype(F32)
                return out

            send[..., columns] = part(False).astype(send.dtype)
            keep[..., columns] = part(True)


def combine(stream, jobs):
    far_count = jobs[0][0][0][0].shape[1]
    operands, in_specs, out_shape, out_specs = [], [], [], []

    def spec(shape):
        return pl.BlockSpec((shape[0], 1) + shape[2:], lambda j: (0, j, 0, 0, 0))

    for groups, bit in jobs:
        out = list(groups[0][0].shape)
        out[4] = sum(terms[0].shape[4] for terms in groups)
        out[2 if bit == STREAM_BIT else 0] = 1
        out = tuple(out)
        for terms in groups:
            operands += terms
            in_specs += [spec(terms[0].shape)] * len(terms)
        out_shape += [like(out, BF16), like(out, F32)]
        out_specs += [spec(out)] * 2
    outs = pl.pallas_call(
        partial(
            combine_body,
            [bit for _, bit in jobs],
            [[len(terms) for terms in groups] for groups, _ in jobs],
        ),
        grid=(far_count,),
        out_shape=out_shape,
        in_specs=[SMEM_SPEC] + in_specs,
        out_specs=out_specs,
        compiler_params=pltpu.CompilerParams(vmem_limit_bytes=20 * 2**20),
        cost_estimate=SHORT,
    )(stream, *operands)
    return [(outs[2 * i], outs[2 * i + 1]) for i in range(len(jobs))]


class Sum:
    def __init__(self, me, *strips):
        self.me, self.stream = me, me % 2
        self.groups, self.got = [], []
        for parts in strips:
            self.add(parts)

    def add(self, parts):
        if len(parts) == 1:
            parts = relative(parts[0], self.me)
        keep, send = parts
        _, self.far_count, pair_rows, columns = keep.shape
        shape = (2, self.far_count, 2, pair_rows // 2, columns)
        self.got = flip(send, CORE_BIT)
        self.groups.append([keep.reshape(shape), self.got.reshape(shape)])

    def flip(self, bit):
        self.got = flip(self.send, bit)
        self.groups[0].append(self.got)
        return self

    def hold(self, *others):
        self.groups[0][-1] = after(self.groups[0][-1], *others)

    def total(self):
        out = self.groups[0][0].astype(F32)
        for t in self.groups[0][1:]:
            out = out + t.astype(F32)
        return out


def pack_body(far_count, counts, *refs):
    ins, (keep, *sends) = refs[: sum(counts)], refs[sum(counts) :]
    _, rows, _ = keep.shape
    part = far_count // (1 + len(sends))
    column = 0
    for count in counts:
        terms, ins = ins[:count], ins[count:]
        wide, columns = terms[0].shape[-2:]
        for z in range(far_count):
            total = terms[0][0, z, 0].astype(F32)
            for t in terms[1:]:
                total = total + t[0, z, 0].astype(F32)
            out = keep if z < part else sends[z // part - 1]
            for fold in range(wide // rows):
                at = slice(column + fold * columns, column + (fold + 1) * columns)
                value = total[fold * rows : (fold + 1) * rows]
                out[z % part, :, at] = value.astype(out.dtype)
        column += wide // rows * columns


class Far:
    def __init__(self, sums, cost=None):
        groups = [s.groups[0] for s in sums]
        far_count, _, rows, _ = groups[0][0].shape[1:]
        shards = [g[0].shape[3:] for g in groups]
        columns = sum(r // rows * c for r, c in shards)
        self.order = list(reversed(far_groups()))
        part = far_count // (1 + len(self.order[0]))
        shape = (part, rows, columns)
        outs = pl.pallas_call(
            partial(pack_body, far_count, [len(g) for g in groups]),
            out_shape=[like(shape, F32)] + [like(shape, BF16)] * len(self.order[0]),
            in_specs=[VMEM_SPEC] * sum(len(g) for g in groups),
            out_specs=[VMEM_SPEC] * (1 + len(self.order[0])),
            compiler_params=pltpu.CompilerParams(vmem_limit_bytes=10 * 2**20),
            cost_estimate=cost or SHORT,
        )(*[t for g in groups for t in g])
        self.keep, self.sends = outs[0], outs[1:]

    def flip(self):
        self.got = [flip(s, mask) for s, mask in zip(self.sends, self.order[0])]
        return self.advance()

    def advance(self):
        for group in self.order[1:]:
            total = self.keep
            for block in self.got:
                total = total + block.astype(F32)
            part = total.shape[0] // (len(group) + 1)
            got = [
                flip(total[(i + 1) * part : (i + 2) * part].astype(BF16), mask)
                for i, mask in enumerate(group)
            ]
            self.keep, self.got = total[:part], got
        return self


def split(*jobs):
    outs = combine(jobs[0][0].stream, [(s.groups, bit) for s, bit in jobs])
    for (s, _), (send, keep) in zip(jobs, outs):
        s.send, s.groups = send, [[keep]]


F32, BF16 = jnp.float32, jnp.bfloat16
SHORT = pl.CostEstimate(flops=1, bytes_accessed=1, transcendentals=0)
LONG = pl.CostEstimate(flops=10**10, bytes_accessed=3 * 10**7, transcendentals=0)
SMEM_SPEC = pl.BlockSpec(memory_space=pltpu.SMEM)
VMEM_SPEC = pl.BlockSpec(memory_space=pltpu.VMEM)


def like(shape, kind):
    return jax.ShapeDtypeStruct(shape, kind)


def in_hbm(*arrays):
    return [pltpu.with_memory_space_constraint(a, pltpu.HBM) for a in arrays]


def doc_layout(pack_lengths, row_count):
    ends = [pack_lengths[0]]
    for i in range(1, pack_lengths.shape[0]):
        ends.append(ends[-1] + pack_lengths[i])
    seq_ends = jnp.stack(ends)
    row_index = jnp.arange(row_count, dtype=jnp.int32)
    passed = seq_ends[None, :] <= row_index[:, None]
    doc_ids = jnp.sum(passed.astype(jnp.int32), axis=1)
    starts = jnp.max(jnp.where(passed, seq_ends[None, :], 0), axis=1)
    return (doc_ids, row_index - starts)


def rotary_tables(positions, head_size):
    half_size = head_size // 2
    frequency = jnp.exp(
        jnp.arange(half_size, dtype=jnp.float32) * (-2.0 * math.log(10000.0) / head_size)
    )
    angles = positions.astype(jnp.float32)[:, None] * frequency[None, :]
    return (jnp.cos(angles), jnp.sin(angles))


PAIR = 2 * HEAD_DIM
TILE = 128
SMALL = 128
REACH = 16
LOG2_E = math.log2(math.e)
SCORE_SCALE = HEAD_DIM ** (-0.5)
GELU_A = math.sqrt(2.0 / math.pi)
GELU_B = 0.044715


def dot(a, b):
    return lax.dot_general(a, b, (((1,), (0,)), ((), ())), preferred_element_type=F32)


def dot_nt(a, b):
    return lax.dot_general(a, b, (((1,), (1,)), ((), ())), preferred_element_type=F32)


def dot_tn(a, b):
    return lax.dot_general(a, b, (((0,), (0,)), ((), ())), preferred_element_type=F32)


def whole_spec(shape):
    return pl.BlockSpec(shape, lambda *_: (0,) * len(shape))


def normed(values):
    center = values - jnp.mean(values, axis=-1, keepdims=True)
    inverse = lax.rsqrt(jnp.mean(center * center, axis=-1, keepdims=True) + EPSILON)
    return center * inverse, inverse


def norm_term(grad_out, norm, inverse, gain):
    grad_norm = grad_out * gain
    return inverse * (
        grad_norm
        - jnp.mean(grad_norm, axis=-1, keepdims=True)
        - norm * jnp.mean(grad_norm * norm, axis=-1, keepdims=True)
    )


def half_swap(block):
    lane = lax.broadcasted_iota(jnp.int32, block.shape, 1)
    quarter = HEAD_DIM // 2
    return jnp.where(
        (lane & quarter) == 0,
        pltpu.roll(block, PAIR - quarter, 1),
        pltpu.roll(block, quarter, 1),
    )


def prepare_body(qkv, out, up, down, attn_gain, mlp_gain, down_bias, up_bias, joint, pair_weights):
    rows, hidden = up.shape
    width = out.shape[1]
    joint[:, : 3 * width] = qkv[...]
    joint[:, 3 * width : 4 * width] = out[...]
    lane = lax.broadcasted_iota(jnp.int32, (rows, SMALL), 1)
    small = jnp.zeros((rows, SMALL), F32)
    column = 0
    for line in (attn_gain, mlp_gain, down_bias, up_bias):
        values = line[...].astype(F32)
        for start in range(0, line.shape[1], rows):
            row = lax.broadcasted_iota(jnp.int32, (rows, line.shape[1]), 0)
            item = lax.broadcasted_iota(jnp.int32, (rows, line.shape[1]), 1)
            picked = jnp.sum(jnp.where(item == row + start, values, 0.0), axis=1, keepdims=True)
            small = jnp.where(lane == column, picked, small)
            column += 1
    joint[:, 4 * width :] = small.astype(BF16)
    pair_weights[:, :hidden] = up[...]
    tall = down[...].astype(F32)
    for fold in range(down.shape[0] // rows):
        at = hidden + fold * width
        pair_weights[:, at : at + width] = tall[fold * rows : (fold + 1) * rows].astype(BF16)


def prepare(qkv, out, up, down, *lines):
    rows, width = out.shape
    shapes = ((rows, 4 * width + SMALL), (rows, up.shape[1] + down.size // rows))
    return pl.pallas_call(
        prepare_body,
        out_shape=[like(shape, BF16) for shape in shapes],
        in_specs=[VMEM_SPEC] * 8,
        out_specs=[VMEM_SPEC] * 2,
        compiler_params=pltpu.CompilerParams(vmem_limit_bytes=8 * 2**20),
        cost_estimate=SHORT,
    )(*in_hbm(qkv, out, up, down, *(v[None] for v in lines)))


def small_row(extra, column):
    lane = lax.broadcasted_iota(jnp.int32, (8, extra.shape[1]), 1)
    return dot_nt((lane == column).astype(BF16), extra[...])[0:1, :]


def both(begin, end):
    return jnp.concatenate([begin[...], end[...]], axis=0).astype(F32)


def front_body(
    noisy_ref, tok, far_tok, far_tok_end, extra, weight, cos, sin,
    first_t, far_first_t, q, k, v, kf, vf, first, far_first,
):
    width = tok.shape[1]
    g = small_row(extra, 0)
    norm, _ = normed(tok[...].astype(F32))
    first[...] = (norm * g).astype(BF16)
    is_noisy = noisy_ref[0] == 1

    @pl.when(is_noisy)
    def _():
        far_norm, _ = normed(both(far_tok, far_tok_end))
        far_first[...] = (far_norm * g).astype(BF16)

    @pl.when(jnp.logical_not(is_noisy))
    def _():
        far_first[...] = first[...]

    first_t[...] = first[...].T
    far_first_t[...] = far_first[...].T
    step = 2 * PAIR
    for rows, outs in ((first, (q, k, v)), (far_first, (None, kf, vf))):
        for part, out in enumerate(outs):
            if out is None:
                continue
            for start in range(0, width, step):
                prod = dot(rows[...], weight[:, part * width + start : part * width + start + step])
                for sub in range(0, step, PAIR):
                    x = prod[:, sub : sub + PAIR]
                    if part < 2:
                        x = x * cos[...] + half_swap(x) * sin[...]
                    out[:, start + sub : start + sub + PAIR] = x.astype(BF16)


def joint_specs(width):
    return (
        pl.BlockSpec((width, SMALL), lambda *_: (0, 4 * width // SMALL)),
        pl.BlockSpec((width, 3 * width), lambda *_: (0, 0)),
        pl.BlockSpec((width, width), lambda *_: (0, 3)),
    )


def front(noisy, tok, far_tok, far_tok_end, joint, cos, sin):
    rows, width = tok.shape
    act, table = whole_spec((rows, width)), whole_spec((rows, PAIR))
    extra, qkv, _ = joint_specs(width)
    return pl.pallas_call(
        front_body,
        grid=(1,),
        out_shape=[pltpu.HBM((width, rows), BF16)] * 2 + [pltpu.HBM((rows, width), BF16)] * 5,
        in_specs=[SMEM_SPEC, act] + [whole_spec((rows // 2, width))] * 2 + [extra, qkv, table, table],
        out_specs=[whole_spec((width, rows))] * 2 + [act] * 5,
        scratch_shapes=[pltpu.VMEM((rows, width), BF16)] * 2,
        compiler_params=pltpu.CompilerParams(vmem_limit_bytes=15 * 2**20),
        cost_estimate=SHORT,
    )(noisy, tok, far_tok, far_tok_end, joint, joint, cos, sin)


def window(i, rows):
    size = TILE + 2 * REACH
    return min(max(i * TILE - REACH, 0), rows - size), size


def far_width(i, rows, noisy):
    return min(rows, (i + 1) * TILE + (0 if noisy else TILE))


def build_masks(lo, hi, code, code_row, far_bias, near_bias):
    rows = far_bias.shape[0]
    for i in range(rows // TILE):
        r = slice(i * TILE, (i + 1) * TILE)
        keys = code_row[...]
        far_bias[r, :] = jnp.where((keys >= lo[r, :]) & (keys <= hi[r, :]), 0.0, NEG_FILL)
        start, size = window(i, rows)
        near_bias[i] = jnp.where(code_row[:, start : start + size] == code[r, :], 0.0, NEG_FILL)


def build_turned_masks(code, lo_row, hi_row, code_row, far_bias, near_bias):
    rows = far_bias.shape[0]
    for i in range(rows // TILE):
        r = slice(i * TILE, (i + 1) * TILE)
        keys = code[r, :]
        far_bias[r, :] = jnp.where((keys >= lo_row[...]) & (keys <= hi_row[...]), 0.0, NEG_FILL)
        start, size = window(i, rows)
        near = code[start : start + size, :] == code_row[:, r]
        near_bias[i] = jnp.where(near, 0.0, NEG_FILL)


def beside(block):
    return jnp.concatenate([block, block], axis=1)


def stack_heads(block):
    lane = lax.broadcasted_iota(jnp.int32, block.shape, 1)
    zero = jnp.zeros_like(block)
    return jnp.concatenate(
        [jnp.where(lane < HEAD_DIM, block, zero), jnp.where(lane < HEAD_DIM, zero, block)], axis=0
    )


def unstack_heads(block):
    half = block.shape[0] // 2
    lane = lax.broadcasted_iota(jnp.int32, (half, block.shape[1]), 1)
    return jnp.where(lane < HEAD_DIM, block[:half], block[half:])


def twice(block):
    return jnp.concatenate([block, block], axis=0)


def attend_body(noisy_ref, lo, hi, code, code_row, q, k, v, kf, vf, o, lse, far_bias, near_bias):
    rows = q.shape[0]

    @pl.when(pl.program_id(0) == 0)
    def _():
        build_masks(lo, hi, code, code_row, far_bias, near_bias)

    def run(noisy):
        for i in range(rows // TILE):
            r = slice(i * TILE, (i + 1) * TILE)
            q2 = stack_heads(q[r, :])
            w = far_width(i, rows, noisy)
            s = dot_nt(q2, kf[:w, :]) * (SCORE_SCALE * LOG2_E) + twice(far_bias[r, :w])
            top = jnp.max(s, axis=-1, keepdims=True)
            if noisy:
                start, size = window(i, rows)
                n = slice(start, start + size)
                sn = dot_nt(q2, k[n, :]) * (SCORE_SCALE * LOG2_E) + twice(near_bias[i])
                top = jnp.maximum(top, jnp.max(sn, axis=-1, keepdims=True))
            e = jnp.exp2(s - top)
            total = jnp.sum(e, axis=-1, keepdims=True)
            mixed = dot(e.astype(BF16), vf[:w, :])
            if noisy:
                en = jnp.exp2(sn - top)
                total = total + jnp.sum(en, axis=-1, keepdims=True)
                mixed = mixed + dot(en.astype(BF16), v[n, :])
            o[r, :] = unstack_heads(mixed * (1.0 / total)).astype(BF16)
            log_sum = jnp.broadcast_to(top + jnp.log2(total), (2 * TILE, PAIR))
            lse[:, 2 * TILE * i : 2 * TILE * (i + 1)] = log_sum.T[:8]

    @pl.when(noisy_ref[0] == 1)
    def _():
        run(True)

    @pl.when(noisy_ref[0] == 0)
    def _():
        run(False)


def mask_scratch(rows):
    return [
        pltpu.VMEM((rows, rows), F32),
        pltpu.VMEM((rows // TILE, TILE, TILE + 2 * REACH), F32),
    ]


def attend(noisy, lo, hi, code, code_row, q, k, v, kf, vf):
    rows, width = q.shape
    pair = pl.BlockSpec((rows, PAIR), lambda j: (0, j))
    return pl.pallas_call(
        attend_body,
        grid=(width // PAIR,),
        out_shape=[like((rows, width), BF16), like((8 * (width // PAIR), 2 * rows), F32)],
        in_specs=[SMEM_SPEC] + [whole_spec((rows, 1))] * 3 + [whole_spec((1, rows))] + [pair] * 5,
        out_specs=[pair, pl.BlockSpec((8, 2 * rows), lambda j: (j, 0))],
        scratch_shapes=mask_scratch(rows),
        compiler_params=pltpu.CompilerParams(vmem_limit_bytes=8 * 2**20),
        cost_estimate=SHORT,
    )(noisy, *in_hbm(lo, hi, code, code_row, q, k, v, kf, vf))


def attend_back_body(
    early, noisy_ref, place_ref, code, lo_row, hi_row, code_row, q, k, v, kf, vf, o, lse, ga, out_w, wq, wk, wv,
    first_t, far_first_t, cos, sin, own, far, *refs,
):
    outs, (far_bias, near_bias, acc_k, acc_v, acc_kf, acc_vf, dw_own, dw_rest) = refs[:-8], refs[-8:]
    rows = q.shape[0]

    @pl.when(pl.program_id(0) == 0)
    def _():
        build_turned_masks(code, lo_row, hi_row, code_row, far_bias, near_bias)
        own[...] = jnp.zeros_like(own)
        far[...] = jnp.zeros_like(far)

    go = dot_nt(ga[...], out_w[...]).astype(BF16)

    def turn_back(x):
        return (x * cos[...] - half_swap(x) * sin[...]).astype(BF16)

    def run(noisy):
        acc_kf[...] = jnp.zeros_like(acc_kf)
        acc_vf[...] = jnp.zeros_like(acc_vf)
        if noisy:
            acc_k[...] = jnp.zeros_like(acc_k)
            acc_v[...] = jnp.zeros_like(acc_v)
        parts = []
        for i in range(rows // TILE):
            r = slice(i * TILE, (i + 1) * TILE)
            q2 = stack_heads(q[r, :])
            go2 = stack_heads(go[r, :])
            delta = jnp.sum(
                (go2.astype(F32) * twice(o[r, :]).astype(F32)).T, axis=0, keepdims=True
            )
            log_sum = lse[0:1, 2 * TILE * i : 2 * TILE * (i + 1)]

            w = far_width(i, rows, noisy)
            keys, values, bias = kf[:w, :], vf[:w, :], far_bias[:w, r]
            if noisy:
                start, size = window(i, rows)
                n = slice(start, start + size)
                keys = jnp.concatenate([keys, k[n, :]], axis=0)
                values = jnp.concatenate([values, v[n, :]], axis=0)
                bias = jnp.concatenate([bias, near_bias[i]], axis=0)
            s = dot_nt(keys, q2) * (SCORE_SCALE * LOG2_E) + beside(bias)
            p = jnp.exp2(s - log_sum)
            gp = dot_nt(values, go2)
            ds = (p * (gp - delta)).astype(BF16)
            g_keys, g_values = dot(ds, q2), dot(p.astype(BF16), go2)
            acc_kf[:w, :] += g_keys[:w]
            acc_vf[:w, :] += g_values[:w]
            if noisy:
                acc_k[n, :] += g_keys[w:]
                acc_v[n, :] += g_values[w:]
            gq = dot_tn(keys, ds)
            parts.append(unstack_heads(gq.T))
        dq = turn_back(jnp.concatenate(parts, axis=0) * SCORE_SCALE)
        dkf = turn_back(acc_kf[...] * SCORE_SCALE)
        dvf = acc_vf[...].astype(BF16)
        g_far = jnp.concatenate([dkf, dvf], axis=1)
        w_far = jnp.concatenate([wk[...], wv[...]], axis=1)
        far[...] += dot_nt(g_far, w_far)
        dw_far = dot(far_first_t[...], g_far)
        if noisy:
            dk = turn_back(acc_k[...] * SCORE_SCALE)
            dv = acc_v[...].astype(BF16)
            g_own = jnp.concatenate([dq, dk, dv], axis=1)
            own[...] += dot_nt(g_own, jnp.concatenate([wq[...], w_far], axis=1))
            dw = dot(first_t[...], g_own)
            dw_far = dw[:, PAIR:] + dw_far
        else:
            own[...] += dot_nt(dq, wq[...])
            dw = dot(first_t[...], dq)
        dw_own[...] = dw[:, :PAIR].astype(BF16)
        dw_rest[...] = dw_far.astype(BF16)

    @pl.when(noisy_ref[0] == 1)
    def _():
        run(True)

    @pl.when(noisy_ref[0] == 0)
    def _():
        run(False)

    def store(some):
        store_rows(dw_own[...], place_ref, some, slice(0, PAIR))
        store_rows(dw_rest[...], place_ref, some, slice(PAIR, 3 * PAIR))

    half = len(outs) // 2

    @pl.when(pl.program_id(0) < early)
    def _():
        store(outs[:half])

    @pl.when(pl.program_id(0) >= early)
    def _():
        store(outs[half:])


def attend_back(noisy, place_in, masks, heads, ga, joint, first_t, far_first_t, cos, sin, early):
    rows, width = ga.shape
    pairs = width // PAIR
    pair = pl.BlockSpec((rows, PAIR), lambda j: (0, j))

    def strip(part):
        return pl.BlockSpec((width, PAIR), lambda j: (0, part * pairs + j))

    shapes, out_specs = [], []
    for first, last in ((0, early), (early, pairs)):
        for shape in row_grad_shapes(width, 3 * PAIR * (last - first)):
            shapes.append(shape)
            out_specs.append(
                pl.BlockSpec(
                    shape[:-1] + (3 * PAIR,),
                    lambda j, first=first, last=last, n=len(shape): (0,) * (n - 1)
                    + (jnp.clip(j, first, last - 1) - first,),
                )
            )
    act = whole_spec((rows, width))
    turned = whole_spec((width, rows))
    outs = pl.pallas_call(
        partial(attend_back_body, early),
        grid=(pairs,),
        out_shape=[like((rows, width), F32)] * 2 + [like(shape, BF16) for shape in shapes],
        in_specs=[SMEM_SPEC] * 2
        + [whole_spec((rows, 1))]
        + [whole_spec((1, rows))] * 3
        + [pair] * 6
        + [pl.BlockSpec((8, 2 * rows), lambda j: (j, 0))]
        + [act, pl.BlockSpec((PAIR, width), lambda j: (j, 3))]
        + [strip(0), strip(1), strip(2), turned, turned]
        + [whole_spec((rows, PAIR))] * 2,
        out_specs=[act] * 2 + out_specs,
        scratch_shapes=[
            pltpu.VMEM((rows, rows), F32),
            pltpu.VMEM((rows // TILE, TILE + 2 * REACH, TILE), F32),
        ]
        + [pltpu.VMEM((rows, PAIR), F32)] * 4
        + [pltpu.VMEM((width, PAIR), BF16), pltpu.VMEM((width, 2 * PAIR), BF16)],
        compiler_params=pltpu.CompilerParams(vmem_limit_bytes=32 * 2**20),
        cost_estimate=SHORT,
    )(
        noisy,
        place_in,
        *in_hbm(*masks, *heads, ga, joint, joint, joint, joint, first_t, far_first_t, cos, sin),
    )
    half = len(shapes) // 2
    return outs[0], outs[1], outs[2 : 2 + half], outs[2 + half :]


def store_rows(value, place_ref, outs, columns):
    if len(outs) == 1:
        outs[0][:, columns] = value.astype(BF16)
        return
    keep, send = outs
    _, far_count, pair_rows, _ = keep.shape
    core, near, far = place_ref[0], place_ref[1], place_ref[2]
    for z in range(far_count):
        for y in range(2):
            start = (z * 2 + y) * 2 * pair_rows
            first = value[start : start + pair_rows].astype(BF16)
            second = value[start + pair_rows : start + 2 * pair_rows].astype(BF16)
            keep[y ^ near, z ^ far, :, columns] = jnp.where(core == 0, first, second)
            send[y ^ near, z ^ far, :, columns] = jnp.where(core == 0, second, first)


def mlp_body(n_up, *refs):
    (
        place_ref, tok, o, cot, out_w, extra, up_w, down_w, within, which,
        layer_out, gy, ga, *dups, lines, up_lines,
        y1, second, out_acc, gsec_acc, up_line, grad_line,
    ) = refs
    dups, ddowns = dups[:n_up], dups[n_up:]
    step = pl.program_id(0)

    @pl.when(step == 0)
    def _():
        rows = tok[...].astype(F32) + dot(o[...], out_w[...])
        y1[...] = rows
        norm, _ = normed(rows)
        second[...] = (norm * small_row(extra, 1)).astype(BF16)
        out_acc[...] = jnp.zeros_like(out_acc)
        gsec_acc[...] = jnp.zeros_like(gsec_acc)
        lines[...] = jnp.zeros_like(lines)
        lines[2:3, :] = jnp.sum(cot[...].astype(F32), axis=0, keepdims=True)
        chunk = up_w.shape[1]
        quarter = chunk // 4
        row = lax.broadcasted_iota(jnp.int32, (8, SMALL), 0)
        lane = lax.broadcasted_iota(jnp.int32, (8, SMALL), 1)
        pick = (lane == row + 3).astype(BF16)
        line = lax.broadcasted_iota(jnp.int32, (8, chunk), 0)
        for j in range(up_line.shape[0]):
            four = dot_nt(pick, extra[j * quarter : (j + 1) * quarter, :]).astype(BF16)
            values = jnp.where(line == which[...], dot_nt(four, within[...]), 0.0)
            up_line[j : j + 1, :] = jnp.sum(values, axis=0, keepdims=True)

    up_b = up_line[pl.ds(step, 1), :]
    x = dot(second[...], up_w[...]) + up_b
    square = x * x
    t = jnp.tanh(x * (GELU_A + (GELU_A * GELU_B) * square))
    half_t = 0.5 + 0.5 * t
    act = (x * half_t).astype(BF16)
    slope = half_t + (0.5 * x) * (1.0 - t * t) * (GELU_A + (3.0 * GELU_A * GELU_B) * square)
    g_pre = (dot_nt(cot[...], down_w[...]) * slope).astype(BF16)
    dup_b = jnp.sum(g_pre.astype(F32), axis=0, keepdims=True)
    grad_line[pl.ds(step, 1), :] = dup_b
    out_acc[...] += dot(act, down_w[...])
    gsec_acc[...] += dot_nt(g_pre, up_w[...])
    down_grad = dot_tn(act, cot[...])
    if len(ddowns) == 1:
        ddowns[0][...] = down_grad.astype(BF16)
    else:
        pair_rows = down_grad.shape[0] // 4
        core, near = place_ref[0], place_ref[1]
        for y in range(2):
            start = 2 * y * pair_rows
            first = down_grad[start : start + pair_rows].astype(BF16)
            other = down_grad[start + pair_rows : start + 2 * pair_rows].astype(BF16)
            ddowns[0][y ^ near, 0] = jnp.where(core == 0, first, other)
            ddowns[1][y ^ near, 0] = jnp.where(core == 0, other, first)
    store_rows(dot_tn(second[...], g_pre), place_ref, dups, slice(None))

    @pl.when(step == pl.num_programs(0) - 1)
    def _():
        up_lines[...] = jnp.zeros_like(up_lines)
        for j in range(4):
            up_lines[j] = dot(jnp.where(which[...] == j, grad_line[...], 0.0).astype(BF16), within[...])
        rows = y1[...]
        layer_out[...] = (rows + out_acc[...] + small_row(extra, 2)).astype(BF16)
        norm, inverse = normed(rows)
        gs = gsec_acc[...]
        lines[1:2, :] = jnp.sum(gs * norm, axis=0, keepdims=True)
        g = cot[...].astype(F32) + norm_term(gs, norm, inverse, small_row(extra, 1))
        gy[...] = g
        ga[...] = g.astype(BF16)


def row_grad_shapes(width, columns):
    pair_rows = 2 * (width // device_count())
    if pair_rows % 16:
        return [(width, columns)]
    return [(2, device_count() // 8, pair_rows, columns)] * 2


def mlp(place_in, tok, o, cot, joint, up_w, down_w):
    rows, width = tok.shape
    hidden = up_w.shape[1]
    ups = row_grad_shapes(width, hidden)
    pair_rows = 2 * (hidden // device_count())
    if len(ups) == 1:
        chunk = hidden // 4
        up_specs = [pl.BlockSpec((width, chunk), lambda j, _: (0, j))]
        downs = [(hidden, width)]
        down_specs = [pl.BlockSpec((chunk, width), lambda j, _: (j, 0))]
    else:
        chunk = 4 * pair_rows
        far_count = device_count() // 8
        up_specs = [pl.BlockSpec(ups[0][:3] + (chunk,), lambda j, _: (0, 0, 0, j))] * 2
        downs = [(2, far_count, pair_rows, width)] * 2
        down_specs = [
            pl.BlockSpec((2, 1, pair_rows, width), lambda j, p: (0, j ^ p[2], 0, 0))
        ] * 2
    act = whole_spec((rows, width))
    extra, _, out_w = joint_specs(width)
    up_in = pl.BlockSpec((width, chunk), lambda j, _: (0, j))
    shard = hidden // device_count()
    unit = np.arange(chunk)
    within = (unit // shard) * (shard // 4) + unit % (shard // 4)
    which = (unit % shard) // (shard // 4)
    within = jnp.asarray(within[:, None] == np.arange(chunk // 4)[None, :], BF16)
    which = jnp.asarray(which[None], jnp.int32)
    down_in = pl.BlockSpec((chunk, width), lambda j, _: (j, 0))
    outs = pl.pallas_call(
        partial(mlp_body, len(ups)),
        grid_spec=pltpu.PrefetchScalarGridSpec(
            num_scalar_prefetch=1,
            grid=(hidden // chunk,),
            in_specs=[act, act, act, out_w, extra, up_in, down_in]
            + [whole_spec((chunk, chunk // 4)), whole_spec((1, chunk))],
            out_specs=[act, act, act]
            + up_specs
            + down_specs
            + [whole_spec((8, width)), whole_spec((8, hidden // chunk, chunk // 4))],
            scratch_shapes=[
                pltpu.VMEM((rows, width), F32),
                pltpu.VMEM((rows, width), BF16),
                pltpu.VMEM((rows, width), F32),
                pltpu.VMEM((rows, width), F32),
                pltpu.VMEM((hidden // chunk, chunk), F32),
                pltpu.VMEM((hidden // chunk, chunk), F32),
            ],
        ),
        out_shape=[like((rows, width), BF16), like((rows, width), F32), like((rows, width), BF16)]
        + [like(shape, BF16) for shape in ups + downs]
        + [like((8, width), F32), like((8, hidden // chunk, chunk // 4), F32)],
        compiler_params=pltpu.CompilerParams(vmem_limit_bytes=32 * 2**20),
        cost_estimate=SHORT,
    )(place_in, *in_hbm(tok), o, *in_hbm(cot), joint, joint, up_w, down_w, *in_hbm(within, which))
    n = len(ups)
    return (*outs[:3], outs[3 : 3 + n], outs[3 + n : 3 + 2 * n], outs[-2], outs[-1])


def finish_body(
    noisy_ref, place_ref, tok, far_tok, far_tok_end, extra, own, far, gy, o, ga, lines, up_lines,
    part, send, *outs
):
    width = tok.shape[1]
    g = small_row(extra, 0)
    norm, inverse = normed(tok[...].astype(F32))
    own, far = own[...], far[...]

    def put_lines(gains):
        row = lax.broadcasted_iota(jnp.int32, (8, width), 0)
        values = jnp.where(row == 0, gains, lines[...]).astype(BF16)
        row = lax.broadcasted_iota(jnp.int32, (8, SMALL), 0)
        lane = lax.broadcasted_iota(jnp.int32, (8, SMALL), 1)
        small = dot_tn(values, (row == lane).astype(BF16))
        later = (row + 3 == lane).astype(BF16)
        biases = [dot_tn(up_lines[:, j, :].astype(BF16), later) for j in range(up_lines.shape[1])]
        small = small + jnp.concatenate(biases, axis=0)
        store_rows(small, place_ref, outs, slice(width, width + SMALL))

    half = width // 2
    for start in (0, half):
        c = slice(start, start + half)
        store_rows(dot_tn(o[...], ga[:, c]), place_ref, outs, c)

    @pl.when(noisy_ref[0] == 1)
    def _():
        part[...] = gy[...] + norm_term(own, norm, inverse, g)
        far_norm, far_inverse = normed(both(far_tok, far_tok_end))
        send[...] = norm_term(far, far_norm, far_inverse, g).astype(BF16)
        put_lines(jnp.sum(own * norm + far * far_norm, axis=0, keepdims=True))

    @pl.when(noisy_ref[0] == 0)
    def _():
        both = own + far
        part[...] = gy[...] + norm_term(both, norm, inverse, g)
        send[...] = jnp.zeros_like(send)
        put_lines(jnp.sum(both * norm, axis=0, keepdims=True))


def finish(noisy, place_in, tok, far_tok, far_tok_end, joint, own, far, gy, o, ga, lines, up_lines):
    rows, width = tok.shape
    act = whole_spec((rows, width))
    extra, _, _ = joint_specs(width)
    shapes = row_grad_shapes(width, width + SMALL)
    outs = pl.pallas_call(
        finish_body,
        grid=(1,),
        out_shape=[like((rows, width), F32)]
        + [like((rows, width), BF16)]
        + [like(shape, BF16) for shape in shapes],
        in_specs=[SMEM_SPEC] * 2
        + [act]
        + [whole_spec((rows // 2, width))] * 2
        + [extra]
        + [act] * 5
        + [whole_spec((8, width)), whole_spec(up_lines.shape)],
        out_specs=[act, act] + [whole_spec(shape) for shape in shapes],
        compiler_params=pltpu.CompilerParams(vmem_limit_bytes=32 * 2**20),
        cost_estimate=SHORT,
    )(noisy, place_in, tok, far_tok, far_tok_end, joint, own, far, gy, o, ga, lines, up_lines)
    return outs[0], outs[1], outs[2:]


def last_sum_body(pairs, keep, *refs):
    got, (qkv, out, small) = refs[:-3], refs[-3:]
    total = keep[0]
    for g in got:
        total = total + g[0].astype(F32)
    width = out.shape[1]
    for i in range(pairs):
        at = 3 * PAIR * i
        for p in range(3):
            qkv[:, p * width + i * PAIR : p * width + (i + 1) * PAIR] = total[
                :, at + p * PAIR : at + (p + 1) * PAIR
            ]
    out[...] = total[:, 3 * width : 4 * width]
    small[...] = total[:, 4 * width :]


def last_sum(keep, got, width):
    rows = keep.shape[1]
    shapes = ((rows, 3 * width), (rows, width), (rows, SMALL))
    return pl.pallas_call(
        partial(last_sum_body, width // PAIR),
        out_shape=[like(shape, F32) for shape in shapes],
        in_specs=[VMEM_SPEC] * (1 + len(got)),
        out_specs=[VMEM_SPEC] * 3,
        compiler_params=pltpu.CompilerParams(vmem_limit_bytes=8 * 2**20),
        cost_estimate=SHORT,
    )(keep, *got)


def mlp_sum_body(keep, *refs):
    got, (up, down) = refs[:-2], refs[-2:]
    total = keep[0]
    for g in got:
        total = total + g[0].astype(F32)
    rows, hidden = up.shape
    width = down.shape[1]
    up[...] = total[:, :hidden]
    for f in range(down.shape[0] // rows):
        at = hidden + f * width
        down[f * rows : (f + 1) * rows, :] = total[:, at : at + width]


def mlp_sum(keep, got, hidden, width):
    _, rows, columns = keep.shape
    return pl.pallas_call(
        mlp_sum_body,
        out_shape=[like((rows, hidden), F32), like(((columns - hidden) // width * rows, width), F32)],
        in_specs=[VMEM_SPEC] * (1 + len(got)),
        out_specs=[VMEM_SPEC] * 2,
        compiler_params=pltpu.CompilerParams(vmem_limit_bytes=8 * 2**20),
        cost_estimate=LONG,
    )(keep, *got)


def add_body(part, got, out):
    out[...] = part[...] + got[...].astype(F32)


def add(part, got):
    rows, width = part.shape
    block = pl.BlockSpec((rows // 4, width), lambda j: (j, 0))
    return pl.pallas_call(
        add_body,
        grid=(4,),
        out_shape=like((rows, width), F32),
        in_specs=[block] * 2,
        out_specs=block,
        compiler_params=pltpu.CompilerParams(vmem_limit_bytes=8 * 2**20),
        cost_estimate=LONG,
    )(part, got)


def local(
    tokens,
    lengths,
    cotangent,
    attn_gain,
    qkv_weight,
    out_weight,
    mlp_gain,
    up_weight,
    up_bias,
    down_weight,
    down_bias,
):
    rows, width = tokens.shape[1:]
    stream = lax.axis_index("stream").astype(jnp.int32)
    me = (lax.axis_index("seq").astype(jnp.int32) * 2 + stream)[None]
    noisy = stream[None]
    n_dev = device_count()
    tok = tokens[0]
    cot = cotangent[0]

    shard_rows, hidden = up_weight.shape
    joint, pair_weights = prepare(
        qkv_weight, out_weight, up_weight, down_weight, attn_gain, mlp_gain, down_bias, up_bias
    )
    cut = 2 * width
    half = rows // 2
    far_tok = [lax.ppermute(tok[:half], "stream", [(0, 1)])]
    (a1, b1), jkey = far_gather(joint, (cut, joint.shape[1] - cut), SHORT, far_tok[0])
    (u1, d1), ukey = far_gather(after(pair_weights, a1), (hidden, hidden), LONG)
    a2, akey = near_gather(a1, jkey, STREAM_BIT)
    b2, bkey = near_gather(b1, jkey, NEAR_BIT)
    far_tok.append(lax.ppermute(after(tok[half:], a2, b2), "stream", [(0, 1)]))
    a3, akey = last_gather(a2, akey, NEAR_BIT, u1, d1)
    b3, bkey = last_gather(b2, bkey, STREAM_BIT, u1, d1)
    u1, d1 = after(u1, a3[1], b3[1]), after(d1, a3[1], b3[1])
    u_got, d_got = flip(u1, NEAR_BIT), flip(d1, STREAM_BIT)
    b3[-1] = after(b3[-1], far_tok[1])
    joint = place([a3, b3], [akey, bkey], me).reshape(width, -1)

    doc_ids, positions = doc_layout(lengths[0], rows)
    cosine, sine = rotary_tables(positions, HEAD_DIM)
    cos = jnp.concatenate([cosine] * 4, axis=1)
    sin = jnp.concatenate([-sine, sine] * 2, axis=1)
    lo = doc_ids * rows
    code = lo + positions // BLOCK
    masks = (lo[:, None], (code - stream)[:, None], code[:, None], code[None, :])

    place_in = jnp.stack([(me[0] // bit) % 2 for bit in (CORE_BIT, NEAR_BIT)] + [me[0] // (2 * NEAR_BIT)])
    first_t, far_first_t, q, k, v, kf, vf = front(noisy, tok, *far_tok, joint, cos, sin)
    u_got, d_got = after(u_got, q), after(d_got, q)
    u2, d2 = jnp.concatenate([u1, u_got], axis=0), jnp.concatenate([d1, d_got], axis=0)
    u_got, d_got = flip(u2, STREAM_BIT), flip(d2, NEAR_BIT)
    u_core, d_core = flip(u2, CORE_BIT), flip(d2, CORE_BIT)

    def keys(*bits):
        out = [ukey]
        for bit in bits:
            out = out + [[key ^ bit for key in line] for line in out]
        return [out[0] + out[1], out[2] + out[3], out[4] + out[5], out[6] + out[7]]

    ukey, dkey = keys(NEAR_BIT, STREAM_BIT, CORE_BIT), keys(STREAM_BIT, NEAR_BIT, CORE_BIT)
    begun = place_pair([u2, u_core], ukey[::2], [d2, d_core], dkey[::2], n_dev, me)
    o, lse = attend(noisy, *masks, after(q, u2, d2), k, v, kf, vf)
    u_got, d_got = after(u_got, o), after(d_got, o)
    up_full, down_full = place_pair(
        [u_got, flip(u_got, CORE_BIT)],
        ukey[1::2],
        [d_got, flip(d_got, CORE_BIT)],
        dkey[1::2],
        n_dev,
        me,
        begun,
    )
    layer_out, gy, ga, dup, ddown, lines, up_lines = mlp(
        place_in, tok, o, cot, joint, up_full.reshape(width, -1), down_full.reshape(-1, width)
    )

    up_sum, down_sum = Sum(me, dup), Sum(me, ddown)
    split((up_sum, NEAR_BIT), (down_sum, STREAM_BIT))
    up_sum.flip(NEAR_BIT)
    down_sum.flip(STREAM_BIT)
    ga_next = after(ga, up_sum.send, down_sum.send)
    heads = (q, k, v, kf, vf, o, lse)
    turned_masks = (code[:, None], lo[None], (code - stream)[None], code[None])
    pairs = width // PAIR
    early = 2 * pairs // 3
    own, far, front_outs, back_outs = attend_back(
        noisy, place_in, turned_masks, heads, ga_next, joint, first_t, far_first_t, cos, sin, early
    )
    up_sum.hold(*front_outs)
    down_sum.hold(*front_outs)
    split((up_sum, STREAM_BIT), (down_sum, NEAR_BIT))
    up_sum.flip(STREAM_BIT)
    down_sum.flip(NEAR_BIT)
    front_sum = Sum(me, [after(a, up_sum.send, down_sum.send) for a in front_outs])
    back_sum = Sum(me, [after(a, up_sum.send, down_sum.send) for a in back_outs])
    up_sum.hold(front_sum.got, back_sum.got)
    down_sum.hold(front_sum.got, back_sum.got)
    gy = after(gy, up_sum.send, down_sum.send)
    part, send, outs = finish(
        noisy, place_in, tok, *far_tok, joint, own, far, gy, o, ga, lines, up_lines
    )
    back_sum.add(outs)
    mlp_far = Far([up_sum, down_sum], LONG)
    back_sum.hold(*mlp_far.sends)
    split((front_sum, STREAM_BIT), (back_sum, NEAR_BIT))
    front_sum.flip(STREAM_BIT)
    back_sum.flip(NEAR_BIT)
    mlp_far.flip()
    split((front_sum, NEAR_BIT), (back_sum, STREAM_BIT))
    front_sum.flip(NEAR_BIT)
    back_sum.flip(STREAM_BIT)
    owned_up, owned_down = mlp_sum(mlp_far.keep, mlp_far.got, hidden, width)
    back_sum.hold(owned_up, owned_down)
    received = lax.ppermute(after(send, front_sum.send, back_sum.send), "stream", [(1, 0)])
    attn_far = Far([front_sum, back_sum])
    attn_far.flip()
    grad_input = add(part, received)
    attn_far.got[0] = after(attn_far.got[0], grad_input)
    owned_qkv, owned_out, owned_small = last_sum(attn_far.keep, attn_far.got, width)

    def small_owned(i):
        return owned_small[:, i]

    return (
        layer_out[None],
        grad_input[None],
        small_owned(0),
        owned_qkv,
        owned_out,
        small_owned(1),
        owned_up,
        owned_small[:, 3:7].T.reshape(-1),
        owned_down,
        small_owned(2),
    )


def solution(mesh):
    placed = (
        P("stream", "seq", None),
        P("seq", None),
        P("stream", "seq", None),
        P(("seq", "stream")),
        P(("seq", "stream"), None),
        P(("seq", "stream"), None),
        P(("seq", "stream")),
        P(("seq", "stream"), None),
        P(("seq", "stream")),
        P(("seq", "stream"), None),
        P(("seq", "stream")),
    )
    return jax.shard_map(
        local,
        mesh=mesh,
        in_specs=placed,
        out_specs=(
            P("stream", "seq", None),
            P("stream", "seq", None),
            P(("seq", "stream")),
            P(("seq", "stream"), None),
            P(("seq", "stream"), None),
            P(("seq", "stream")),
            P(("seq", "stream"), None),
            P(("seq", "stream")),
            P(("seq", "stream"), None),
            P(("seq", "stream")),
        ),
        check_vma=False,
    )
```

```python
from functools import partial
import math

import jax
import jax.numpy as jnp
import numpy as np
from jax import lax
from jax.experimental import pallas as pl
from jax.experimental.pallas import tpu as pltpu
from jax.sharding import PartitionSpec as P

HEADS = 12
HEAD_DIM = 64
BLOCK = 16


EPSILON = 1e-05
NEG_FILL = -1e30


ALL = ("seq", "stream")
STREAM_BIT, CORE_BIT, NEAR_BIT = 1, 2, 4


def device_count():
    return lax.axis_size("seq") * lax.axis_size("stream")


def far_groups():
    bits = []
    bit = 2 * NEAR_BIT
    while bit < device_count():
        bits.append(bit)
        bit *= 2
    groups = []
    while bits:
        taken, bits = bits[:2], bits[2:]
        groups.append(taken if len(taken) == 1 else [taken[0], taken[1], taken[0] + taken[1]])
    return groups


def flip(block, mask):
    return lax.ppermute(block, ALL, [(i, i ^ mask) for i in range(device_count())])


def place(pieces, keys, me):
    total = sum(len(key) for key in keys[0])
    rows = pieces[0][0].shape[1]
    widths = [strip[0].shape[2] for strip in pieces]
    shape = (total, rows, sum(widths))
    flat = [p for strip in pieces for p in strip]

    def body(me_ref, *refs):
        out, sem = refs[-2], refs[-1]
        taken, column = 0, 0
        for key_set, width in zip(keys, widths):
            for key in key_set:
                piece = refs[taken]
                taken += 1
                for j, rel in enumerate(key):
                    to = out.at[me_ref[0] ^ rel]
                    if len(widths) > 1:
                        to = to.at[:, pl.ds(column, width)]
                    pltpu.make_async_copy(piece.at[j], to, sem).start()
            column += width
        pltpu.make_async_copy(out, out, sem).wait()

    return pl.pallas_call(
        body,
        out_shape=like(shape, flat[0].dtype),
        in_specs=[SMEM_SPEC] + [pl.BlockSpec(memory_space=pl.ANY)] * len(flat),
        out_specs=VMEM_SPEC,
        scratch_shapes=[pltpu.SemaphoreType.DMA],
        compiler_params=pltpu.CompilerParams(
            vmem_limit_bytes=2 * math.prod(shape) * (16 // min(16, rows)) * 2 + 2**20
        ),
        cost_estimate=SHORT,
    )(me, *flat)


def place_pair(up, up_keys, down, down_keys, total, me, begun=()):
    rows, hidden = up[0].shape[1:]
    width = total * rows
    folds = down[0].shape[2] // width

    def body(me_ref, *refs):
        up_out, down_out, up_sem, down_sem = refs[-4:]
        pieces = refs[len(begun) : -4]
        copies = []
        for piece, key in zip(pieces, up_keys):
            for j, rel in enumerate(key):
                copies.append((piece.at[j], up_out.at[me_ref[0] ^ rel], up_sem))
        for piece, key in zip(pieces[len(up) :], down_keys):
            for j, rel in enumerate(key):
                for f in range(folds):
                    part = piece.at[j, :, pl.ds(f * width, width)]
                    copies.append((part, down_out.at[me_ref[0] ^ rel, f], down_sem))
        for source, target, sem in copies:
            pltpu.make_async_copy(source, target, sem).start()
        count = sum(len(key) for key in up_keys)
        for out, sem in ((up_out, up_sem), (down_out, down_sem)):
            some = out.at[pl.ds(0, count)]
            pltpu.make_async_copy(some, some, sem).wait()

    shapes = ((total, rows, hidden), (total, folds, rows, width))
    return pl.pallas_call(
        body,
        out_shape=[pltpu.VMEM(shape, BF16) for shape in shapes],
        in_specs=[SMEM_SPEC]
        + [VMEM_SPEC] * len(begun)
        + [pl.BlockSpec(memory_space=pl.ANY)] * len(up + down),
        out_specs=[VMEM_SPEC] * 2,
        scratch_shapes=[pltpu.SemaphoreType.DMA] * 2,
        input_output_aliases={1: 0, 2: 1} if begun else {},
        compiler_params=pltpu.CompilerParams(
            vmem_limit_bytes=4 * total * rows * hidden * (16 // min(16, rows)) + 2**20
        ),
        cost_estimate=SHORT,
    )(me, *(pltpu.with_memory_space_constraint(b, pltpu.VMEM) for b in begun), *up, *down)


def after(block, *others):
    return lax.optimization_barrier((block,) + others)[0]


def stack_body(count, widths, *refs):
    ins, outs = refs[:count], refs[count:]
    column = 0
    for out, width in zip(outs, widths):
        at = 0
        for piece in ins:
            out[at : at + piece.shape[0]] = piece[:, :, column : column + width]
            at += piece.shape[0]
        column += width


def stack(pieces, widths, cost):
    total, rows = sum(p.shape[0] for p in pieces), pieces[0].shape[1]
    return pl.pallas_call(
        partial(stack_body, len(pieces), widths),
        out_shape=[like((total, rows, width), BF16) for width in widths],
        in_specs=[VMEM_SPEC] * len(pieces),
        out_specs=[VMEM_SPEC] * len(widths),
        compiler_params=pltpu.CompilerParams(vmem_limit_bytes=6 * 2**20),
        cost_estimate=cost,
    )(*pieces)


def far_gather(shard, widths, cost, *others):
    piece, key = shard[None], [0]
    groups = far_groups()
    for group in groups:
        got = [piece] + [flip(piece, mask) for mask in group]
        key = [k ^ mask for mask in [0] + group for k in key]
        if group != groups[-1]:
            piece = jnp.concatenate(got, axis=0)
    if others:
        got[-1] = after(got[-1], *others)
    return stack(got, widths, cost), key


def near_gather(piece, key, bit):
    return jnp.concatenate([piece, flip(piece, bit)], axis=0), key + [k ^ bit for k in key]


def last_gather(piece, key, bit, *others):
    got = flip(piece, bit)
    if others:
        got = after(got, *others)
    pieces, keys = [piece, got], [key, [k ^ bit for k in key]]
    pieces = pieces + [flip(after(piece, *others), CORE_BIT), flip(got, CORE_BIT)]
    return pieces, keys + [[k ^ CORE_BIT for k in key] for key in keys]


def relative(whole, me):
    pairs = device_count() // 2
    rows = whole.reshape((pairs, 2, -1) + whole.shape[1:]) if whole.ndim < 3 else whole
    rows = rows.reshape((pairs, -1) + whole.shape[-1:])
    bits = pairs.bit_length() - 1
    rows = rows.reshape((2,) * bits + rows.shape[1:])
    for axis in range(bits):
        mine = (me[0] >> (bits - axis)) % 2
        rows = jnp.where(mine == 1, jnp.flip(rows, axis), rows)
    order = (bits - 1, bits - 2) + tuple(range(bits - 2)) + (bits, bits + 1)
    rows = rows.transpose(order).reshape((2, 2, pairs // 4) + rows.shape[-2:])
    return rows[0], rows[1]


def combine_body(bits, counts, stream_ref, *refs):
    total = sum(sum(groups) for groups in counts)
    ins, outs = refs[:total], refs[total:]
    stream = stream_ref[0]
    for bit, groups in zip(bits, counts):
        (send, keep), outs = outs[:2], outs[2:]
        column = 0
        for count in groups:
            terms, ins = ins[:count], ins[count:]
            columns = slice(column, column + terms[0].shape[-1])
            column = columns.stop

            def part(own):
                if bit == STREAM_BIT:
                    where = (slice(None), slice(None), pl.ds(stream if own else 1 - stream, 1))
                else:
                    where = (slice(0, 1) if own else slice(1, 2),)
                out = terms[0][where].astype(F32)
                for t in terms[1:]:
                    out = out + t[where].astype(F32)
                return out

            send[..., columns] = part(False).astype(send.dtype)
            keep[..., columns] = part(True)


def combine(stream, jobs):
    far_count = jobs[0][0][0][0].shape[1]
    operands, in_specs, out_shape, out_specs = [], [], [], []

    def spec(shape):
        return pl.BlockSpec((shape[0], 1) + shape[2:], lambda j: (0, j, 0, 0, 0))

    for groups, bit in jobs:
        out = list(groups[0][0].shape)
        out[4] = sum(terms[0].shape[4] for terms in groups)
        out[2 if bit == STREAM_BIT else 0] = 1
        out = tuple(out)
        for terms in groups:
            operands += terms
            in_specs += [spec(terms[0].shape)] * len(terms)
        out_shape += [like(out, BF16), like(out, F32)]
        out_specs += [spec(out)] * 2
    outs = pl.pallas_call(
        partial(
            combine_body,
            [bit for _, bit in jobs],
            [[len(terms) for terms in groups] for groups, _ in jobs],
        ),
        grid=(far_count,),
        out_shape=out_shape,
        in_specs=[SMEM_SPEC] + in_specs,
        out_specs=out_specs,
        compiler_params=pltpu.CompilerParams(vmem_limit_bytes=20 * 2**20),
        cost_estimate=SHORT,
    )(stream, *operands)
    return [(outs[2 * i], outs[2 * i + 1]) for i in range(len(jobs))]


class Sum:
    def __init__(self, me, *strips):
        self.me, self.stream = me, me % 2
        self.groups, self.got = [], []
        for parts in strips:
            self.add(parts)

    def add(self, parts):
        if len(parts) == 1:
            parts = relative(parts[0], self.me)
        keep, send = parts
        _, self.far_count, pair_rows, columns = keep.shape
        shape = (2, self.far_count, 2, pair_rows // 2, columns)
        self.got = flip(send, CORE_BIT)
        self.groups.append([keep.reshape(shape), self.got.reshape(shape)])

    def flip(self, bit):
        self.got = flip(self.send, bit)
        self.groups[0].append(self.got)
        return self

    def hold(self, *others):
        self.groups[0][-1] = after(self.groups[0][-1], *others)

    def total(self):
        out = self.groups[0][0].astype(F32)
        for t in self.groups[0][1:]:
            out = out + t.astype(F32)
        return out


def pack_body(far_count, counts, *refs):
    ins, (keep, *sends) = refs[: sum(counts)], refs[sum(counts) :]
    _, rows, _ = keep.shape
    part = far_count // (1 + len(sends))
    column = 0
    for count in counts:
        terms, ins = ins[:count], ins[count:]
        wide, columns = terms[0].shape[-2:]
        for z in range(far_count):
            total = terms[0][0, z, 0].astype(F32)
            for t in terms[1:]:
                total = total + t[0, z, 0].astype(F32)
            out = keep if z < part else sends[z // part - 1]
            for fold in range(wide // rows):
                at = slice(column + fold * columns, column + (fold + 1) * columns)
                value = total[fold * rows : (fold + 1) * rows]
                out[z % part, :, at] = value.astype(out.dtype)
        column += wide // rows * columns


class Far:
    def __init__(self, sums, cost=None):
        groups = [s.groups[0] for s in sums]
        far_count, _, rows, _ = groups[0][0].shape[1:]
        shards = [g[0].shape[3:] for g in groups]
        columns = sum(r // rows * c for r, c in shards)
        self.order = list(reversed(far_groups()))
        part = far_count // (1 + len(self.order[0]))
        shape = (part, rows, columns)
        outs = pl.pallas_call(
            partial(pack_body, far_count, [len(g) for g in groups]),
            out_shape=[like(shape, F32)] + [like(shape, BF16)] * len(self.order[0]),
            in_specs=[VMEM_SPEC] * sum(len(g) for g in groups),
            out_specs=[VMEM_SPEC] * (1 + len(self.order[0])),
            compiler_params=pltpu.CompilerParams(vmem_limit_bytes=10 * 2**20),
            cost_estimate=cost or SHORT,
        )(*[t for g in groups for t in g])
        self.keep, self.sends = outs[0], outs[1:]

    def flip(self):
        self.got = [flip(s, mask) for s, mask in zip(self.sends, self.order[0])]
        return self.advance()

    def advance(self):
        for group in self.order[1:]:
            total = self.keep
            for block in self.got:
                total = total + block.astype(F32)
            part = total.shape[0] // (len(group) + 1)
            got = [
                flip(total[(i + 1) * part : (i + 2) * part].astype(BF16), mask)
                for i, mask in enumerate(group)
            ]
            self.keep, self.got = total[:part], got
        return self


def split(*jobs):
    outs = combine(jobs[0][0].stream, [(s.groups, bit) for s, bit in jobs])
    for (s, _), (send, keep) in zip(jobs, outs):
        s.send, s.groups = send, [[keep]]


F32, BF16 = jnp.float32, jnp.bfloat16
SHORT = pl.CostEstimate(flops=1, bytes_accessed=1, transcendentals=0)
LONG = pl.CostEstimate(flops=10**10, bytes_accessed=3 * 10**7, transcendentals=0)
SMEM_SPEC = pl.BlockSpec(memory_space=pltpu.SMEM)
VMEM_SPEC = pl.BlockSpec(memory_space=pltpu.VMEM)


def like(shape, kind):
    return jax.ShapeDtypeStruct(shape, kind)


def in_hbm(*arrays):
    return [pltpu.with_memory_space_constraint(a, pltpu.HBM) for a in arrays]


def doc_layout(pack_lengths, row_count):
    ends = [pack_lengths[0]]
    for i in range(1, pack_lengths.shape[0]):
        ends.append(ends[-1] + pack_lengths[i])
    seq_ends = jnp.stack(ends)
    row_index = jnp.arange(row_count, dtype=jnp.int32)
    passed = seq_ends[None, :] <= row_index[:, None]
    doc_ids = jnp.sum(passed.astype(jnp.int32), axis=1)
    starts = jnp.max(jnp.where(passed, seq_ends[None, :], 0), axis=1)
    return (doc_ids, row_index - starts)


def rotary_tables(positions, head_size):
    half_size = head_size // 2
    frequency = jnp.exp(
        jnp.arange(half_size, dtype=jnp.float32) * (-2.0 * math.log(10000.0) / head_size)
    )
    angles = positions.astype(jnp.float32)[:, None] * frequency[None, :]
    return (jnp.cos(angles), jnp.sin(angles))


PAIR = 2 * HEAD_DIM
TILE = 128
SMALL = 128
REACH = 16
LOG2_E = math.log2(math.e)
SCORE_SCALE = HEAD_DIM ** (-0.5)
GELU_A = math.sqrt(2.0 / math.pi)
GELU_B = 0.044715


def dot(a, b):
    return lax.dot_general(a, b, (((1,), (0,)), ((), ())), preferred_element_type=F32)


def dot_nt(a, b):
    return lax.dot_general(a, b, (((1,), (1,)), ((), ())), preferred_element_type=F32)


def dot_tn(a, b):
    return lax.dot_general(a, b, (((0,), (0,)), ((), ())), preferred_element_type=F32)


def whole_spec(shape):
    return pl.BlockSpec(shape, lambda *_: (0,) * len(shape))


def normed(values):
    center = values - jnp.mean(values, axis=-1, keepdims=True)
    inverse = lax.rsqrt(jnp.mean(center * center, axis=-1, keepdims=True) + EPSILON)
    return center * inverse, inverse


def norm_term(grad_out, norm, inverse, gain):
    grad_norm = grad_out * gain
    return inverse * (
        grad_norm
        - jnp.mean(grad_norm, axis=-1, keepdims=True)
        - norm * jnp.mean(grad_norm * norm, axis=-1, keepdims=True)
    )


def half_swap(block):
    lane = lax.broadcasted_iota(jnp.int32, block.shape, 1)
    quarter = HEAD_DIM // 2
    return jnp.where(
        (lane & quarter) == 0,
        pltpu.roll(block, PAIR - quarter, 1),
        pltpu.roll(block, quarter, 1),
    )


def prepare_body(qkv, out, up, down, attn_gain, mlp_gain, down_bias, up_bias, joint, pair_weights):
    rows, hidden = up.shape
    width = out.shape[1]
    joint[:, : 3 * width] = qkv[...]
    joint[:, 3 * width : 4 * width] = out[...]
    lane = lax.broadcasted_iota(jnp.int32, (rows, SMALL), 1)
    small = jnp.zeros((rows, SMALL), F32)
    column = 0
    for line in (attn_gain, mlp_gain, down_bias, up_bias):
        values = line[...].astype(F32)
        for start in range(0, line.shape[1], rows):
            row = lax.broadcasted_iota(jnp.int32, (rows, line.shape[1]), 0)
            item = lax.broadcasted_iota(jnp.int32, (rows, line.shape[1]), 1)
            picked = jnp.sum(jnp.where(item == row + start, values, 0.0), axis=1, keepdims=True)
            small = jnp.where(lane == column, picked, small)
            column += 1
    joint[:, 4 * width :] = small.astype(BF16)
    pair_weights[:, :hidden] = up[...]
    tall = down[...].astype(F32)
    for fold in range(down.shape[0] // rows):
        at = hidden + fold * width
        pair_weights[:, at : at + width] = tall[fold * rows : (fold + 1) * rows].astype(BF16)


def prepare(qkv, out, up, down, *lines):
    rows, width = out.shape
    shapes = ((rows, 4 * width + SMALL), (rows, up.shape[1] + down.size // rows))
    return pl.pallas_call(
        prepare_body,
        out_shape=[like(shape, BF16) for shape in shapes],
        in_specs=[VMEM_SPEC] * 8,
        out_specs=[VMEM_SPEC] * 2,
        compiler_params=pltpu.CompilerParams(vmem_limit_bytes=8 * 2**20),
        cost_estimate=SHORT,
    )(*in_hbm(qkv, out, up, down, *(v[None] for v in lines)))


def small_row(extra, column):
    lane = lax.broadcasted_iota(jnp.int32, (8, extra.shape[1]), 1)
    return dot_nt((lane == column).astype(BF16), extra[...])[0:1, :]


def both(begin, end):
    return jnp.concatenate([begin[...], end[...]], axis=0).astype(F32)


def front_body(
    noisy_ref, tok, far_tok, far_tok_end, extra, weight, cos, sin,
    first_t, far_first_t, q, k, v, kf, vf, first, far_first,
):
    width = tok.shape[1]
    g = small_row(extra, 0)
    norm, _ = normed(tok[...].astype(F32))
    first[...] = (norm * g).astype(BF16)
    is_noisy = noisy_ref[0] == 1

    @pl.when(is_noisy)
    def _():
        far_norm, _ = normed(both(far_tok, far_tok_end))
        far_first[...] = (far_norm * g).astype(BF16)

    @pl.when(jnp.logical_not(is_noisy))
    def _():
        far_first[...] = first[...]

    first_t[...] = first[...].T
    far_first_t[...] = far_first[...].T
    step = 2 * PAIR
    for rows, outs in ((first, (q, k, v)), (far_first, (None, kf, vf))):
        for part, out in enumerate(outs):
            if out is None:
                continue
            for start in range(0, width, step):
                prod = dot(rows[...], weight[:, part * width + start : part * width + start + step])
                for sub in range(0, step, PAIR):
                    x = prod[:, sub : sub + PAIR]
                    if part < 2:
                        x = x * cos[...] + half_swap(x) * sin[...]
                    out[:, start + sub : start + sub + PAIR] = x.astype(BF16)


def joint_specs(width):
    return (
        pl.BlockSpec((width, SMALL), lambda *_: (0, 4 * width // SMALL)),
        pl.BlockSpec((width, 3 * width), lambda *_: (0, 0)),
        pl.BlockSpec((width, width), lambda *_: (0, 3)),
    )


def front(noisy, tok, far_tok, far_tok_end, joint, cos, sin):
    rows, width = tok.shape
    act, table = whole_spec((rows, width)), whole_spec((rows, PAIR))
    extra, qkv, _ = joint_specs(width)
    return pl.pallas_call(
        front_body,
        grid=(1,),
        out_shape=[pltpu.HBM((width, rows), BF16)] * 2 + [pltpu.HBM((rows, width), BF16)] * 5,
        in_specs=[SMEM_SPEC, act] + [whole_spec((rows // 2, width))] * 2 + [extra, qkv, table, table],
        out_specs=[whole_spec((width, rows))] * 2 + [act] * 5,
        scratch_shapes=[pltpu.VMEM((rows, width), BF16)] * 2,
        compiler_params=pltpu.CompilerParams(vmem_limit_bytes=15 * 2**20),
        cost_estimate=SHORT,
    )(noisy, tok, far_tok, far_tok_end, joint, joint, cos, sin)


def window(i, rows):
    size = TILE + 2 * REACH
    return min(max(i * TILE - REACH, 0), rows - size), size


def far_width(i, rows, noisy):
    return min(rows, (i + 1) * TILE + (0 if noisy else TILE))


def build_masks(lo, hi, code, code_row, far_bias, near_bias):
    rows = far_bias.shape[0]
    for i in range(rows // TILE):
        r = slice(i * TILE, (i + 1) * TILE)
        keys = code_row[...]
        far_bias[r, :] = jnp.where((keys >= lo[r, :]) & (keys <= hi[r, :]), 0.0, NEG_FILL)
        start, size = window(i, rows)
        near_bias[i] = jnp.where(code_row[:, start : start + size] == code[r, :], 0.0, NEG_FILL)


def build_turned_masks(code, lo_row, hi_row, code_row, far_bias, near_bias):
    rows = far_bias.shape[0]
    for i in range(rows // TILE):
        r = slice(i * TILE, (i + 1) * TILE)
        keys = code[r, :]
        far_bias[r, :] = jnp.where((keys >= lo_row[...]) & (keys <= hi_row[...]), 0.0, NEG_FILL)
        start, size = window(i, rows)
        near = code[start : start + size, :] == code_row[:, r]
        near_bias[i] = jnp.where(near, 0.0, NEG_FILL)


def beside(block):
    return jnp.concatenate([block, block], axis=1)


def stack_heads(block):
    lane = lax.broadcasted_iota(jnp.int32, block.shape, 1)
    zero = jnp.zeros_like(block)
    return jnp.concatenate(
        [jnp.where(lane < HEAD_DIM, block, zero), jnp.where(lane < HEAD_DIM, zero, block)], axis=0
    )


def unstack_heads(block):
    half = block.shape[0] // 2
    lane = lax.broadcasted_iota(jnp.int32, (half, block.shape[1]), 1)
    return jnp.where(lane < HEAD_DIM, block[:half], block[half:])


def twice(block):
    return jnp.concatenate([block, block], axis=0)


def attend_body(noisy_ref, lo, hi, code, code_row, q, k, v, kf, vf, o, lse, far_bias, near_bias):
    rows = q.shape[0]

    @pl.when(pl.program_id(0) == 0)
    def _():
        build_masks(lo, hi, code, code_row, far_bias, near_bias)

    def run(noisy):
        for i in range(rows // TILE):
            r = slice(i * TILE, (i + 1) * TILE)
            q2 = stack_heads(q[r, :])
            w = far_width(i, rows, noisy)
            s = dot_nt(q2, kf[:w, :]) * (SCORE_SCALE * LOG2_E) + twice(far_bias[r, :w])
            top = jnp.max(s, axis=-1, keepdims=True)
            if noisy:
                start, size = window(i, rows)
                n = slice(start, start + size)
                sn = dot_nt(q2, k[n, :]) * (SCORE_SCALE * LOG2_E) + twice(near_bias[i])
                top = jnp.maximum(top, jnp.max(sn, axis=-1, keepdims=True))
            e = jnp.exp2(s - top)
            total = jnp.sum(e, axis=-1, keepdims=True)
            mixed = dot(e.astype(BF16), vf[:w, :])
            if noisy:
                en = jnp.exp2(sn - top)
                total = total + jnp.sum(en, axis=-1, keepdims=True)
                mixed = mixed + dot(en.astype(BF16), v[n, :])
            o[r, :] = unstack_heads(mixed * (1.0 / total)).astype(BF16)
            log_sum = jnp.broadcast_to(top + jnp.log2(total), (2 * TILE, PAIR))
            lse[:, 2 * TILE * i : 2 * TILE * (i + 1)] = log_sum.T[:8]

    @pl.when(noisy_ref[0] == 1)
    def _():
        run(True)

    @pl.when(noisy_ref[0] == 0)
    def _():
        run(False)


def mask_scratch(rows):
    return [
        pltpu.VMEM((rows, rows), F32),
        pltpu.VMEM((rows // TILE, TILE, TILE + 2 * REACH), F32),
    ]


def attend(noisy, lo, hi, code, code_row, q, k, v, kf, vf):
    rows, width = q.shape
    pair = pl.BlockSpec((rows, PAIR), lambda j: (0, j))
    return pl.pallas_call(
        attend_body,
        grid=(width // PAIR,),
        out_shape=[like((rows, width), BF16), like((8 * (width // PAIR), 2 * rows), F32)],
        in_specs=[SMEM_SPEC] + [whole_spec((rows, 1))] * 3 + [whole_spec((1, rows))] + [pair] * 5,
        out_specs=[pair, pl.BlockSpec((8, 2 * rows), lambda j: (j, 0))],
        scratch_shapes=mask_scratch(rows),
        compiler_params=pltpu.CompilerParams(vmem_limit_bytes=8 * 2**20),
        cost_estimate=SHORT,
    )(noisy, *in_hbm(lo, hi, code, code_row, q, k, v, kf, vf))


def attend_back_body(
    early, noisy_ref, place_ref, code, lo_row, hi_row, code_row, q, k, v, kf, vf, o, lse, ga, out_w, wq, wk, wv,
    first_t, far_first_t, cos, sin, own, far, *refs,
):
    outs, (far_bias, near_bias, acc_k, acc_v, acc_kf, acc_vf, dw_own, dw_rest) = refs[:-8], refs[-8:]
    rows = q.shape[0]

    @pl.when(pl.program_id(0) == 0)
    def _():
        build_turned_masks(code, lo_row, hi_row, code_row, far_bias, near_bias)
        own[...] = jnp.zeros_like(own)
        far[...] = jnp.zeros_like(far)

    go = dot_nt(ga[...], out_w[...]).astype(BF16)

    def turn_back(x):
        return (x * cos[...] - half_swap(x) * sin[...]).astype(BF16)

    def run(noisy):
        acc_kf[...] = jnp.zeros_like(acc_kf)
        acc_vf[...] = jnp.zeros_like(acc_vf)
        if noisy:
            acc_k[...] = jnp.zeros_like(acc_k)
            acc_v[...] = jnp.zeros_like(acc_v)
        parts = []
        for i in range(rows // TILE):
            r = slice(i * TILE, (i + 1) * TILE)
            q2 = stack_heads(q[r, :])
            go2 = stack_heads(go[r, :])
            delta = jnp.sum(
                (go2.astype(F32) * twice(o[r, :]).astype(F32)).T, axis=0, keepdims=True
            )
            log_sum = lse[0:1, 2 * TILE * i : 2 * TILE * (i + 1)]

            w = far_width(i, rows, noisy)
            keys, values, bias = kf[:w, :], vf[:w, :], far_bias[:w, r]
            if noisy:
                start, size = window(i, rows)
                n = slice(start, start + size)
                keys = jnp.concatenate([keys, k[n, :]], axis=0)
                values = jnp.concatenate([values, v[n, :]], axis=0)
                bias = jnp.concatenate([bias, near_bias[i]], axis=0)
            s = dot_nt(keys, q2) * (SCORE_SCALE * LOG2_E) + beside(bias)
            p = jnp.exp2(s - log_sum)
            gp = dot_nt(values, go2)
            ds = (p * (gp - delta)).astype(BF16)
            g_keys, g_values = dot(ds, q2), dot(p.astype(BF16), go2)
            acc_kf[:w, :] += g_keys[:w]
            acc_vf[:w, :] += g_values[:w]
            if noisy:
                acc_k[n, :] += g_keys[w:]
                acc_v[n, :] += g_values[w:]
            gq = dot_tn(keys, ds)
            parts.append(unstack_heads(gq.T))
        dq = turn_back(jnp.concatenate(parts, axis=0) * SCORE_SCALE)
        dkf = turn_back(acc_kf[...] * SCORE_SCALE)
        dvf = acc_vf[...].astype(BF16)
        g_far = jnp.concatenate([dkf, dvf], axis=1)
        w_far = jnp.concatenate([wk[...], wv[...]], axis=1)
        far[...] += dot_nt(g_far, w_far)
        dw_far = dot(far_first_t[...], g_far)
        if noisy:
            dk = turn_back(acc_k[...] * SCORE_SCALE)
            dv = acc_v[...].astype(BF16)
            g_own = jnp.concatenate([dq, dk, dv], axis=1)
            own[...] += dot_nt(g_own, jnp.concatenate([wq[...], w_far], axis=1))
            dw = dot(first_t[...], g_own)
            dw_far = dw[:, PAIR:] + dw_far
        else:
            own[...] += dot_nt(dq, wq[...])
            dw = dot(first_t[...], dq)
        dw_own[...] = dw[:, :PAIR].astype(BF16)
        dw_rest[...] = dw_far.astype(BF16)

    @pl.when(noisy_ref[0] == 1)
    def _():
        run(True)

    @pl.when(noisy_ref[0] == 0)
    def _():
        run(False)

    def store(some):
        store_rows(dw_own[...], place_ref, some, slice(0, PAIR))
        store_rows(dw_rest[...], place_ref, some, slice(PAIR, 3 * PAIR))

    half = len(outs) // 2

    @pl.when(pl.program_id(0) < early)
    def _():
        store(outs[:half])

    @pl.when(pl.program_id(0) >= early)
    def _():
        store(outs[half:])


def attend_back(noisy, place_in, masks, heads, ga, joint, first_t, far_first_t, cos, sin, early):
    rows, width = ga.shape
    pairs = width // PAIR
    pair = pl.BlockSpec((rows, PAIR), lambda j: (0, j))

    def strip(part):
        return pl.BlockSpec((width, PAIR), lambda j: (0, part * pairs + j))

    shapes, out_specs = [], []
    for first, last in ((0, early), (early, pairs)):
        for shape in row_grad_shapes(width, 3 * PAIR * (last - first)):
            shapes.append(shape)
            out_specs.append(
                pl.BlockSpec(
                    shape[:-1] + (3 * PAIR,),
                    lambda j, first=first, last=last, n=len(shape): (0,) * (n - 1)
                    + (jnp.clip(j, first, last - 1) - first,),
                )
            )
    act = whole_spec((rows, width))
    turned = whole_spec((width, rows))
    outs = pl.pallas_call(
        partial(attend_back_body, early),
        grid=(pairs,),
        out_shape=[like((rows, width), F32)] * 2 + [like(shape, BF16) for shape in shapes],
        in_specs=[SMEM_SPEC] * 2
        + [whole_spec((rows, 1))]
        + [whole_spec((1, rows))] * 3
        + [pair] * 6
        + [pl.BlockSpec((8, 2 * rows), lambda j: (j, 0))]
        + [act, pl.BlockSpec((PAIR, width), lambda j: (j, 3))]
        + [strip(0), strip(1), strip(2), turned, turned]
        + [whole_spec((rows, PAIR))] * 2,
        out_specs=[act] * 2 + out_specs,
        scratch_shapes=[
            pltpu.VMEM((rows, rows), F32),
            pltpu.VMEM((rows // TILE, TILE + 2 * REACH, TILE), F32),
        ]
        + [pltpu.VMEM((rows, PAIR), F32)] * 4
        + [pltpu.VMEM((width, PAIR), BF16), pltpu.VMEM((width, 2 * PAIR), BF16)],
        compiler_params=pltpu.CompilerParams(vmem_limit_bytes=32 * 2**20),
        cost_estimate=SHORT,
    )(
        noisy,
        place_in,
        *in_hbm(*masks, *heads, ga, joint, joint, joint, joint, first_t, far_first_t, cos, sin),
    )
    half = len(shapes) // 2
    return outs[0], outs[1], outs[2 : 2 + half], outs[2 + half :]


def store_rows(value, place_ref, outs, columns):
    if len(outs) == 1:
        outs[0][:, columns] = value.astype(BF16)
        return
    keep, send = outs
    _, far_count, pair_rows, _ = keep.shape
    core, near, far = place_ref[0], place_ref[1], place_ref[2]
    for z in range(far_count):
        for y in range(2):
            start = (z * 2 + y) * 2 * pair_rows
            first = value[start : start + pair_rows].astype(BF16)
            second = value[start + pair_rows : start + 2 * pair_rows].astype(BF16)
            keep[y ^ near, z ^ far, :, columns] = jnp.where(core == 0, first, second)
            send[y ^ near, z ^ far, :, columns] = jnp.where(core == 0, second, first)


def mlp_body(n_up, *refs):
    (
        place_ref, tok, o, cot, out_w, extra, up_w, down_w, within, which,
        layer_out, gy, ga, *dups, lines, up_lines,
        y1, second, out_acc, gsec_acc, up_line, grad_line,
    ) = refs
    dups, ddowns = dups[:n_up], dups[n_up:]
    step = pl.program_id(0)

    @pl.when(step == 0)
    def _():
        rows = tok[...].astype(F32) + dot(o[...], out_w[...])
        y1[...] = rows
        norm, _ = normed(rows)
        second[...] = (norm * small_row(extra, 1)).astype(BF16)
        out_acc[...] = jnp.zeros_like(out_acc)
        gsec_acc[...] = jnp.zeros_like(gsec_acc)
        lines[...] = jnp.zeros_like(lines)
        lines[2:3, :] = jnp.sum(cot[...].astype(F32), axis=0, keepdims=True)
        chunk = up_w.shape[1]
        quarter = chunk // 4
        row = lax.broadcasted_iota(jnp.int32, (8, SMALL), 0)
        lane = lax.broadcasted_iota(jnp.int32, (8, SMALL), 1)
        pick = (lane == row + 3).astype(BF16)
        line = lax.broadcasted_iota(jnp.int32, (8, chunk), 0)
        for j in range(up_line.shape[0]):
            four = dot_nt(pick, extra[j * quarter : (j + 1) * quarter, :]).astype(BF16)
            values = jnp.where(line == which[...], dot_nt(four, within[...]), 0.0)
            up_line[j : j + 1, :] = jnp.sum(values, axis=0, keepdims=True)

    up_b = up_line[pl.ds(step, 1), :]
    x = dot(second[...], up_w[...]) + up_b
    square = x * x
    t = jnp.tanh(x * (GELU_A + (GELU_A * GELU_B) * square))
    half_t = 0.5 + 0.5 * t
    act = (x * half_t).astype(BF16)
    slope = half_t + (0.5 * x) * (1.0 - t * t) * (GELU_A + (3.0 * GELU_A * GELU_B) * square)
    g_pre = (dot_nt(cot[...], down_w[...]) * slope).astype(BF16)
    dup_b = jnp.sum(g_pre.astype(F32), axis=0, keepdims=True)
    grad_line[pl.ds(step, 1), :] = dup_b
    out_acc[...] += dot(act, down_w[...])
    gsec_acc[...] += dot_nt(g_pre, up_w[...])
    down_grad = dot_tn(act, cot[...])
    if len(ddowns) == 1:
        ddowns[0][...] = down_grad.astype(BF16)
    else:
        pair_rows = down_grad.shape[0] // 4
        core, near = place_ref[0], place_ref[1]
        for y in range(2):
            start = 2 * y * pair_rows
            first = down_grad[start : start + pair_rows].astype(BF16)
            other = down_grad[start + pair_rows : start + 2 * pair_rows].astype(BF16)
            ddowns[0][y ^ near, 0] = jnp.where(core == 0, first, other)
            ddowns[1][y ^ near, 0] = jnp.where(core == 0, other, first)
    store_rows(dot_tn(second[...], g_pre), place_ref, dups, slice(None))

    @pl.when(step == pl.num_programs(0) - 1)
    def _():
        up_lines[...] = jnp.zeros_like(up_lines)
        for j in range(4):
            up_lines[j] = dot(jnp.where(which[...] == j, grad_line[...], 0.0).astype(BF16), within[...])
        rows = y1[...]
        layer_out[...] = (rows + out_acc[...] + small_row(extra, 2)).astype(BF16)
        norm, inverse = normed(rows)
        gs = gsec_acc[...]
        lines[1:2, :] = jnp.sum(gs * norm, axis=0, keepdims=True)
        g = cot[...].astype(F32) + norm_term(gs, norm, inverse, small_row(extra, 1))
        gy[...] = g
        ga[...] = g.astype(BF16)


def row_grad_shapes(width, columns):
    pair_rows = 2 * (width // device_count())
    if pair_rows % 16:
        return [(width, columns)]
    return [(2, device_count() // 8, pair_rows, columns)] * 2


def mlp(place_in, tok, o, cot, joint, up_w, down_w):
    rows, width = tok.shape
    hidden = up_w.shape[1]
    ups = row_grad_shapes(width, hidden)
    pair_rows = 2 * (hidden // device_count())
    if len(ups) == 1:
        chunk = hidden // 4
        up_specs = [pl.BlockSpec((width, chunk), lambda j, _: (0, j))]
        downs = [(hidden, width)]
        down_specs = [pl.BlockSpec((chunk, width), lambda j, _: (j, 0))]
    else:
        chunk = 4 * pair_rows
        far_count = device_count() // 8
        up_specs = [pl.BlockSpec(ups[0][:3] + (chunk,), lambda j, _: (0, 0, 0, j))] * 2
        downs = [(2, far_count, pair_rows, width)] * 2
        down_specs = [
            pl.BlockSpec((2, 1, pair_rows, width), lambda j, p: (0, j ^ p[2], 0, 0))
        ] * 2
    act = whole_spec((rows, width))
    extra, _, out_w = joint_specs(width)
    up_in = pl.BlockSpec((width, chunk), lambda j, _: (0, j))
    shard = hidden // device_count()
    unit = np.arange(chunk)
    within = (unit // shard) * (shard // 4) + unit % (shard // 4)
    which = (unit % shard) // (shard // 4)
    within = jnp.asarray(within[:, None] == np.arange(chunk // 4)[None, :], BF16)
    which = jnp.asarray(which[None], jnp.int32)
    down_in = pl.BlockSpec((chunk, width), lambda j, _: (j, 0))
    outs = pl.pallas_call(
        partial(mlp_body, len(ups)),
        grid_spec=pltpu.PrefetchScalarGridSpec(
            num_scalar_prefetch=1,
            grid=(hidden // chunk,),
            in_specs=[act, act, act, out_w, extra, up_in, down_in]
            + [whole_spec((chunk, chunk // 4)), whole_spec((1, chunk))],
            out_specs=[act, act, act]
            + up_specs
            + down_specs
            + [whole_spec((8, width)), whole_spec((8, hidden // chunk, chunk // 4))],
            scratch_shapes=[
                pltpu.VMEM((rows, width), F32),
                pltpu.VMEM((rows, width), BF16),
                pltpu.VMEM((rows, width), F32),
                pltpu.VMEM((rows, width), F32),
                pltpu.VMEM((hidden // chunk, chunk), F32),
                pltpu.VMEM((hidden // chunk, chunk), F32),
            ],
        ),
        out_shape=[like((rows, width), BF16), like((rows, width), F32), like((rows, width), BF16)]
        + [like(shape, BF16) for shape in ups + downs]
        + [like((8, width), F32), like((8, hidden // chunk, chunk // 4), F32)],
        compiler_params=pltpu.CompilerParams(vmem_limit_bytes=32 * 2**20),
        cost_estimate=SHORT,
    )(place_in, *in_hbm(tok), o, *in_hbm(cot), joint, joint, up_w, down_w, *in_hbm(within, which))
    n = len(ups)
    return (*outs[:3], outs[3 : 3 + n], outs[3 + n : 3 + 2 * n], outs[-2], outs[-1])


def finish_body(
    noisy_ref, place_ref, tok, far_tok, far_tok_end, extra, own, far, gy, o, ga, lines, up_lines,
    part, send, *outs
):
    width = tok.shape[1]
    g = small_row(extra, 0)
    norm, inverse = normed(tok[...].astype(F32))
    own, far = own[...], far[...]

    def put_lines(gains):
        row = lax.broadcasted_iota(jnp.int32, (8, width), 0)
        values = jnp.where(row == 0, gains, lines[...]).astype(BF16)
        row = lax.broadcasted_iota(jnp.int32, (8, SMALL), 0)
        lane = lax.broadcasted_iota(jnp.int32, (8, SMALL), 1)
        small = dot_tn(values, (row == lane).astype(BF16))
        later = (row + 3 == lane).astype(BF16)
        biases = [dot_tn(up_lines[:, j, :].astype(BF16), later) for j in range(up_lines.shape[1])]
        small = small + jnp.concatenate(biases, axis=0)
        store_rows(small, place_ref, outs, slice(width, width + SMALL))

    half = width // 2
    for start in (0, half):
        c = slice(start, start + half)
        store_rows(dot_tn(o[...], ga[:, c]), place_ref, outs, c)

    @pl.when(noisy_ref[0] == 1)
    def _():
        part[...] = gy[...] + norm_term(own, norm, inverse, g)
        far_norm, far_inverse = normed(both(far_tok, far_tok_end))
        send[...] = norm_term(far, far_norm, far_inverse, g).astype(BF16)
        put_lines(jnp.sum(own * norm + far * far_norm, axis=0, keepdims=True))

    @pl.when(noisy_ref[0] == 0)
    def _():
        both = own + far
        part[...] = gy[...] + norm_term(both, norm, inverse, g)
        send[...] = jnp.zeros_like(send)
        put_lines(jnp.sum(both * norm, axis=0, keepdims=True))


def finish(noisy, place_in, tok, far_tok, far_tok_end, joint, own, far, gy, o, ga, lines, up_lines):
    rows, width = tok.shape
    act = whole_spec((rows, width))
    extra, _, _ = joint_specs(width)
    shapes = row_grad_shapes(width, width + SMALL)
    outs = pl.pallas_call(
        finish_body,
        grid=(1,),
        out_shape=[like((rows, width), F32)]
        + [like((rows, width), BF16)]
        + [like(shape, BF16) for shape in shapes],
        in_specs=[SMEM_SPEC] * 2
        + [act]
        + [whole_spec((rows // 2, width))] * 2
        + [extra]
        + [act] * 5
        + [whole_spec((8, width)), whole_spec(up_lines.shape)],
        out_specs=[act, act] + [whole_spec(shape) for shape in shapes],
        compiler_params=pltpu.CompilerParams(vmem_limit_bytes=32 * 2**20),
        cost_estimate=SHORT,
    )(noisy, place_in, tok, far_tok, far_tok_end, joint, own, far, gy, o, ga, lines, up_lines)
    return outs[0], outs[1], outs[2:]


def last_sum_body(pairs, keep, *refs):
    got, (qkv, out, small) = refs[:-3], refs[-3:]
    total = keep[0]
    for g in got:
        total = total + g[0].astype(F32)
    width = out.shape[1]
    for i in range(pairs):
        at = 3 * PAIR * i
        for p in range(3):
            qkv[:, p * width + i * PAIR : p * width + (i + 1) * PAIR] = total[
                :, at + p * PAIR : at + (p + 1) * PAIR
            ]
    out[...] = total[:, 3 * width : 4 * width]
    row = lax.broadcasted_iota(jnp.int32, (8, SMALL), 0)
    lane = lax.broadcasted_iota(jnp.int32, (8, SMALL), 1)
    small[...] = lax.dot_general(
        (row == lane).astype(F32),
        total[:, 4 * width :],
        (((1,), (1,)), ((), ())),
        precision=lax.Precision.HIGHEST,
        preferred_element_type=F32,
    )


def last_sum(keep, got, width):
    rows = keep.shape[1]
    shapes = ((rows, 3 * width), (rows, width), (8, rows))
    return pl.pallas_call(
        partial(last_sum_body, width // PAIR),
        out_shape=[like(shape, F32) for shape in shapes],
        in_specs=[VMEM_SPEC] * (1 + len(got)),
        out_specs=[VMEM_SPEC] * 3,
        compiler_params=pltpu.CompilerParams(vmem_limit_bytes=8 * 2**20),
        cost_estimate=SHORT,
    )(keep, *got)


def mlp_sum_body(keep, *refs):
    got, (up, down) = refs[:-2], refs[-2:]
    total = keep[0]
    for g in got:
        total = total + g[0].astype(F32)
    rows, hidden = up.shape
    width = down.shape[1]
    up[...] = total[:, :hidden]
    for f in range(down.shape[0] // rows):
        at = hidden + f * width
        down[f * rows : (f + 1) * rows, :] = total[:, at : at + width]


def mlp_sum(keep, got, hidden, width):
    _, rows, columns = keep.shape
    return pl.pallas_call(
        mlp_sum_body,
        out_shape=[like((rows, hidden), F32), like(((columns - hidden) // width * rows, width), F32)],
        in_specs=[VMEM_SPEC] * (1 + len(got)),
        out_specs=[VMEM_SPEC] * 2,
        compiler_params=pltpu.CompilerParams(vmem_limit_bytes=8 * 2**20),
        cost_estimate=LONG,
    )(keep, *got)


def add_body(part, got, out):
    out[...] = part[...] + got[...].astype(F32)


def add(part, got):
    rows, width = part.shape
    block = pl.BlockSpec((rows // 4, width), lambda j: (j, 0))
    return pl.pallas_call(
        add_body,
        grid=(4,),
        out_shape=like((rows, width), F32),
        in_specs=[block] * 2,
        out_specs=block,
        compiler_params=pltpu.CompilerParams(vmem_limit_bytes=8 * 2**20),
        cost_estimate=LONG,
    )(part, got)


def local(
    tokens,
    lengths,
    cotangent,
    attn_gain,
    qkv_weight,
    out_weight,
    mlp_gain,
    up_weight,
    up_bias,
    down_weight,
    down_bias,
):
    rows, width = tokens.shape[1:]
    stream = lax.axis_index("stream").astype(jnp.int32)
    me = (lax.axis_index("seq").astype(jnp.int32) * 2 + stream)[None]
    noisy = stream[None]
    n_dev = device_count()
    tok = tokens[0]
    cot = cotangent[0]

    shard_rows, hidden = up_weight.shape
    joint, pair_weights = prepare(
        qkv_weight, out_weight, up_weight, down_weight, attn_gain, mlp_gain, down_bias, up_bias
    )
    cut = 2 * width
    half = rows // 2
    far_tok = [lax.ppermute(tok[:half], "stream", [(0, 1)])]
    (a1, b1), jkey = far_gather(joint, (cut, joint.shape[1] - cut), SHORT, far_tok[0])
    (u1, d1), ukey = far_gather(after(pair_weights, a1), (hidden, hidden), LONG)
    a2, akey = near_gather(a1, jkey, STREAM_BIT)
    b2, bkey = near_gather(b1, jkey, NEAR_BIT)
    far_tok.append(lax.ppermute(after(tok[half:], a2, b2), "stream", [(0, 1)]))
    a3, akey = last_gather(a2, akey, NEAR_BIT, u1, d1)
    b3, bkey = last_gather(b2, bkey, STREAM_BIT, u1, d1)
    u1, d1 = after(u1, a3[1], b3[1]), after(d1, a3[1], b3[1])
    u_got, d_got = flip(u1, NEAR_BIT), flip(d1, STREAM_BIT)
    b3[-1] = after(b3[-1], far_tok[1])
    joint = place([a3, b3], [akey, bkey], me).reshape(width, -1)

    doc_ids, positions = doc_layout(lengths[0], rows)
    cosine, sine = rotary_tables(positions, HEAD_DIM)
    cos = jnp.concatenate([cosine] * 4, axis=1)
    sin = jnp.concatenate([-sine, sine] * 2, axis=1)
    lo = doc_ids * rows
    code = lo + positions // BLOCK
    masks = (lo[:, None], (code - stream)[:, None], code[:, None], code[None, :])

    place_in = jnp.stack([(me[0] // bit) % 2 for bit in (CORE_BIT, NEAR_BIT)] + [me[0] // (2 * NEAR_BIT)])
    first_t, far_first_t, q, k, v, kf, vf = front(noisy, tok, *far_tok, joint, cos, sin)
    u_got, d_got = after(u_got, q), after(d_got, q)
    u2, d2 = jnp.concatenate([u1, u_got], axis=0), jnp.concatenate([d1, d_got], axis=0)
    u_got, d_got = flip(u2, STREAM_BIT), flip(d2, NEAR_BIT)
    u_core, d_core = flip(u2, CORE_BIT), flip(d2, CORE_BIT)

    def keys(*bits):
        out = [ukey]
        for bit in bits:
            out = out + [[key ^ bit for key in line] for line in out]
        return [out[0] + out[1], out[2] + out[3], out[4] + out[5], out[6] + out[7]]

    ukey, dkey = keys(NEAR_BIT, STREAM_BIT, CORE_BIT), keys(STREAM_BIT, NEAR_BIT, CORE_BIT)
    begun = place_pair([u2, u_core], ukey[::2], [d2, d_core], dkey[::2], n_dev, me)
    o, lse = attend(noisy, *masks, after(q, u2, d2), k, v, kf, vf)
    u_got, d_got = after(u_got, o), after(d_got, o)
    up_full, down_full = place_pair(
        [u_got, flip(u_got, CORE_BIT)],
        ukey[1::2],
        [d_got, flip(d_got, CORE_BIT)],
        dkey[1::2],
        n_dev,
        me,
        begun,
    )
    layer_out, gy, ga, dup, ddown, lines, up_lines = mlp(
        place_in, tok, o, cot, joint, up_full.reshape(width, -1), down_full.reshape(-1, width)
    )

    up_sum, down_sum = Sum(me, dup), Sum(me, ddown)
    split((up_sum, NEAR_BIT), (down_sum, STREAM_BIT))
    up_sum.flip(NEAR_BIT)
    down_sum.flip(STREAM_BIT)
    ga_next = after(ga, up_sum.send, down_sum.send)
    heads = (q, k, v, kf, vf, o, lse)
    turned_masks = (code[:, None], lo[None], (code - stream)[None], code[None])
    pairs = width // PAIR
    early = 2 * pairs // 3
    own, far, front_outs, back_outs = attend_back(
        noisy, place_in, turned_masks, heads, ga_next, joint, first_t, far_first_t, cos, sin, early
    )
    up_sum.hold(*front_outs)
    down_sum.hold(*front_outs)
    split((up_sum, STREAM_BIT), (down_sum, NEAR_BIT))
    up_sum.flip(STREAM_BIT)
    down_sum.flip(NEAR_BIT)
    front_sum = Sum(me, [after(a, up_sum.send, down_sum.send) for a in front_outs])
    back_sum = Sum(me, [after(a, up_sum.send, down_sum.send) for a in back_outs])
    up_sum.hold(front_sum.got, back_sum.got)
    down_sum.hold(front_sum.got, back_sum.got)
    gy = after(gy, up_sum.send, down_sum.send)
    part, send, outs = finish(
        noisy, place_in, tok, *far_tok, joint, own, far, gy, o, ga, lines, up_lines
    )
    back_sum.add(outs)
    mlp_far = Far([up_sum, down_sum], LONG)
    back_sum.hold(*mlp_far.sends)
    split((front_sum, STREAM_BIT), (back_sum, NEAR_BIT))
    front_sum.flip(STREAM_BIT)
    back_sum.flip(NEAR_BIT)
    mlp_far.flip()
    split((front_sum, NEAR_BIT), (back_sum, STREAM_BIT))
    front_sum.flip(NEAR_BIT)
    back_sum.flip(STREAM_BIT)
    owned_up, owned_down = mlp_sum(mlp_far.keep, mlp_far.got, hidden, width)
    back_sum.hold(owned_up, owned_down)
    received = lax.ppermute(after(send, front_sum.send, back_sum.send), "stream", [(1, 0)])
    attn_far = Far([front_sum, back_sum])
    attn_far.flip()
    grad_input = add(part, received)
    attn_far.got[0] = after(attn_far.got[0], grad_input)
    owned_qkv, owned_out, owned_small = last_sum(attn_far.keep, attn_far.got, width)

    def small_owned(i):
        return owned_small[i]

    return (
        layer_out[None],
        grad_input[None],
        small_owned(0),
        owned_qkv,
        owned_out,
        small_owned(1),
        owned_up,
        owned_small[3:7].reshape(-1),
        owned_down,
        small_owned(2),
    )


def solution(mesh):
    placed = (
        P("stream", "seq", None),
        P("seq", None),
        P("stream", "seq", None),
        P(("seq", "stream")),
        P(("seq", "stream"), None),
        P(("seq", "stream"), None),
        P(("seq", "stream")),
        P(("seq", "stream"), None),
        P(("seq", "stream")),
        P(("seq", "stream"), None),
        P(("seq", "stream")),
    )
    return jax.shard_map(
        local,
        mesh=mesh,
        in_specs=placed,
        out_specs=(
            P("stream", "seq", None),
            P("stream", "seq", None),
            P(("seq", "stream")),
            P(("seq", "stream"), None),
            P(("seq", "stream"), None),
            P(("seq", "stream")),
            P(("seq", "stream"), None),
            P(("seq", "stream")),
            P(("seq", "stream"), None),
            P(("seq", "stream")),
        ),
        check_vma=False,
    )
```
